128 devices in a mesh: replica: 4 (over x_lo, core), shard: 32 (over z, y, x_hi).
Axes of the slice: x: 4 (x_hi: 2, x_lo: 2; x = x_hi * 2 + x_lo), y: 4, z: 4, core: 2. Of those that a mesh axis runs over, the one named last changes fastest.
Arguments:
- hidden_in: bfloat16 [4, 3, 2048, 1536], P('replica', None, 'shard'), may hold values from -6 to 6
- doc_ids: int32 [4, 3, 2048], P('replica', None, 'shard'), may hold values from 0 to 7, as said below
- out_grad: bfloat16 [4, 3, 2048, 1536], P('replica', None, 'shard'), may hold values from -6 to 6
- norm_attn: bfloat16 [1536], P('shard'), may hold values from 0.5 to 1.5
- w_query: bfloat16 [1536, 1536], P('shard'), may hold values from -0.15625 to 0.15625
- w_key: bfloat16 [1536, 512], P('shard'), may hold values from -0.15625 to 0.15625
- w_value: bfloat16 [1536, 512], P('shard'), may hold values from -0.15625 to 0.15625
- w_out: bfloat16 [1536, 1536], P('shard'), may hold values from -6 to 6
- norm_ffn: bfloat16 [1536], P('shard'), may hold values from 0.5 to 1.5
- w_gate: bfloat16 [1536, 3840], P('shard'), may hold values from -0.15625 to 0.15625
- w_up: bfloat16 [1536, 3840], P('shard'), may hold values from -0.15625 to 0.15625
- w_down: bfloat16 [3840, 1536], P('shard'), may hold values from -0.5 to 0.5
Outputs:
- output: bfloat16 [4, 3, 2048, 1536], P('replica', None, 'shard')
- grad_in: bfloat16 [4, 3, 2048, 1536], P('replica', None, 'shard')
- grad_norm_attn: float32 [1536], P('shard')
- grad_query: float32 [1536, 1536], P('shard')
- grad_key: float32 [1536, 512], P('shard')
- grad_value: float32 [1536, 512], P('shard')
- grad_out: float32 [1536, 1536], P('shard')
- grad_norm_ffn: float32 [1536], P('shard')
- grad_gate: float32 [1536, 3840], P('shard')
- grad_up: float32 [1536, 3840], P('shard')
- grad_down: float32 [3840, 1536], P('shard')
The draws below stay inside these ranges and needn't reach their ends.
Inputs may be any that keep to these rules, and one draw needn't show every extreme that they name: `doc_ids`: within each sequence the document numbers start at 0 and never fall; a sequence holds at most 8 documents; in each replica group one of its 3 sequences is a single document.
All inputs are finite; a program needn't handle non-finite values.
Results may differ from the reference program's by a relative error of at most 0.028.
Values may be sent and summed in bfloat16 or wider, within the bound.
No kernel may reach another device: no remote copies, remote signals or barrier semaphores. Data moves between devices by JAX's collectives and lax.ppermute only.
A program may use at most 320 MiB of HBM per device.

```python
import math
import jax
import jax.numpy as jnp
from jax import lax

D = 1536
HEADS = 24
KVH = 8
HD = 64
FF = 3840
MB = 3
DOCS = 8
SEQ = 2048
REPS = 4
QW = 1536
KW = 512


def draw_doc_ids(key, part):
    key = jax.random.fold_in(key, 7)
    pick_key, bound_key = jax.random.split(key)
    chosen = jax.random.randint(pick_key, (REPS,), 0, MB)
    bounds = jax.random.randint(bound_key, (REPS, MB, DOCS - 1), 1, SEQ)
    places = jnp.arange(SEQ, dtype=jnp.int32)
    counted = jnp.sum((places[None, None, :, None] >= bounds[:, :, None, :]).astype(jnp.int32), axis=-1)
    single = jnp.arange(MB, dtype=jnp.int32)[None, :] == chosen[:, None]
    return jnp.where(single[:, :, None], 0, counted).astype(jnp.int32)


def block_scale(key, extent, cuts, smallest, high):
    def one(position, shards_of):
        draws = jax.random.uniform(jax.random.fold_in(jax.random.fold_in(key, 6), position), (shards_of,), jnp.float32, smallest / len(cuts), high / len(cuts))
        return jnp.repeat(jnp.exp(draws), extent[position] // shards_of).reshape((-1,) + (1,) * (len(extent) - position - 1))

    factor_of = one(*cuts[0])
    for cut in cuts[1:]:
        factor_of = factor_of * one(*cut)
    return factor_of


def gaussian(stream_key, dims, scale, reach, cuts=(), kind=jnp.bfloat16):
    values = scale * jax.random.normal(stream_key, dims, jnp.float32)
    if cuts:
        values = values * block_scale(stream_key, dims, cuts, -0.22, 0.18)
    return jnp.clip(values, -reach, reach).astype(kind)


def setup_inputs(seed: int = 0) -> dict:
    key_of = jax.random.split(jax.random.key(seed), 13)
    hidden_in = gaussian(key_of[0], (REPS, MB, SEQ, D), 1.0, 6.0, ((0, 4), (2, 32)))
    doc_ids = draw_doc_ids(jax.random.fold_in(key_of[12], 71), 0)
    out_grad = gaussian(key_of[2], (REPS, MB, SEQ, D), 1.0, 6.0, ((0, 4), (2, 32)))
    norm_attn = jnp.clip(1.0 + 0.1 * jax.random.normal(key_of[3], (D,), jnp.float32), 0.5, 1.5).astype(jnp.bfloat16)
    w_query = gaussian(key_of[4], (D, QW), D ** -0.5, 0.15625, ((0, 32),))
    w_key = gaussian(key_of[5], (D, KW), D ** -0.5, 0.15625, ((0, 32),))
    w_value = gaussian(key_of[6], (D, KW), D ** -0.5, 0.15625, ((0, 32),))
    w_out = gaussian(key_of[7], (QW, D), 1 ** -0.5, 6.0, ((0, 32),))
    norm_ffn = jnp.clip(1.0 + 0.1 * jax.random.normal(key_of[8], (D,), jnp.float32), 0.5, 1.5).astype(jnp.bfloat16)
    w_gate = gaussian(key_of[9], (D, FF), D ** -0.5, 0.15625, ((0, 32),))
    w_up = gaussian(key_of[10], (D, FF), D ** -0.5, 0.15625, ((0, 32),))
    w_down = gaussian(key_of[11], (FF, D), (FF // 32) ** -0.5, 0.5, ((0, 32),))
    return dict(hidden_in=hidden_in, doc_ids=doc_ids, out_grad=out_grad, norm_attn=norm_attn, w_query=w_query, w_key=w_key, w_value=w_value, w_out=w_out, norm_ffn=norm_ffn, w_gate=w_gate, w_up=w_up, w_down=w_down)


@jax.custom_vjp
def low(v):
    return lax.optimization_barrier(v.astype(jnp.bfloat16)).astype(jnp.float32)

@jax.custom_vjp
def low_back(v):
    return v

def low_keep(v):
    return (low(v), None)

def low_pass(kept, grad):
    return (grad,)

def back_keep(v):
    return (v, None)

def back_low(kept, grad):
    return (low(grad),)
low.defvjp(low_keep, low_pass)
low_back.defvjp(back_keep, back_low)
HIGHEST = lax.Precision.HIGHEST
branch_scale = 1.4 / math.sqrt(52.0)
eps_norm = 1e-05

def product(left, right):
    return jnp.dot(left, right, precision=HIGHEST, preferred_element_type=jnp.float32)

def angle_tables(places):
    half_size = HD // 2
    inverse = jnp.exp(-jnp.arange(half_size, dtype=jnp.float32) * (math.log(10000.0) / half_size))
    angles = places.astype(jnp.float32)[:, None] * inverse[None, :]
    return (jnp.cos(angles)[:, None, :], jnp.sin(angles)[:, None, :])

def rotate(values, cosine, sine):
    row_count = values.shape[0]
    split_heads = values.reshape(row_count, -1, HD)
    half_size = HD // 2
    front_half = split_heads[..., :half_size]
    back_half = split_heads[..., half_size:]
    turned = jnp.concatenate([front_half * cosine - back_half * sine, back_half * cosine + front_half * sine], axis=-1)
    return turned.reshape(row_count, -1)

def layer(resid, documents, gain_attn, w_query, w_key, w_value, w_out, gain_ffn, w_gate, w_up, w_down):
    length = resid.shape[0]
    places = jnp.arange(length, dtype=jnp.int32)
    cosine, sine = angle_tables(places)
    scale_one = lax.rsqrt(lax.optimization_barrier(jnp.mean(resid * resid, axis=-1, keepdims=True)) + eps_norm)
    normed = low(resid * scale_one * gain_attn)
    queries = low(rotate(low_back(product(normed, w_query)), cosine, sine))
    keys_rot = low(rotate(low_back(product(normed, w_key)), cosine, sine))
    values_in = low(low_back(product(normed, w_value)))
    allowed = (documents[:, None] == documents[None, :]) & (places[None, :] <= places[:, None])
    groups = HEADS // KVH
    q_heads = queries.reshape(length, KVH, groups, HD).transpose(1, 2, 0, 3)
    k_heads = keys_rot.reshape(length, KVH, HD).transpose(1, 0, 2)
    v_heads = values_in.reshape(length, KVH, HD).transpose(1, 0, 2)

    def attend(pieces):
        q_part, k_part, v_part = pieces
        scores = low_back(jnp.einsum('gcd,kd->gck', q_part, k_part, precision=HIGHEST) * 0.125)
        scores = jnp.where(allowed[None], scores, -1e+30)
        highest = lax.optimization_barrier(jnp.max(scores, axis=-1, keepdims=True))
        expo = jnp.exp(scores - highest)
        probs = low(expo / lax.optimization_barrier(jnp.sum(expo, axis=-1, keepdims=True)))
        return jnp.einsum('gck,kd->gcd', probs, v_part, precision=HIGHEST)
    mixed = lax.map(jax.checkpoint(attend), (q_heads, k_heads, v_heads))
    attn = low(low_back(mixed.transpose(2, 0, 1, 3).reshape(length, HEADS * HD)))
    middle = resid + branch_scale * low_back(product(attn, w_out))
    scale_two = lax.rsqrt(lax.optimization_barrier(jnp.mean(middle * middle, axis=-1, keepdims=True)) + eps_norm)
    normed_two = low(middle * scale_two * gain_ffn)
    gate_pre = low_back(product(normed_two, w_gate))
    up_pre = low_back(product(normed_two, w_up))
    hidden_act = low(jax.nn.silu(gate_pre) * up_pre)
    return middle + branch_scale * low_back(product(hidden_act, w_down))

def reference(hidden_in, doc_ids, out_grad, norm_attn, w_query, w_key, w_value, w_out, norm_ffn, w_gate, w_up, w_down):
    params = tuple((p.astype(jnp.float32) for p in (norm_attn, w_query, w_key, w_value, w_out, norm_ffn, w_gate, w_up, w_down)))
    inputs = hidden_in.reshape(REPS * MB, SEQ, D).astype(jnp.float32)
    documents = doc_ids.reshape(REPS * MB, SEQ).astype(jnp.int32)
    cotangents = out_grad.reshape(REPS * MB, SEQ, D).astype(jnp.float32)

    def one_sequence(totals, item):
        resid, docs_one, cot = item

        def apply(resid_arg, *weights):
            return layer(resid_arg, docs_one, *weights)
        result, pullback = jax.vjp(apply, resid, *params)
        grads = pullback(cot)
        totals = tuple((acc + g for acc, g in zip(totals, grads[1:])))
        return (totals, (result.astype(jnp.bfloat16), grads[0].astype(jnp.bfloat16)))
    start = tuple((jnp.zeros(p.shape, jnp.float32) for p in params))
    totals, (results, grad_rows) = lax.scan(one_sequence, start, (inputs, documents, cotangents))
    output = results.reshape(REPS, MB, SEQ, D)
    grad_in = grad_rows.reshape(REPS, MB, SEQ, D)
    return (output, grad_in, totals[0], totals[1], totals[2], totals[3], totals[4], totals[5], totals[6], totals[7], totals[8])
```

```python
from functools import partial
import math

import jax
import jax.numpy as jnp
from jax import lax
from jax.experimental import pallas as pl
from jax.experimental.pallas import tpu as pltpu
from jax.sharding import Mesh
from jax.sharding import PartitionSpec as P

HEADS = 24
KVH = 8
HD = 64
D = 1536
FF = 3840
MB = 3
SPAN = 64
SHARDS = 32
SEQ = 2048
PARTS = 4
ROWS = MB * SPAN
BOTH = 2 * ROWS
GROUP = HEADS // KVH
HALF_KV = KVH // 2
HQ = HALF_KV * GROUP * HD
HK = HALF_KV * HD
HF = FF // 2
CHUNK = SPAN // PARTS
TILE = 4
TILES = SHARDS // TILE
BLOCK = TILE * SPAN
TROWS = GROUP * TILE * CHUNK

SHARD = ("z", "y", "xh")
branch_scale = 1.4 / math.sqrt(52.0)
eps_norm = 1e-05
NEG = -1e30
VMEM_LIMIT = 48 * 1024 * 1024


def product(left, right):
    return jnp.dot(left, right, preferred_element_type=jnp.float32)


def product_t(left, right):
    return lax.dot_general(left, right, (((1,), (1,)), ((), ())), preferred_element_type=jnp.float32)


def t_product(left, right):
    return lax.dot_general(left, right, (((0,), (0,)), ((), ())), preferred_element_type=jnp.float32)


def swap(values):
    return lax.ppermute(values, "c", [(0, 1), (1, 0)])


def exchange(values):
    return lax.all_to_all(values, SHARD, 0, 0, tiled=True)


def stack_heads(rows):
    return jnp.concatenate([rows[:, g * HD : (g + 1) * HD] for g in range(GROUP)], axis=0)


def lay_heads(rows):
    size = TILE * CHUNK
    return jnp.concatenate([rows[g * size : (g + 1) * size] for g in range(GROUP)], axis=1)


def tile_mask(part, start_rows, tile, blocks):
    wide = blocks * BLOCK
    row = lax.broadcasted_iota(jnp.int32, (TROWS, 1), 0)
    inside = lax.rem(row, TILE * CHUNK)
    q_pos = tile * BLOCK + (inside // CHUNK) * SPAN + part * CHUNK + lax.rem(inside, CHUNK)
    k_pos = (tile + 1 - blocks) * BLOCK + lax.broadcasted_iota(jnp.int32, (TROWS, wide), 1)
    return (k_pos >= start_rows) & (k_pos <= q_pos)


def fwd_kernel(part_ref, first_ref, q_ref, kv_ref, start_ref, o_ref, lse_ref):
    micro = pl.program_id(0)
    part = part_ref[0]

    def tile_body(tile, carry):
        first = first_ref[micro * TILES + tile]

        def work(blocks):
            wide = blocks * BLOCK
            begin = tile + 1 - blocks
            q_rows = stack_heads(
                q_ref[pl.ds(tile * TILE, TILE), 0].reshape(TILE * CHUNK, GROUP * HD)
            ) * jnp.bfloat16(0.125)
            keys = kv_ref[pl.ds(begin * TILE, blocks * TILE), 0].reshape(wide, 2 * HD)
            scores = product_t(q_rows, keys[:, :HD])
            start_rows = start_ref[0, tile][:, :1]
            allowed = tile_mask(part, start_rows, tile, blocks)
            scores = jnp.where(allowed, scores, NEG)
            highest = jnp.max(scores, axis=-1, keepdims=True)
            expo = jnp.exp(scores - highest)
            total = jnp.sum(expo, axis=-1, keepdims=True)
            mixed = product(expo.astype(jnp.bfloat16), keys[:, HD:]) / total
            o_ref[pl.ds(tile * TILE, TILE), 0] = (
                lay_heads(mixed).astype(jnp.bfloat16).reshape(TILE, CHUNK, GROUP * HD)
            )
            lse_ref[0, tile] = jnp.broadcast_to(highest + jnp.log(total), (TROWS, 128))

        for blocks in range(1, TILES + 1):
            pl.when(tile + 1 - first == blocks)(partial(work, blocks))
        return carry

    lax.fori_loop(0, TILES, tile_body, 0)


def bwd_kernel(part_ref, first_ref, q_ref, kv_ref, start_ref, do_ref, lse_ref, dq_ref, dkv_ref, acc):
    micro = pl.program_id(0)
    part = part_ref[0]
    acc[...] = jnp.zeros_like(acc)

    def tile_body(tile, carry):
        first = first_ref[micro * TILES + tile]

        def work(blocks):
            wide = blocks * BLOCK
            begin = tile + 1 - blocks
            q_rows = stack_heads(
                q_ref[pl.ds(tile * TILE, TILE), 0].reshape(TILE * CHUNK, GROUP * HD)
            ) * jnp.bfloat16(0.125)
            d_rows = stack_heads(
                do_ref[pl.ds(tile * TILE, TILE), 0].reshape(TILE * CHUNK, GROUP * HD)
            )
            keys = kv_ref[pl.ds(begin * TILE, blocks * TILE), 0].reshape(wide, 2 * HD)
            scores = product_t(q_rows, keys[:, :HD])
            start_rows = start_ref[0, tile][:, :1]
            allowed = tile_mask(part, start_rows, tile, blocks)
            probs = jnp.where(allowed, jnp.exp(scores - lse_ref[0, tile][:, :1]), 0.0)
            d_probs = product_t(d_rows, keys[:, HD:])
            offset = jnp.sum(d_probs * probs, axis=-1, keepdims=True)
            d_scores = (probs * (d_probs - offset)).astype(jnp.bfloat16)
            d_query = product(d_scores, keys[:, :HD]) * 0.125
            dq_ref[pl.ds(tile * TILE, TILE), 0] = (
                lay_heads(d_query).astype(jnp.bfloat16).reshape(TILE, CHUNK, GROUP * HD)
            )
            d_key = t_product(d_scores, q_rows)
            d_value = t_product(probs.astype(jnp.bfloat16), d_rows)
            where = pl.ds(begin * BLOCK, wide)
            acc[where, :] += jnp.concatenate([d_key, d_value], axis=1)

        for blocks in range(1, TILES + 1):
            pl.when(tile + 1 - first == blocks)(partial(work, blocks))
        return carry

    lax.fori_loop(0, TILES, tile_body, 0)
    dkv_ref[:, 0] = acc[...].astype(jnp.bfloat16).reshape(SHARDS, SPAN, 2 * HD)


SMEM = pl.BlockSpec(memory_space=pltpu.SMEM)
Q_SPEC = pl.BlockSpec((SHARDS, 1, CHUNK, GROUP * HD), lambda m: (0, m, 0, 0))
KV_SPEC = pl.BlockSpec((SHARDS, 1, SPAN, 2 * HD), lambda m: (0, m, 0, 0))
COL_SPEC = pl.BlockSpec((1, TILES, TROWS, 128), lambda m: (m, 0, 0, 0))
Q_SHAPE = jax.ShapeDtypeStruct((SHARDS, MB, CHUNK, GROUP * HD), jnp.bfloat16)
KV_SHAPE = jax.ShapeDtypeStruct((SHARDS, MB, SPAN, 2 * HD), jnp.bfloat16)
COL_SHAPE = jax.ShapeDtypeStruct((MB, TILES, TROWS, 128), jnp.float32)


def attend_fwd(part, first, queries, keys, starts):
    return pl.pallas_call(
        fwd_kernel,
        grid=(MB,),
        in_specs=[SMEM, SMEM, Q_SPEC, KV_SPEC, COL_SPEC],
        out_specs=[Q_SPEC, COL_SPEC],
        out_shape=[Q_SHAPE, COL_SHAPE],
        compiler_params=pltpu.CompilerParams(vmem_limit_bytes=VMEM_LIMIT),
        name="attend_forward",
    )(part, first, queries, keys, starts)


def attend_bwd(part, first, queries, keys, starts, d_mixed, lse):
    return pl.pallas_call(
        bwd_kernel,
        grid=(MB,),
        in_specs=[SMEM, SMEM, Q_SPEC, KV_SPEC, COL_SPEC, Q_SPEC, COL_SPEC],
        out_specs=[Q_SPEC, KV_SPEC],
        out_shape=[Q_SHAPE, KV_SHAPE],
        scratch_shapes=[pltpu.VMEM((SEQ, 2 * HD), jnp.float32)],
        compiler_params=pltpu.CompilerParams(vmem_limit_bytes=VMEM_LIMIT),
        name="attend_backward",
    )(part, first, queries, keys, starts, d_mixed, lse)


def rotate(values, cosine, sine, sign):
    half = HD // 2
    front, back = values[..., :half], values[..., half:]
    turned = sine * sign
    return jnp.concatenate([front * cosine - back * turned, back * cosine + front * turned], axis=-1)


def to_units_q(rows):
    split = rows.reshape(2, MB, PARTS, CHUNK, HALF_KV, GROUP * HD)
    return split.transpose(4, 0, 2, 1, 3, 5).reshape(SHARDS, MB, CHUNK, GROUP * HD)


def from_units_q(units):
    split = units.reshape(HALF_KV, 2, PARTS, MB, CHUNK, GROUP * HD)
    return split.transpose(1, 3, 2, 4, 0, 5).reshape(BOTH, HQ)


def to_units_kv(keys, values):
    both = jnp.concatenate([keys, values], axis=-1).transpose(3, 0, 1, 2, 4)
    wide = jnp.broadcast_to(both[:, :, None], (HALF_KV, 2, PARTS, MB, SPAN, 2 * HD))
    return wide.reshape(SHARDS, MB, SPAN, 2 * HD)


def piece_perm():
    return [(k * SHARDS + s, (s // 16) * SHARDS + 2 * (s % 16) + k) for k in range(2) for s in range(SHARDS)]


def row_pieces(core, local):
    half = lax.dynamic_slice_in_dim(local, core * (D // 2), D // 2, axis=1)
    return lax.ppermute(half, ("c",) + SHARD, piece_perm())


def row_half(piece):
    rows = piece.shape[0]
    whole = lax.all_gather(piece, SHARD, axis=0, tiled=True)
    return whole.reshape(16, 2, rows, D // 2).transpose(0, 2, 1, 3).reshape(16 * rows, D)


def col_half(core, local):
    half = local.shape[1] // 2
    return lax.dynamic_slice_in_dim(local, core * half, half, axis=1)


def add_x(values):
    return values.astype(jnp.float32) + lax.ppermute(values, "xl", [(0, 1), (1, 0)]).astype(jnp.float32)


def join_cores(core, mine):
    other = swap(mine)
    first = jnp.where(core == 0, mine, other)
    second = jnp.where(core == 0, other, mine)
    return jnp.concatenate([first, second], axis=1).astype(jnp.float32)


def scatter_sum(values):
    return jnp.sum(exchange(values).astype(jnp.float32), axis=0).astype(jnp.bfloat16)


def own_rows(core, piece):
    back = lax.ppermute(piece, ("c",) + SHARD, [(b, a) for a, b in piece_perm()])
    return join_cores(core, back)


def to_pieces(grad):
    rows = grad.shape[0] // 16
    return grad.reshape(16, rows, 2, D // 2).transpose(0, 2, 1, 3).reshape(SHARDS, rows, D // 2)


def on_device(
    hidden_in,
    doc_ids,
    out_grad,
    norm_attn,
    w_query,
    w_key,
    w_value,
    w_out,
    norm_ffn,
    w_gate,
    w_up,
    w_down,
):
    core = lax.axis_index("c")
    shard = lax.axis_index(SHARD)
    low = jnp.bfloat16

    packed = jnp.concatenate([doc_ids.reshape(-1).astype(low), norm_attn, norm_ffn])
    small = exchange(jnp.broadcast_to(packed[None, None], (SHARDS, 1, packed.shape[0])))[:, 0]
    docs_mine = small[:, :ROWS].reshape(SHARDS, MB, SPAN).transpose(1, 0, 2).reshape(MB, SEQ)
    gain_attn = small[:, ROWS : ROWS + 48].reshape(D).astype(jnp.float32)
    gain_ffn = small[:, ROWS + 48 :].reshape(D).astype(jnp.float32)
    docs_other = swap(docs_mine)

    w_qkv = lax.all_gather(
        jnp.concatenate([col_half(core, w_query), col_half(core, w_key), col_half(core, w_value)], axis=1),
        SHARD,
        axis=0,
        tiled=True,
    )
    w_o = row_half(row_pieces(core, w_out))
    w_gu = lax.all_gather(
        jnp.concatenate([col_half(core, w_gate), col_half(core, w_up)], axis=1), SHARD, axis=0, tiled=True
    )
    w_d = row_half(row_pieces(core, w_down))

    x_low = hidden_in.reshape(ROWS, D)
    x = x_low.astype(jnp.float32)
    x_both = jnp.concatenate([x_low, swap(x_low)], axis=0).astype(jnp.float32)
    dy_low = out_grad.reshape(ROWS, D)
    dy = dy_low.astype(jnp.float32)
    df = (branch_scale * jnp.concatenate([dy_low, swap(dy_low)], axis=0).astype(jnp.float32)).astype(low)

    which = lax.rem(shard // PARTS, 2)
    part = lax.rem(shard, PARTS)
    docs = jnp.where(which == 0, docs_mine, docs_other).astype(jnp.float32)
    counted = jnp.sum((docs[:, None, :] < docs[:, :, None]).astype(jnp.int32), axis=-1)
    q_start = lax.dynamic_slice_in_dim(counted.reshape(MB, SHARDS, SPAN), part * CHUNK, CHUNK, axis=2)
    q_start = q_start.reshape(MB, TILES, 1, TILE * CHUNK)
    first = (q_start[:, :, 0, 0] // BLOCK).reshape(-1)
    starts = jnp.broadcast_to(q_start, (MB, TILES, GROUP, TILE * CHUNK)).reshape(MB, TILES, TROWS, 1)
    starts = jnp.broadcast_to(starts, (MB, TILES, TROWS, 128))
    part_arr = part.reshape(1).astype(jnp.int32)

    places = (shard * SPAN + jnp.arange(SPAN, dtype=jnp.int32)).astype(jnp.float32)
    half_size = HD // 2
    inverse = jnp.exp(-jnp.arange(half_size, dtype=jnp.float32) * (math.log(10000.0) / half_size))
    angles = places[:, None] * inverse[None, :]
    cosine, sine = jnp.cos(angles)[:, None, :], jnp.sin(angles)[:, None, :]

    r1_both = lax.rsqrt(jnp.mean(x_both * x_both, axis=-1, keepdims=True) + eps_norm)
    r1 = r1_both[:ROWS]
    n1 = (x_both * r1_both * gain_attn).astype(low)
    qkv = product(n1, w_qkv)
    q5 = qkv[:, :HQ].reshape(2, MB, SPAN, HALF_KV * GROUP, HD)
    k5 = qkv[:, HQ : HQ + HK].reshape(2, MB, SPAN, HALF_KV, HD)
    v5 = qkv[:, HQ + HK :].reshape(2, MB, SPAN, HALF_KV, HD).astype(low)
    q_rot = rotate(q5, cosine, sine, 1.0).astype(low).reshape(BOTH, HQ)
    k_rot = rotate(k5, cosine, sine, 1.0).astype(low)
    unit_q = exchange(to_units_q(q_rot))
    unit_kv = exchange(to_units_kv(k_rot, v5))
    unit_o, lse = attend_fwd(part_arr, first, unit_q, unit_kv, starts)
    attn = from_units_q(exchange(unit_o))
    y1 = product(attn, w_o)
    hmid = x + branch_scale * (y1[:ROWS] + swap(y1[ROWS:].astype(low)).astype(jnp.float32))

    r2 = lax.rsqrt(jnp.mean(hmid * hmid, axis=-1, keepdims=True) + eps_norm)
    z2 = hmid * r2
    n2_mine = (z2 * gain_ffn).astype(low)
    n2 = jnp.concatenate([n2_mine, swap(n2_mine)], axis=0)
    gu = product(n2, w_gu)
    gate, up = gu[:, :HF], gu[:, HF:]
    sigma = jax.nn.sigmoid(gate)
    silu = gate * sigma
    act = (silu * up).astype(low)
    y2 = product(act, w_d)
    result = hmid + branch_scale * (y2[:ROWS] + swap(y2[ROWS:].astype(low)).astype(jnp.float32))

    g_down = t_product(act, df).astype(low)
    d_act = product_t(df, w_d)
    d_gate = (d_act * up * sigma * (1.0 + gate * (1.0 - sigma))).astype(low)
    d_up = (d_act * silu).astype(low)
    d_gu = jnp.concatenate([d_gate, d_up], axis=1)
    g_gu = t_product(n2, d_gu).astype(low)
    dn2_both = product_t(d_gu, w_gu)
    dn2 = dn2_both[:ROWS] + swap(dn2_both[ROWS:].astype(low)).astype(jnp.float32)
    e2 = dn2 * gain_ffn
    g_gain_ffn = jnp.sum(dn2 * z2, axis=0)
    dh = dy + r2 * (e2 - z2 * jnp.mean(e2 * z2, axis=-1, keepdims=True))

    da_mine = (branch_scale * dh).astype(low)
    da = jnp.concatenate([da_mine, swap(da_mine)], axis=0)
    g_o = t_product(attn, da).astype(low)
    do = product_t(da, w_o).astype(low)
    unit_do = exchange(to_units_q(do))
    unit_dq, unit_dkv = attend_bwd(part_arr, first, unit_q, unit_kv, starts, unit_do, lse)
    dq = from_units_q(exchange(unit_dq)).astype(jnp.float32)
    dkv = exchange(unit_dkv).reshape(HALF_KV, 2, PARTS, MB, SPAN, 2 * HD).astype(jnp.float32)
    dkv = jnp.sum(dkv, axis=2).transpose(1, 2, 3, 0, 4)
    dq = rotate(dq.reshape(2, MB, SPAN, HALF_KV * GROUP, HD), cosine, sine, -1.0).reshape(BOTH, HQ)
    dk = rotate(dkv[..., :HD], cosine, sine, -1.0).reshape(BOTH, HK)
    dv = dkv[..., HD:].reshape(BOTH, HK)
    d_qkv = jnp.concatenate([dq, dk, dv], axis=1).astype(low)
    g_qkv = t_product(n1, d_qkv).astype(low)
    dn1_both = product_t(d_qkv, w_qkv)
    dn1 = dn1_both[:ROWS] + swap(dn1_both[ROWS:].astype(low)).astype(jnp.float32)
    z1 = x * r1
    e1 = dn1 * gain_attn
    g_gain_attn = jnp.sum(dn1 * z1, axis=0)
    grad_in = (dh + r1 * (e1 - z1 * jnp.mean(e1 * z1, axis=-1, keepdims=True))).astype(low)

    s_gu = add_x(lax.psum_scatter(g_gu, SHARD, scatter_dimension=0, tiled=True)).astype(low)
    s_d = add_x(
        lax.psum_scatter(to_pieces(g_down), SHARD, scatter_dimension=0, tiled=True)[0]
    ).astype(low)
    s_qkv = add_x(scatter_sum(g_qkv.reshape(SHARDS, 48, HQ + 2 * HK))).astype(low)
    s_o = add_x(scatter_sum(to_pieces(g_o))).astype(low)
    gains = jnp.stack([g_gain_attn.reshape(SHARDS, 48), g_gain_ffn.reshape(SHARDS, 48)], axis=1)
    s_gain = add_x(jnp.sum(exchange(gains), axis=0))
    s_gain = s_gain + swap(s_gain)

    return (
        result.reshape(1, MB, SPAN, D).astype(low),
        grad_in.reshape(1, MB, SPAN, D),
        s_gain[0],
        join_cores(core, s_qkv[:, :HQ]),
        join_cores(core, s_qkv[:, HQ : HQ + HK]),
        join_cores(core, s_qkv[:, HQ + HK :]),
        own_rows(core, s_o),
        s_gain[1],
        join_cores(core, s_gu[:, :HF]),
        join_cores(core, s_gu[:, HF:]),
        own_rows(core, s_d),
    )


def solution(mesh):
    fine = Mesh(mesh.devices.reshape(2, 2, 4, 4, 2), ("xl", "c", "z", "y", "xh"))
    replica = ("xl", "c")
    tokens = P(replica, None, SHARD, None)
    matrix = P(SHARD, None)
    vector = P(SHARD)
    return jax.shard_map(
        on_device,
        mesh=fine,
        in_specs=(
            tokens,
            P(replica, None, SHARD),
            tokens,
            vector,
            matrix,
            matrix,
            matrix,
            matrix,
            vector,
            matrix,
            matrix,
            matrix,
        ),
        out_specs=(
            tokens,
            tokens,
            vector,
            matrix,
            matrix,
            matrix,
            matrix,
            vector,
            matrix,
            matrix,
            matrix,
        ),
        check_vma=False,
    )
```

```python
from functools import partial
import math

import jax
import jax.numpy as jnp
from jax import lax
from jax.experimental import pallas as pl
from jax.experimental.pallas import tpu as pltpu
from jax.sharding import Mesh
from jax.sharding import PartitionSpec as P

HEADS = 24
KVH = 8
HD = 64
D = 1536
FF = 3840
MB = 3
SPAN = 64
SHARDS = 32
SEQ = 2048
PARTS = 4
ROWS = MB * SPAN
BOTH = 2 * ROWS
GROUP = HEADS // KVH
HALF_KV = KVH // 2
HQ = HALF_KV * GROUP * HD
HK = HALF_KV * HD
HF = FF // 2
QKV = HQ + 2 * HK
CHUNK = SPAN // PARTS
TILE = 4
TILES = SHARDS // TILE
BLOCK = TILE * SPAN
TROWS = GROUP * TILE * CHUNK

SHARD = ("z", "y", "xh")
branch_scale = 1.4 / math.sqrt(52.0)
eps_norm = 1e-05
NEG = -1e30
VMEM_LIMIT = 48 * 1024 * 1024


def product(left, right):
    return jnp.dot(left, right, preferred_element_type=jnp.float32)


def product_t(left, right):
    return lax.dot_general(left, right, (((1,), (1,)), ((), ())), preferred_element_type=jnp.float32)


def t_product(left, right):
    return lax.dot_general(left, right, (((0,), (0,)), ((), ())), preferred_element_type=jnp.float32)


def swap(values):
    return lax.ppermute(values, "c", [(0, 1), (1, 0)])


def exchange(values):
    return lax.all_to_all(values, SHARD, 0, 0, tiled=True)


Q_ROWS = 2 * CHUNK
ALL_ROWS = SPAN + Q_ROWS


def to_groups(rows):
    parts = [rows[:, 192 * j : 192 * j + 128] for j in range(HALF_KV)]
    parts += [rows[:, 192 * j + 128 : 192 * j + 192] for j in range(HALF_KV)]
    return jnp.concatenate(parts, axis=1)


def from_groups(rows):
    parts = []
    for j in range(HALF_KV):
        parts += [rows[:, 128 * j : 128 * j + 128], rows[:, 512 + 64 * j : 576 + 64 * j]]
    return jnp.concatenate(parts, axis=1)


def interleave(keys, values):
    parts = []
    for j in range(HALF_KV):
        parts += [keys[:, HD * j : HD * j + HD], values[:, HD * j : HD * j + HD]]
    return jnp.concatenate(parts, axis=1)


def turn(values, cosine, sine):
    lane = lax.broadcasted_iota(jnp.int32, values.shape, values.ndim - 1)
    axis = values.ndim - 1
    other = jnp.where(lane % HD < HD // 2, pltpu.roll(values, 128 - HD // 2, axis), pltpu.roll(values, HD // 2, axis))
    return values * cosine + other * sine


def project_kernel(n_ref, w_ref, table_ref, out_ref):
    rows = n_ref[...]

    def group(g, table):
        wide = product(rows, w_ref[:, 128 * g : 128 * g + 128]).reshape(2 * MB, SPAN, 128)
        return turn(wide, table_ref[table][None], table_ref[table + 1][None]).astype(jnp.bfloat16)

    for j in range(HALF_KV):
        first, both = group(j, 0), group(6 + j, 2)
        if j % 2 == 0:
            third = group(4 + j // 2, 0)
        for o in range(2):
            for m in range(MB):
                for p in range(PARTS):
                    cut = slice(p * CHUNK, (p + 1) * CHUNK)
                    out_ref[j, o, p, m, 0:SPAN, :] = both[o * MB + m]
                    out_ref[j, o, p, m, SPAN : SPAN + CHUNK, :] = first[o * MB + m, cut]
                    out_ref[j, o, p, m, SPAN + CHUNK : ALL_ROWS, :] = third[o * MB + m, cut]


def third_head(pair_even, pair_odd):
    lane = lax.broadcasted_iota(jnp.int32, pair_even.shape, pair_even.ndim - 1)
    return jnp.where(lane < HD, pair_even, pair_odd)


def out_kernel(u_ref, left_ref, right_ref, attn_ref, mine_ref, other_ref):
    for o in range(2):
        for m in range(MB):
            for p in range(PARTS):
                thirds = [
                    third_head(u_ref[2 * k, o, p, m, CHUNK:, :], u_ref[2 * k + 1, o, p, m, CHUNK:, :])
                    for k in range(2)
                ]
                parts = []
                for j in range(HALF_KV):
                    parts += [u_ref[j, o, p, m, :CHUNK, :], thirds[j // 2][:, HD * (j % 2) : HD * (j % 2) + HD]]
                at = (o * MB + m) * SPAN + p * CHUNK
                attn_ref[at : at + CHUNK, :] = jnp.concatenate(parts, axis=1)
    attn = attn_ref[...]
    for k, w_ref in enumerate((left_ref, right_ref)):
        result = product(attn, w_ref[...])
        cols = slice(k * (D // 2), (k + 1) * (D // 2))
        mine_ref[:, cols] = result[:ROWS]
        other_ref[:, cols] = result[ROWS:].astype(jnp.bfloat16)


def d_out_kernel(da_ref, left_ref, right_ref, out_ref):
    rows = product_t(da_ref[:, : D // 2], left_ref[...]) + product_t(da_ref[:, D // 2 :], right_ref[...])
    rows = rows.astype(jnp.bfloat16)
    for j in range(HALF_KV):
        first = rows[:, 192 * j : 192 * j + 128]
        if j % 2 == 0:
            third = jnp.concatenate([rows[:, 192 * j + 128 : 192 * j + 192], rows[:, 192 * j + 320 : 192 * j + 384]], axis=1)
        for o in range(2):
            for m in range(MB):
                for p in range(PARTS):
                    at = (o * MB + m) * SPAN + p * CHUNK
                    out_ref[j, o, p, m, :CHUNK, :] = first[at : at + CHUNK]
                    out_ref[j, o, p, m, CHUNK:, :] = third[at : at + CHUNK]


def collect_kernel(u_ref, table_ref, out_ref):
    def put(g, o, m, at, size, values, table, row):
        cosine = table_ref[table, row : row + size]
        sine = table_ref[table + 1, row : row + size]
        out_ref[at : at + size, 128 * g : 128 * g + 128] = turn(values, cosine, -sine).astype(jnp.bfloat16)

    wide = jnp.float32
    for o in range(2):
        for m in range(MB):
            base = (o * MB + m) * SPAN
            for j in range(HALF_KV):
                total = u_ref[j, o, 0, m, 0:SPAN, :].astype(wide)
                for p in range(1, PARTS):
                    total = total + u_ref[j, o, p, m, 0:SPAN, :].astype(wide)
                put(6 + j, o, m, base, SPAN, total, 2, 0)
            for p in range(PARTS):
                at = base + p * CHUNK
                for j in range(HALF_KV):
                    first = u_ref[j, o, p, m, SPAN : SPAN + CHUNK, :].astype(wide)
                    put(j, o, m, at, CHUNK, first, 0, p * CHUNK)
                for k in range(2):
                    third = third_head(
                        u_ref[2 * k, o, p, m, SPAN + CHUNK : ALL_ROWS, :].astype(wide),
                        u_ref[2 * k + 1, o, p, m, SPAN + CHUNK : ALL_ROWS, :].astype(wide),
                    )
                    put(4 + k, o, m, at, CHUNK, third, 0, p * CHUNK)


def stack_heads(first, third, odd):
    last = jnp.where(odd == 1, third[:, HD:], third[:, :HD])
    return jnp.concatenate([first[:, :HD], first[:, HD:], last], axis=0)


def lay_heads(rows):
    size = TILE * CHUNK
    parts = [rows[g * size : (g + 1) * size] for g in range(GROUP)]
    shape = (TILE, CHUNK, 128)
    return (
        jnp.concatenate(parts[:2], axis=1).astype(jnp.bfloat16).reshape(shape),
        jnp.concatenate([parts[2], parts[2]], axis=1).astype(jnp.bfloat16).reshape(shape),
    )


def tile_mask(part, start_rows, tile, blocks):
    wide = blocks * BLOCK
    row = lax.broadcasted_iota(jnp.int32, (TROWS, 1), 0)
    inside = lax.rem(row, TILE * CHUNK)
    q_pos = tile * BLOCK + (inside // CHUNK) * SPAN + part * CHUNK + lax.rem(inside, CHUNK)
    k_pos = (tile + 1 - blocks) * BLOCK + lax.broadcasted_iota(jnp.int32, (TROWS, wide), 1)
    return (k_pos >= start_rows) & (k_pos <= q_pos)


def tile_queries(ref, tile, begin, odd):
    where = pl.ds(tile * TILE, TILE)
    first = ref[where, 0, begin : begin + CHUNK, :].reshape(TILE * CHUNK, 128)
    third = ref[where, 0, begin + CHUNK : begin + 2 * CHUNK, :].reshape(TILE * CHUNK, 128)
    return stack_heads(first, third, odd)


def tile_keys(ref, begin, blocks):
    return ref[pl.ds(begin * TILE, blocks * TILE), 0, 0:SPAN, :].reshape(blocks * BLOCK, 128)


def each_tile(first_ref, work):
    micro = pl.program_id(0)

    def body(tile, carry):
        needed = tile + 1 - first_ref[micro * TILES + tile]
        for blocks in range(1, TILES + 1):
            pl.when(needed == blocks)(partial(work, tile, blocks))
        return carry

    lax.fori_loop(0, TILES, body, 0)


def fwd_kernel(unit_ref, first_ref, u_ref, start_ref, o_ref, lse_ref):
    part, odd = unit_ref[0], unit_ref[1]

    def work(tile, blocks):
        q_rows = tile_queries(u_ref, tile, SPAN, odd) * jnp.bfloat16(0.125)
        keys = tile_keys(u_ref, tile + 1 - blocks, blocks)
        scores = product_t(q_rows, keys[:, :HD])
        allowed = tile_mask(part, start_ref[0, tile][:, :1], tile, blocks)
        scores = jnp.where(allowed, scores, NEG)
        highest = jnp.max(scores, axis=-1, keepdims=True)
        expo = jnp.exp(scores - highest)
        total = jnp.sum(expo, axis=-1, keepdims=True)
        mixed = product(expo.astype(jnp.bfloat16), keys[:, HD:]) / total
        where = pl.ds(tile * TILE, TILE)
        o_ref[where, 0, :CHUNK, :], o_ref[where, 0, CHUNK:, :] = lay_heads(mixed)
        lse_ref[0, tile] = jnp.broadcast_to(highest + jnp.log(total), (TROWS, 128))

    each_tile(first_ref, work)


def bwd_kernel(unit_ref, first_ref, u_ref, start_ref, do_ref, lse_ref, d_ref, acc):
    part, odd = unit_ref[0], unit_ref[1]
    acc[...] = jnp.zeros_like(acc)

    def work(tile, blocks):
        begin = tile + 1 - blocks
        q_rows = tile_queries(u_ref, tile, SPAN, odd) * jnp.bfloat16(0.125)
        d_rows = tile_queries(do_ref, tile, 0, odd)
        keys = tile_keys(u_ref, begin, blocks)
        scores = product_t(q_rows, keys[:, :HD])
        allowed = tile_mask(part, start_ref[0, tile][:, :1], tile, blocks)
        probs = jnp.where(allowed, jnp.exp(scores - lse_ref[0, tile][:, :1]), 0.0)
        d_probs = product_t(d_rows, keys[:, HD:])
        offset = jnp.sum(d_probs * probs, axis=-1, keepdims=True)
        d_scores = (probs * (d_probs - offset)).astype(jnp.bfloat16)
        d_query = product(d_scores, keys[:, :HD]) * 0.125
        at = pl.ds(tile * TILE, TILE)
        d_ref[at, 0, SPAN : SPAN + CHUNK, :], d_ref[at, 0, SPAN + CHUNK : ALL_ROWS, :] = lay_heads(d_query)
        d_key = t_product(d_scores, q_rows)
        d_value = t_product(probs.astype(jnp.bfloat16), d_rows)
        where = pl.ds(begin * BLOCK, blocks * BLOCK)
        acc[where, :] += jnp.concatenate([d_key, d_value], axis=1)

    each_tile(first_ref, work)
    d_ref[:, 0, 0:SPAN, :] = acc[...].astype(jnp.bfloat16).reshape(SHARDS, SPAN, 128)


SMEM = pl.BlockSpec(memory_space=pltpu.SMEM)
UNIT_SPEC = pl.BlockSpec((SHARDS, 1, ALL_ROWS, 128), lambda m: (0, m, 0, 0))
QUERY_SPEC = pl.BlockSpec((SHARDS, 1, Q_ROWS, 128), lambda m: (0, m, 0, 0))
COL_SPEC = pl.BlockSpec((1, TILES, TROWS, 128), lambda m: (m, 0, 0, 0))
COL_SHAPE = jax.ShapeDtypeStruct((MB, TILES, TROWS, 128), jnp.float32)
PARAMS = pltpu.CompilerParams(vmem_limit_bytes=VMEM_LIMIT)


def split_units(values):
    return values.reshape((HALF_KV, 2, PARTS) + values.shape[1:])


def low_shape(*dims):
    return jax.ShapeDtypeStruct(dims, jnp.bfloat16)


def project(n1, w_qkv, tables):
    shape = low_shape(HALF_KV, 2, PARTS, MB, ALL_ROWS, 128)
    out = pl.pallas_call(project_kernel, out_shape=shape, compiler_params=PARAMS, name="project")(n1, w_qkv, tables)
    return out.reshape(SHARDS, MB, ALL_ROWS, 128)


def out_project(units, w_o):
    return pl.pallas_call(
        out_kernel,
        out_shape=[low_shape(BOTH, HQ), jax.ShapeDtypeStruct((ROWS, D), jnp.float32), low_shape(ROWS, D)],
        compiler_params=PARAMS,
        name="out_project",
    )(split_units(units), *w_o)


def d_out_project(da, w_o):
    shape = low_shape(HALF_KV, 2, PARTS, MB, Q_ROWS, 128)
    out = pl.pallas_call(d_out_kernel, out_shape=shape, compiler_params=PARAMS, name="d_out_project")(da, *w_o)
    return out.reshape(SHARDS, MB, Q_ROWS, 128)


def collect(units, tables):
    shape = low_shape(BOTH, HQ + 2 * HK)
    return pl.pallas_call(collect_kernel, out_shape=shape, compiler_params=PARAMS, name="collect")(
        split_units(units), tables
    )


def attend_fwd(unit, first, units, starts):
    return pl.pallas_call(
        fwd_kernel,
        grid=(MB,),
        in_specs=[SMEM, SMEM, UNIT_SPEC, COL_SPEC],
        out_specs=[QUERY_SPEC, COL_SPEC],
        out_shape=[low_shape(SHARDS, MB, Q_ROWS, 128), COL_SHAPE],
        compiler_params=PARAMS,
        name="attend_forward",
    )(unit, first, units, starts)


def attend_bwd(unit, first, units, starts, d_mixed, lse):
    return pl.pallas_call(
        bwd_kernel,
        grid=(MB,),
        in_specs=[SMEM, SMEM, UNIT_SPEC, COL_SPEC, QUERY_SPEC, COL_SPEC],
        out_specs=UNIT_SPEC,
        out_shape=low_shape(SHARDS, MB, ALL_ROWS, 128),
        scratch_shapes=[pltpu.VMEM((SEQ, 128), jnp.float32)],
        compiler_params=PARAMS,
        name="attend_backward",
    )(unit, first, units, starts, d_mixed, lse)


def piece_perm():
    return [(k * SHARDS + s, (s // 16) * SHARDS + 2 * (s % 16) + k) for k in range(2) for s in range(SHARDS)]


def shift(values, axis, step):
    if axis == "x":
        line = lambda x: (x % 2) * 2 + x // 2
        return lax.ppermute(values, ("xl", "xh"), [(line(i), line((i + step) % 4)) for i in range(4)])
    return lax.ppermute(values, axis, [(i, (i + step) % 4) for i in range(4)])


def place(axis):
    if axis == "x":
        return lax.axis_index("xh") * 2 + lax.axis_index("xl")
    return lax.axis_index(axis)


def flip(values, axis):
    return lax.ppermute(values, axis, [(0, 1), (1, 0)])


def col_half(core, local):
    half = local.shape[1] // 2
    return lax.dynamic_slice_in_dim(local, core * half, half, axis=1)


def fold(rows, parts):
    n, r, w = rows.shape
    return rows.reshape(n, r, parts, w // parts).transpose(0, 2, 1, 3).reshape(n, parts * r, w // parts)


def unfold(rows, parts):
    n, r, w = rows.shape
    return rows.reshape(n, parts, r // parts, w).transpose(0, 2, 1, 3).reshape(n, r // parts, parts * w)


def wide_sum(*values):
    total = values[0].astype(jnp.float32)
    for value in values[1:]:
        total = total + value.astype(jnp.float32)
    return total.astype(jnp.bfloat16)


def after(values, event):
    return lax.optimization_barrier((values, event))[0]


def total_axis(values, axis):
    return values + shift(values, axis, 1) + shift(values, axis, 2) + shift(values, axis, 3)


def reduce_pair(values, axis, dim):
    size = values.shape[dim] // 2
    me = lax.axis_index(axis)
    keep = lax.dynamic_slice_in_dim(values, me * size, size, axis=dim)
    send = lax.dynamic_slice_in_dim(values, (1 - me) * size, size, axis=dim)
    return wide_sum(keep, flip(send, axis))


def add_pair(values, axis):
    return wide_sum(values, flip(values, axis))


def join_pair(mine, axis, dim):
    other = flip(mine, axis)
    lower = lax.axis_index(axis) == 0
    return jnp.concatenate([jnp.where(lower, mine, other), jnp.where(lower, other, mine)], axis=dim)


def join_cores(mine):
    return join_pair(mine, "c", 1).astype(jnp.float32)


def scatter_sum(values):
    return jnp.sum(exchange(values).astype(jnp.float32), axis=0).astype(jnp.bfloat16)


def on_device(
    hidden_in,
    doc_ids,
    out_grad,
    norm_attn,
    w_query,
    w_key,
    w_value,
    w_out,
    norm_ffn,
    w_gate,
    w_up,
    w_down,
):
    core = lax.axis_index("c")
    shard = lax.axis_index(SHARD)
    low = jnp.bfloat16

    rows_in = lax.ppermute(jnp.concatenate([w_out, w_down], axis=0), ("c",) + SHARD, piece_perm())
    gu_piece = jnp.concatenate([col_half(core, w_gate), col_half(core, w_up)], axis=1)
    w_all = lax.all_gather(
        jnp.concatenate(
            [
                join_pair(gu_piece, "xh", 0),
                rows_in[48:144],
                fold(rows_in[144:][None], 4)[0],
                fold(rows_in[:48][None], 2)[0],
            ],
            axis=1,
        ),
        ("z", "y"),
        axis=0,
        tiled=True,
    )
    w_gu = w_all[:, :FF]
    w_d = jnp.concatenate(
        [w_all[:, FF : FF + D].reshape(16, 96, D), unfold(w_all[:, FF + D : FF + 5 * D // 4].reshape(16, 96, D // 4), 4)],
        axis=1,
    ).reshape(HF, D)
    w_o = w_all[:, FF + 5 * D // 4 :].reshape(16, 2, 48, D // 2)
    w_o = [w_o[:, k].reshape(HQ, D // 2) for k in range(2)]
    small = jnp.concatenate(
        [norm_attn[:, None], norm_ffn[:, None], doc_ids.reshape(48, 4).astype(low), jnp.zeros((48, 122), low)], axis=1
    )
    piece = jnp.concatenate(
        [to_groups(col_half(core, w_query)), interleave(col_half(core, w_key), col_half(core, w_value)), small], axis=1
    )
    w_first = exchange(jnp.broadcast_to(piece[None], (SHARDS, 48, QKV + 128)))
    small = w_first[:, :, QKV : QKV + 6]
    w_first = w_first.reshape(D, QKV + 128)
    w_qkv = w_first[:, :QKV]
    gain_attn = small[:, :, 0].reshape(1, D).astype(jnp.float32)
    gain_ffn = small[:, :, 1].reshape(1, D).astype(jnp.float32)
    docs_mine = small[:, :, 2:].reshape(SHARDS, MB, SPAN).transpose(1, 0, 2).reshape(MB, SEQ)
    docs_other = swap(docs_mine)

    x_low = hidden_in.reshape(ROWS, D)
    x = x_low.astype(jnp.float32)
    x_both = jnp.concatenate([x_low, swap(x_low)], axis=0).astype(jnp.float32)
    dy_low = out_grad.reshape(ROWS, D)
    dy = dy_low.astype(jnp.float32)
    df = (branch_scale * jnp.concatenate([dy_low, swap(dy_low)], axis=0).astype(jnp.float32)).astype(low)

    which = lax.rem(shard // PARTS, 2)
    part = lax.rem(shard, PARTS)
    docs = jnp.where(which == 0, docs_mine, docs_other).astype(jnp.float32)
    counted = jnp.sum((docs[:, None, :] < docs[:, :, None]).astype(jnp.int32), axis=-1)
    q_start = lax.dynamic_slice_in_dim(counted.reshape(MB, SHARDS, SPAN), part * CHUNK, CHUNK, axis=2)
    q_start = q_start.reshape(MB, TILES, 1, TILE * CHUNK)
    first = (q_start[:, :, 0, 0] // BLOCK).reshape(-1)
    starts = jnp.broadcast_to(q_start, (MB, TILES, GROUP, TILE * CHUNK)).reshape(MB, TILES, TROWS, 1)
    starts = jnp.broadcast_to(starts, (MB, TILES, TROWS, 128))
    unit = jnp.stack([part, lax.rem(shard // (2 * PARTS), 2)]).astype(jnp.int32)

    places = (shard * SPAN + jnp.arange(SPAN, dtype=jnp.int32)).astype(jnp.float32)
    half_size = HD // 2
    inverse = jnp.exp(-jnp.arange(half_size, dtype=jnp.float32) * (math.log(10000.0) / half_size))
    angles = places[:, None] * inverse[None, :]
    cosine, sine = jnp.cos(angles), jnp.sin(angles)
    cosine = jnp.concatenate([cosine, cosine], axis=1)
    sine = jnp.concatenate([-sine, sine], axis=1)
    tables = jnp.stack(
        [
            jnp.concatenate([cosine, cosine], axis=1),
            jnp.concatenate([sine, sine], axis=1),
            jnp.concatenate([cosine, jnp.ones_like(cosine)], axis=1),
            jnp.concatenate([sine, jnp.zeros_like(sine)], axis=1),
        ]
    )

    r1_both = lax.rsqrt(jnp.mean(x_both * x_both, axis=-1, keepdims=True) + eps_norm)
    r1 = r1_both[:ROWS]
    n1 = (x_both * r1_both * gain_attn).astype(low)
    units = exchange(project(n1, w_first, tables))
    unit_o, lse = attend_fwd(unit, first, units, starts)
    attn, y1_mine, y1_other = out_project(exchange(unit_o), w_o)
    hmid = x + branch_scale * (y1_mine + swap(y1_other).astype(jnp.float32))

    r2 = lax.rsqrt(jnp.mean(hmid * hmid, axis=-1, keepdims=True) + eps_norm)
    z2 = hmid * r2
    n2_mine = (z2 * gain_ffn).astype(low)
    n2 = jnp.concatenate([n2_mine, swap(n2_mine)], axis=0)
    gu = product(n2, w_gu)
    gate, up = gu[:, :HF], gu[:, HF:]
    sigma = jax.nn.sigmoid(gate)
    silu = gate * sigma
    act = (silu * up).astype(low)
    y2 = product(act, w_d)
    result = hmid + branch_scale * (y2[:ROWS] + swap(y2[ROWS:].astype(low)).astype(jnp.float32))

    d_act = product_t(df, w_d)
    d_gate = (d_act * up * sigma * (1.0 + gate * (1.0 - sigma))).astype(low)
    d_up = (d_act * silu).astype(low)
    d_gu = jnp.concatenate([d_gate, d_up], axis=1)
    g_down = t_product(act, df).astype(low).reshape(16, 120, D)
    g_ffn = jnp.concatenate(
        [t_product(n2, d_gu).astype(low), g_down[:, :96].reshape(D, D), fold(g_down[:, 96:], 4).reshape(D, D // 4)],
        axis=1,
    )
    s_ffn = lax.psum_scatter(g_ffn, ("z", "y"), scatter_dimension=0, tiled=True)
    dn2_both = product_t(d_gu, w_gu)
    dn2 = dn2_both[:ROWS] + swap(dn2_both[ROWS:].astype(low)).astype(jnp.float32)
    e2 = dn2 * gain_ffn
    g_gain_ffn = jnp.sum(dn2 * z2, axis=0)
    dh = dy + r2 * (e2 - z2 * jnp.mean(e2 * z2, axis=-1, keepdims=True))

    da_mine = (branch_scale * dh).astype(low)
    da = jnp.concatenate([da_mine, swap(da_mine)], axis=0)
    unit_do = exchange(d_out_project(da, w_o))
    g_o = [t_product(attn, da[:, k * (D // 2) : (k + 1) * (D // 2)]).astype(low) for k in range(2)]
    g_o = jnp.stack([g.reshape(16, 48, D // 2) for g in g_o], axis=1).reshape(SHARDS, 48, D // 2)
    s_o = scatter_sum(after(g_o, unit_do))
    unit_d = attend_bwd(unit, first, units, starts, unit_do, lse)
    d_qkv = collect(exchange(unit_d), tables)

    g_qkv = t_product(n1, d_qkv).astype(low)
    s_qkv = scatter_sum(g_qkv.reshape(SHARDS, 48, HQ + 2 * HK))
    dn1_both = product_t(d_qkv, w_qkv)
    dn1 = dn1_both[:ROWS] + swap(dn1_both[ROWS:].astype(low)).astype(jnp.float32)
    z1 = x * r1
    e1 = dn1 * gain_attn
    g_gain_attn = jnp.sum(dn1 * z1, axis=0)
    grad_in = (dh + r1 * (e1 - z1 * jnp.mean(e1 * z1, axis=-1, keepdims=True))).astype(low)

    s_ffn, s_o = after((s_ffn, s_o), d_qkv)
    back = [(b, a) for a, b in piece_perm()]
    s_o = join_cores(lax.ppermute(add_pair(s_o, "xl"), ("c",) + SHARD, back))
    s_d = jnp.concatenate([s_ffn[:, FF : FF + D], unfold(s_ffn[None, :, FF + D :], 4)[0]], axis=0)
    s_d = lax.ppermute(add_pair(s_d, "xl"), ("c",) + SHARD, back)
    s_d = s_d.astype(jnp.float32) + swap(s_d).astype(jnp.float32)
    s_gu = add_pair(reduce_pair(s_ffn[:, :FF], "xh", 0), "xl")
    other = swap(s_gu)
    lower = core == 0
    g_g, g_u = [
        jnp.concatenate([jnp.where(lower, m, t), jnp.where(lower, t, m)], axis=1).astype(jnp.float32)
        for m, t in ((s_gu[:, :HF], other[:, :HF]), (s_gu[:, HF:], other[:, HF:]))
    ]
    gains = jnp.stack([g_gain_attn, g_gain_ffn])
    gains = gains + swap(gains)
    gains = total_axis(total_axis(total_axis(gains, "x"), "y"), "z")
    gains = lax.dynamic_slice_in_dim(gains, shard * 48, 48, axis=1)
    s_qkv = add_pair(s_qkv, "xl")
    other = swap(s_qkv)
    whole = [jnp.where(lower, s_qkv, other), jnp.where(lower, other, s_qkv)]

    def heads_of(offset):
        return jnp.concatenate(
            [w[:, HQ + 128 * j + offset : HQ + 128 * j + offset + HD] for w in whole for j in range(HALF_KV)], axis=1
        ).astype(jnp.float32)

    return (
        result.reshape(1, MB, SPAN, D).astype(low),
        grad_in.reshape(1, MB, SPAN, D),
        gains[0],
        jnp.concatenate([from_groups(w[:, :HQ]) for w in whole], axis=1).astype(jnp.float32),
        heads_of(0),
        heads_of(HD),
        s_o,
        gains[1],
        g_g,
        g_u,
        s_d,
    )


def solution(mesh):
    fine = Mesh(mesh.devices.reshape(2, 2, 4, 4, 2), ("xl", "c", "z", "y", "xh"))
    replica = ("xl", "c")
    tokens = P(replica, None, SHARD, None)
    matrix = P(SHARD, None)
    vector = P(SHARD)
    return jax.shard_map(
        on_device,
        mesh=fine,
        in_specs=(
            tokens,
            P(replica, None, SHARD),
            tokens,
            vector,
            matrix,
            matrix,
            matrix,
            matrix,
            vector,
            matrix,
            matrix,
            matrix,
        ),
        out_specs=(
            tokens,
            tokens,
            vector,
            matrix,
            matrix,
            matrix,
            matrix,
            vector,
            matrix,
            matrix,
            matrix,
        ),
        check_vma=False,
    )
```

```python
from functools import partial
import math

import jax
import jax.numpy as jnp
from jax import lax
from jax.experimental import pallas as pl
from jax.experimental.pallas import tpu as pltpu
from jax.sharding import Mesh
from jax.sharding import PartitionSpec as P

HEADS = 24
KVH = 8
HD = 64
D = 1536
FF = 3840
MB = 3
SPAN = 64
SHARDS = 32
SEQ = 2048
PARTS = 4
ROWS = MB * SPAN
BOTH = 2 * ROWS
GROUP = HEADS // KVH
HALF_KV = KVH // 2
HQ = HALF_KV * GROUP * HD
HK = HALF_KV * HD
HF = FF // 2
QKV = HQ + 2 * HK
UNIT_FF = 128
PAD_FF = 16 * UNIT_FF
REST_AT = D
GATE_AT = D + D // 3
UP_AT = GATE_AT + PAD_FF
OUT_AT = UP_AT + PAD_FF
FF_TILE = 256
FF_TILES = PAD_FF // FF_TILE
FF_ROWS = 96 * FF_TILE // UNIT_FF
CHUNK = SPAN // PARTS
TILE = 4
TILES = SHARDS // TILE
BLOCK = TILE * SPAN
TROWS = GROUP * TILE * CHUNK

SHARD = ("z", "y", "xh")
branch_scale = 1.4 / math.sqrt(52.0)
eps_norm = 1e-05
NEG = -1e30
VMEM_LIMIT = 48 * 1024 * 1024


def product(left, right):
    return jnp.dot(left, right, preferred_element_type=jnp.float32)


def product_t(left, right):
    return lax.dot_general(left, right, (((1,), (1,)), ((), ())), preferred_element_type=jnp.float32)


def t_product(left, right):
    return lax.dot_general(left, right, (((0,), (0,)), ((), ())), preferred_element_type=jnp.float32)


def swap(values):
    return lax.ppermute(values, "c", [(0, 1), (1, 0)])


def exchange(values):
    return lax.all_to_all(values, SHARD, 0, 0, tiled=True)


Q_ROWS = 2 * CHUNK
ALL_ROWS = SPAN + Q_ROWS


def to_groups(rows):
    parts = [rows[:, 192 * j : 192 * j + 128] for j in range(HALF_KV)]
    parts += [rows[:, 192 * j + 128 : 192 * j + 192] for j in range(HALF_KV)]
    return jnp.concatenate(parts, axis=1)


def from_groups(rows):
    parts = []
    for j in range(HALF_KV):
        parts += [rows[:, 128 * j : 128 * j + 128], rows[:, 512 + 64 * j : 576 + 64 * j]]
    return jnp.concatenate(parts, axis=1)


def interleave(keys, values):
    parts = []
    for j in range(HALF_KV):
        parts += [keys[:, HD * j : HD * j + HD], values[:, HD * j : HD * j + HD]]
    return jnp.concatenate(parts, axis=1)


def turn(values, cosine, sine):
    lane = lax.broadcasted_iota(jnp.int32, values.shape, values.ndim - 1)
    axis = values.ndim - 1
    other = jnp.where(lane % HD < HD // 2, pltpu.roll(values, 128 - HD // 2, axis), pltpu.roll(values, HD // 2, axis))
    return values * cosine + other * sine


def project_kernel(n_ref, w_ref, table_ref, out_ref):
    rows = n_ref[...]

    def group(g, table):
        wide = product(rows, w_ref[:, 128 * g : 128 * g + 128]).reshape(2 * MB, SPAN, 128)
        return turn(wide, table_ref[table][None], table_ref[table + 1][None]).astype(jnp.bfloat16)

    for j in range(HALF_KV):
        first, both = group(j, 0), group(6 + j, 2)
        if j % 2 == 0:
            third = group(4 + j // 2, 0)
        for o in range(2):
            for m in range(MB):
                for p in range(PARTS):
                    cut = slice(p * CHUNK, (p + 1) * CHUNK)
                    out_ref[j, o, p, m, 0:SPAN, :] = both[o * MB + m]
                    out_ref[j, o, p, m, SPAN : SPAN + CHUNK, :] = first[o * MB + m, cut]
                    out_ref[j, o, p, m, SPAN + CHUNK : ALL_ROWS, :] = third[o * MB + m, cut]


def third_head(pair_even, pair_odd):
    lane = lax.broadcasted_iota(jnp.int32, pair_even.shape, pair_even.ndim - 1)
    return jnp.where(lane < HD, pair_even, pair_odd)


def out_halves(ref):
    whole = ref[...].reshape(16, 2, 48, D // 2)
    return whole[:, 0].reshape(HQ, D // 2), whole[:, 1].reshape(HQ, D // 2)


def out_kernel(u_ref, w_ref, attn_ref, mine_ref, other_ref):
    for o in range(2):
        for m in range(MB):
            for p in range(PARTS):
                thirds = [
                    third_head(u_ref[2 * k, o, p, m, CHUNK:, :], u_ref[2 * k + 1, o, p, m, CHUNK:, :])
                    for k in range(2)
                ]
                parts = []
                for j in range(HALF_KV):
                    parts += [u_ref[j, o, p, m, :CHUNK, :], thirds[j // 2][:, HD * (j % 2) : HD * (j % 2) + HD]]
                at = (o * MB + m) * SPAN + p * CHUNK
                attn_ref[at : at + CHUNK, :] = jnp.concatenate(parts, axis=1)
    attn = attn_ref[...]
    for k, half in enumerate(out_halves(w_ref)):
        result = product(attn, half)
        cols = slice(k * (D // 2), (k + 1) * (D // 2))
        mine_ref[:, cols] = result[:ROWS]
        other_ref[:, cols] = result[ROWS:].astype(jnp.bfloat16)


def d_out_kernel(da_ref, w_ref, attn_ref, held_ref, out_ref, grad_ref, g_out, sem):
    attn_t = attn_ref[...].T
    for k in range(2):
        half = product(attn_t, da_ref[:, k * (D // 2) : (k + 1) * (D // 2)]).astype(jnp.bfloat16)
        for j in range(16):
            g_out[j * 96 + k * 48 : j * 96 + k * 48 + 48, :] = half[j * 48 : j * 48 + 48]
    copy = pltpu.make_async_copy(g_out, grad_ref.at[:, pl.ds(OUT_AT, D // 2)], sem)
    copy.start()
    left, right = out_halves(w_ref)
    rows = product_t(da_ref[:, : D // 2], left) + product_t(da_ref[:, D // 2 :], right)
    rows = rows.astype(jnp.bfloat16)
    for j in range(HALF_KV):
        first = rows[:, 192 * j : 192 * j + 128]
        if j % 2 == 0:
            third = jnp.concatenate([rows[:, 192 * j + 128 : 192 * j + 192], rows[:, 192 * j + 320 : 192 * j + 384]], axis=1)
        for o in range(2):
            for m in range(MB):
                for p in range(PARTS):
                    at = (o * MB + m) * SPAN + p * CHUNK
                    out_ref[j, o, p, m, :CHUNK, :] = first[at : at + CHUNK]
                    out_ref[j, o, p, m, CHUNK:, :] = third[at : at + CHUNK]
    copy.wait()


def collect_kernel(u_ref, table_ref, out_ref):
    def put(g, o, m, at, size, values, table, row):
        cosine = table_ref[table, row : row + size]
        sine = table_ref[table + 1, row : row + size]
        out_ref[at : at + size, 128 * g : 128 * g + 128] = turn(values, cosine, -sine).astype(jnp.bfloat16)

    wide = jnp.float32
    for o in range(2):
        for m in range(MB):
            base = (o * MB + m) * SPAN
            for j in range(HALF_KV):
                total = u_ref[j, o, 0, m, 0:SPAN, :].astype(wide)
                for p in range(1, PARTS):
                    total = total + u_ref[j, o, p, m, 0:SPAN, :].astype(wide)
                put(6 + j, o, m, base, SPAN, total, 2, 0)
            for p in range(PARTS):
                at = base + p * CHUNK
                for j in range(HALF_KV):
                    first = u_ref[j, o, p, m, SPAN : SPAN + CHUNK, :].astype(wide)
                    put(j, o, m, at, CHUNK, first, 0, p * CHUNK)
                for k in range(2):
                    third = third_head(
                        u_ref[2 * k, o, p, m, SPAN + CHUNK : ALL_ROWS, :].astype(wide),
                        u_ref[2 * k + 1, o, p, m, SPAN + CHUNK : ALL_ROWS, :].astype(wide),
                    )
                    put(4 + k, o, m, at, CHUNK, third, 0, p * CHUNK)


def stack_heads(first, third, odd):
    last = jnp.where(odd == 1, third[:, HD:], third[:, :HD])
    return jnp.concatenate([first[:, :HD], first[:, HD:], last], axis=0)


def lay_heads(rows):
    size = TILE * CHUNK
    parts = [rows[g * size : (g + 1) * size] for g in range(GROUP)]
    shape = (TILE, CHUNK, 128)
    return (
        jnp.concatenate(parts[:2], axis=1).astype(jnp.bfloat16).reshape(shape),
        jnp.concatenate([parts[2], parts[2]], axis=1).astype(jnp.bfloat16).reshape(shape),
    )


def tile_mask(part, start_rows, tile, blocks):
    wide = blocks * BLOCK
    row = lax.broadcasted_iota(jnp.int32, (TROWS, 1), 0)
    inside = lax.rem(row, TILE * CHUNK)
    q_pos = tile * BLOCK + (inside // CHUNK) * SPAN + part * CHUNK + lax.rem(inside, CHUNK)
    k_pos = (tile + 1 - blocks) * BLOCK + lax.broadcasted_iota(jnp.int32, (TROWS, wide), 1)
    return (k_pos >= start_rows) & (k_pos <= q_pos)


def tile_queries(ref, tile, begin, odd):
    where = pl.ds(tile * TILE, TILE)
    first = ref[where, 0, begin : begin + CHUNK, :].reshape(TILE * CHUNK, 128)
    third = ref[where, 0, begin + CHUNK : begin + 2 * CHUNK, :].reshape(TILE * CHUNK, 128)
    return stack_heads(first, third, odd)


def tile_keys(ref, begin, blocks):
    return ref[pl.ds(begin * TILE, blocks * TILE), 0, 0:SPAN, :].reshape(blocks * BLOCK, 128)


def each_tile(first_ref, work):
    micro = pl.program_id(0)

    def body(tile, carry):
        needed = tile + 1 - first_ref[micro * TILES + tile]
        for blocks in range(1, TILES + 1):
            pl.when(needed == blocks)(partial(work, tile, blocks))
        return carry

    lax.fori_loop(0, TILES, body, 0)


def fwd_kernel(unit_ref, first_ref, u_ref, start_ref, o_ref, lse_ref):
    part, odd = unit_ref[0], unit_ref[1]

    def work(tile, blocks):
        q_rows = tile_queries(u_ref, tile, SPAN, odd) * jnp.bfloat16(0.125)
        keys = tile_keys(u_ref, tile + 1 - blocks, blocks)
        scores = product_t(q_rows, keys[:, :HD])
        allowed = tile_mask(part, start_ref[0, tile][:, :1], tile, blocks)
        scores = jnp.where(allowed, scores, NEG)
        highest = jnp.max(scores, axis=-1, keepdims=True)
        expo = jnp.exp(scores - highest)
        total = jnp.sum(expo, axis=-1, keepdims=True)
        mixed = product(expo.astype(jnp.bfloat16), keys[:, HD:]) / total
        where = pl.ds(tile * TILE, TILE)
        o_ref[where, 0, :CHUNK, :], o_ref[where, 0, CHUNK:, :] = lay_heads(mixed)
        lse_ref[0, tile] = jnp.broadcast_to(highest + jnp.log(total), (TROWS, 128))

    each_tile(first_ref, work)


def bwd_kernel(unit_ref, first_ref, u_ref, start_ref, do_ref, lse_ref, d_ref, acc):
    part, odd = unit_ref[0], unit_ref[1]
    acc[...] = jnp.zeros_like(acc)

    def work(tile, blocks):
        begin = tile + 1 - blocks
        q_rows = tile_queries(u_ref, tile, SPAN, odd) * jnp.bfloat16(0.125)
        d_rows = tile_queries(do_ref, tile, 0, odd)
        keys = tile_keys(u_ref, begin, blocks)
        scores = product_t(q_rows, keys[:, :HD])
        allowed = tile_mask(part, start_ref[0, tile][:, :1], tile, blocks)
        probs = jnp.where(allowed, jnp.exp(scores - lse_ref[0, tile][:, :1]), 0.0)
        d_probs = product_t(d_rows, keys[:, HD:])
        offset = jnp.sum(d_probs * probs, axis=-1, keepdims=True)
        d_scores = (probs * (d_probs - offset)).astype(jnp.bfloat16)
        d_query = product(d_scores, keys[:, :HD]) * 0.125
        at = pl.ds(tile * TILE, TILE)
        d_ref[at, 0, SPAN : SPAN + CHUNK, :], d_ref[at, 0, SPAN + CHUNK : ALL_ROWS, :] = lay_heads(d_query)
        d_key = t_product(d_scores, q_rows)
        d_value = t_product(probs.astype(jnp.bfloat16), d_rows)
        where = pl.ds(begin * BLOCK, blocks * BLOCK)
        acc[where, :] += jnp.concatenate([d_key, d_value], axis=1)

    each_tile(first_ref, work)
    d_ref[:, 0, 0:SPAN, :] = acc[...].astype(jnp.bfloat16).reshape(SHARDS, SPAN, 128)


SMEM = pl.BlockSpec(memory_space=pltpu.SMEM)
UNIT_SPEC = pl.BlockSpec((SHARDS, 1, ALL_ROWS, 128), lambda m: (0, m, 0, 0))
QUERY_SPEC = pl.BlockSpec((SHARDS, 1, Q_ROWS, 128), lambda m: (0, m, 0, 0))
COL_SPEC = pl.BlockSpec((1, TILES, TROWS, 128), lambda m: (m, 0, 0, 0))
COL_SHAPE = jax.ShapeDtypeStruct((MB, TILES, TROWS, 128), jnp.float32)
PARAMS = pltpu.CompilerParams(vmem_limit_bytes=VMEM_LIMIT)


def split_units(values):
    return values.reshape((HALF_KV, 2, PARTS) + values.shape[1:])


def low_shape(*dims):
    return jax.ShapeDtypeStruct(dims, jnp.bfloat16)


def project(n1, w_qkv, tables):
    shape = low_shape(HALF_KV, 2, PARTS, MB, ALL_ROWS, 128)
    out = pl.pallas_call(project_kernel, out_shape=shape, compiler_params=PARAMS, cost_estimate=cost(6), name="project")(n1, w_qkv, tables)
    return out.reshape(SHARDS, MB, ALL_ROWS, 128)


def whole_spec(*dims):
    return pl.BlockSpec(dims, lambda i: (0,) * len(dims))


OUT_SPEC = pl.BlockSpec((D, D // 2), lambda i: (0, OUT_AT // (D // 2)))


def cost(micros):
    return pl.CostEstimate(flops=int(micros * 1e9), bytes_accessed=1 << 20, transcendentals=0)


def out_project(units, w_all):
    return pl.pallas_call(
        out_kernel,
        grid=(1,),
        in_specs=[whole_spec(HALF_KV, 2, PARTS, MB, Q_ROWS, 128), OUT_SPEC],
        out_specs=[whole_spec(BOTH, HQ), whole_spec(ROWS, D), whole_spec(ROWS, D)],
        out_shape=[low_shape(BOTH, HQ), jax.ShapeDtypeStruct((ROWS, D), jnp.float32), low_shape(ROWS, D)],
        compiler_params=PARAMS,
        cost_estimate=cost(3),
        name="out_project",
    )(split_units(units), w_all)


def d_out_project(da, w_all, attn, g_ffn):
    dims = (HALF_KV, 2, PARTS, MB, Q_ROWS, 128)
    anywhere = pl.BlockSpec(memory_space=pl.ANY)
    out, grads = pl.pallas_call(
        d_out_kernel,
        grid=(1,),
        in_specs=[whole_spec(BOTH, D), OUT_SPEC, whole_spec(BOTH, HQ), anywhere],
        out_specs=[whole_spec(*dims), anywhere],
        out_shape=[low_shape(*dims), low_shape(*g_ffn.shape)],
        scratch_shapes=[pltpu.VMEM((D, D // 2), jnp.bfloat16), pltpu.SemaphoreType.DMA],
        input_output_aliases={3: 1},
        compiler_params=PARAMS,
        cost_estimate=cost(5),
        name="d_out_project",
    )(da, w_all, attn, g_ffn)
    return out.reshape(SHARDS, MB, Q_ROWS, 128), grads


def ffn_kernel(
    n_ref, df_ref, main_ref, rest_ref, gate_ref, up_ref,
    y_mine_ref, y_other_ref, dn_mine_ref, dn_other_ref, grad_ref,
    n_t, y_acc, dn_acc, g_gate, g_up, g_main, g_rest, sems,
):
    step = pl.program_id(0)
    slot = lax.rem(step, 2)

    def copies(at, slot):
        cols, rows = at * FF_TILE, at * FF_ROWS
        return [
            pltpu.make_async_copy(
                g_gate.at[slot], grad_ref.at[:, pl.ds(pl.multiple_of(GATE_AT + cols, FF_TILE), FF_TILE)], sems.at[slot, 0]
            ),
            pltpu.make_async_copy(
                g_up.at[slot], grad_ref.at[:, pl.ds(pl.multiple_of(UP_AT + cols, FF_TILE), FF_TILE)], sems.at[slot, 1]
            ),
            pltpu.make_async_copy(
                g_main.at[slot], grad_ref.at[pl.ds(pl.multiple_of(rows, 64), FF_ROWS), pl.ds(0, D)], sems.at[slot, 2]
            ),
            pltpu.make_async_copy(
                g_rest.at[slot],
                grad_ref.at[pl.ds(pl.multiple_of(rows, 64), FF_ROWS), pl.ds(REST_AT, D // 3)],
                sems.at[slot, 3],
            ),
        ]

    @pl.when(step == 0)
    def _():
        n_t[...] = n_ref[...].T
        y_acc[...] = jnp.zeros_like(y_acc)
        dn_acc[...] = jnp.zeros_like(dn_acc)

    @pl.when(step >= 2)
    def _():
        for copy in copies(step - 2, slot):
            copy.wait()

    low = jnp.bfloat16
    units = []
    for j in range(FF_TILE // UNIT_FF):
        rest = [rest_ref[j * 96 + q * 32 : j * 96 + q * 32 + 32, :] for q in range(3)]
        units += [main_ref[j * 96 : j * 96 + 96, :], jnp.concatenate(rest, axis=1)]
    w_down = jnp.concatenate(units, axis=0)
    rows, df = n_ref[...], df_ref[...]
    gate, up = product(rows, gate_ref[...]), product(rows, up_ref[...])
    sigma = jax.nn.sigmoid(gate)
    silu = gate * sigma
    act = (silu * up).astype(low)
    d_act = product_t(df, w_down)
    d_gate = (d_act * up * sigma * (1.0 + gate * (1.0 - sigma))).astype(low)
    d_up = (d_act * silu).astype(low)
    y_acc[...] += product(act, w_down)
    dn_acc[...] += product_t(d_gate, gate_ref[...]) + product_t(d_up, up_ref[...])
    g_gate[slot] = product(n_t[...], d_gate).astype(low)
    g_up[slot] = product(n_t[...], d_up).astype(low)
    g_down = product(act.T, df).astype(low)
    for j in range(FF_TILE // UNIT_FF):
        g_main[slot, j * 96 : j * 96 + 96, :] = g_down[j * UNIT_FF : j * UNIT_FF + 96]
        for q in range(3):
            g_rest[slot, j * 96 + q * 32 : j * 96 + q * 32 + 32, :] = g_down[
                j * UNIT_FF + 96 : (j + 1) * UNIT_FF, q * (D // 3) : (q + 1) * (D // 3)
            ]
    for copy in copies(step, slot):
        copy.start()

    @pl.when(step == FF_TILES - 1)
    def _():
        y_mine_ref[...] = y_acc[:ROWS]
        y_other_ref[...] = y_acc[ROWS:].astype(low)
        dn_mine_ref[...] = dn_acc[:ROWS]
        dn_other_ref[...] = dn_acc[ROWS:].astype(low)
        for back in (1, 0):
            for copy in copies(step - back, lax.rem(step - back, 2)):
                copy.wait()


def feed_forward(n2, df, w_all):
    wide = jax.ShapeDtypeStruct((ROWS, D), jnp.float32)
    return pl.pallas_call(
        ffn_kernel,
        grid=(FF_TILES,),
        in_specs=[
            whole_spec(BOTH, D),
            whole_spec(BOTH, D),
            pl.BlockSpec((FF_ROWS, D), lambda t: (t, 0)),
            pl.BlockSpec((FF_ROWS, D // 3), lambda t: (t, REST_AT // (D // 3))),
            pl.BlockSpec((D, FF_TILE), lambda t: (0, GATE_AT // FF_TILE + t)),
            pl.BlockSpec((D, FF_TILE), lambda t: (0, UP_AT // FF_TILE + t)),
        ],
        out_specs=[whole_spec(ROWS, D)] * 4 + [pl.BlockSpec(memory_space=pl.ANY)],
        out_shape=[wide, low_shape(ROWS, D), wide, low_shape(ROWS, D), low_shape(D, OUT_AT + D // 2)],
        scratch_shapes=[
            pltpu.VMEM((D, BOTH), jnp.bfloat16),
            pltpu.VMEM((BOTH, D), jnp.float32),
            pltpu.VMEM((BOTH, D), jnp.float32),
            pltpu.VMEM((2, D, FF_TILE), jnp.bfloat16),
            pltpu.VMEM((2, D, FF_TILE), jnp.bfloat16),
            pltpu.VMEM((2, FF_ROWS, D), jnp.bfloat16),
            pltpu.VMEM((2, FF_ROWS, D // 3), jnp.bfloat16),
            pltpu.SemaphoreType.DMA((2, 4)),
        ],
        compiler_params=PARAMS,
        cost_estimate=cost(30),
        name="feed_forward",
    )(n2, df, w_all, w_all, w_all, w_all)


def collect(units, tables):
    shape = low_shape(BOTH, HQ + 2 * HK)
    return pl.pallas_call(collect_kernel, out_shape=shape, compiler_params=PARAMS, cost_estimate=cost(4), name="collect")(
        split_units(units), tables
    )


def attend_fwd(unit, first, units, starts):
    return pl.pallas_call(
        fwd_kernel,
        grid=(MB,),
        in_specs=[SMEM, SMEM, UNIT_SPEC, COL_SPEC],
        out_specs=[QUERY_SPEC, COL_SPEC],
        out_shape=[low_shape(SHARDS, MB, Q_ROWS, 128), COL_SHAPE],
        compiler_params=PARAMS,
        cost_estimate=cost(20),
        name="attend_forward",
    )(unit, first, units, starts)


def attend_bwd(unit, first, units, starts, d_mixed, lse):
    return pl.pallas_call(
        bwd_kernel,
        grid=(MB,),
        in_specs=[SMEM, SMEM, UNIT_SPEC, COL_SPEC, QUERY_SPEC, COL_SPEC],
        out_specs=UNIT_SPEC,
        out_shape=low_shape(SHARDS, MB, ALL_ROWS, 128),
        scratch_shapes=[pltpu.VMEM((SEQ, 128), jnp.float32)],
        compiler_params=PARAMS,
        cost_estimate=cost(27),
        name="attend_backward",
    )(unit, first, units, starts, d_mixed, lse)


def piece_perm():
    return [(k * SHARDS + s, (s // 16) * SHARDS + 2 * (s % 16) + k) for k in range(2) for s in range(SHARDS)]


def shift(values, axis, step):
    if axis == "x":
        line = lambda x: (x % 2) * 2 + x // 2
        return lax.ppermute(values, ("xl", "xh"), [(line(i), line((i + step) % 4)) for i in range(4)])
    return lax.ppermute(values, axis, [(i, (i + step) % 4) for i in range(4)])


def place(axis):
    if axis == "x":
        return lax.axis_index("xh") * 2 + lax.axis_index("xl")
    return lax.axis_index(axis)


def flip(values, axis):
    return lax.ppermute(values, axis, [(0, 1), (1, 0)])


def col_half(core, local):
    half = local.shape[1] // 2
    return lax.dynamic_slice_in_dim(local, core * half, half, axis=1)


def pad_units(local):
    return jnp.pad(local.reshape(-1, 16, 120), ((0, 0), (0, 0), (0, UNIT_FF - 120))).reshape(-1, PAD_FF)


def crop_units(local):
    return local.reshape(-1, 16, UNIT_FF)[:, :, :120].reshape(-1, HF)


def fold(rows, parts):
    n, r, w = rows.shape
    return rows.reshape(n, r, parts, w // parts).transpose(0, 2, 1, 3).reshape(n, parts * r, w // parts)


def unfold(rows, parts):
    n, r, w = rows.shape
    return rows.reshape(n, parts, r // parts, w).transpose(0, 2, 1, 3).reshape(n, r // parts, parts * w)


def wide_sum(*values):
    total = values[0].astype(jnp.float32)
    for value in values[1:]:
        total = total + value.astype(jnp.float32)
    return total.astype(jnp.bfloat16)


def after(values, event):
    return lax.optimization_barrier((values, event))[0]


def total_axis(values, axis):
    return values + shift(values, axis, 1) + shift(values, axis, 2) + shift(values, axis, 3)


def reduce_x(values):
    size = values.shape[0] // 2
    me = lax.axis_index("xh")
    keep = lax.dynamic_slice_in_dim(values, me * size, size, axis=0)
    send = lax.dynamic_slice_in_dim(values, (1 - me) * size, size, axis=0)
    cross = lax.ppermute(send, ("xl", "xh"), [(i, 3 - i) for i in range(4)])
    return wide_sum(keep, flip(keep, "xl"), flip(send, "xh"), cross)


def return_rows(rows, a, b):
    pairs = []
    for xl in range(2):
        for c in range(2):
            for j in range(16):
                for xh in range(2):
                    source = ((xl * 2 + c) * 16 + j) * 2 + xh
                    pairs.append((source, ((xl ^ b) * 2 + (xh ^ a)) * SHARDS + 16 * c + j))
    return lax.ppermute(rows, ("xl", "c") + SHARD, pairs)


def add_pair(values, axis):
    return wide_sum(values, flip(values, axis))


def join_pair(mine, axis, dim):
    other = flip(mine, axis)
    lower = lax.axis_index(axis) == 0
    return jnp.concatenate([jnp.where(lower, mine, other), jnp.where(lower, other, mine)], axis=dim)


def join_cores(mine):
    return join_pair(mine, "c", 1).astype(jnp.float32)


def scatter_sum(values):
    return jnp.sum(exchange(values).astype(jnp.float32), axis=0).astype(jnp.bfloat16)


def on_device(
    hidden_in,
    doc_ids,
    out_grad,
    norm_attn,
    w_query,
    w_key,
    w_value,
    w_out,
    norm_ffn,
    w_gate,
    w_up,
    w_down,
):
    core = lax.axis_index("c")
    shard = lax.axis_index(SHARD)
    low = jnp.bfloat16

    rows_in = lax.ppermute(jnp.concatenate([w_out, w_down], axis=0), ("c",) + SHARD, piece_perm())
    gu_piece = jnp.concatenate([pad_units(col_half(core, w_gate)), pad_units(col_half(core, w_up))], axis=1)
    w_all = lax.all_gather(
        jnp.concatenate(
            [
                rows_in[48:144],
                fold(jnp.pad(rows_in[144:], ((0, 8), (0, 0)))[None], 3)[0],
                join_pair(gu_piece, "xh", 0),
                fold(rows_in[:48][None], 2)[0],
            ],
            axis=1,
        ),
        ("z", "y"),
        axis=0,
        tiled=True,
    )
    small = jnp.concatenate(
        [norm_attn[:, None], norm_ffn[:, None], doc_ids.reshape(48, 4).astype(low), jnp.zeros((48, 122), low)], axis=1
    )
    piece = jnp.concatenate(
        [to_groups(col_half(core, w_query)), interleave(col_half(core, w_key), col_half(core, w_value)), small], axis=1
    )
    w_first = exchange(jnp.broadcast_to(piece[None], (SHARDS, 48, QKV + 128)))
    small = w_first[:, :, QKV : QKV + 6]
    w_first = w_first.reshape(D, QKV + 128)
    w_qkv = w_first[:, :QKV]
    gain_attn = small[:, :, 0].reshape(1, D).astype(jnp.float32)
    gain_ffn = small[:, :, 1].reshape(1, D).astype(jnp.float32)
    docs_mine = small[:, :, 2:].reshape(SHARDS, MB, SPAN).transpose(1, 0, 2).reshape(MB, SEQ)
    docs_other = swap(docs_mine)

    x_low = hidden_in.reshape(ROWS, D)
    x = x_low.astype(jnp.float32)
    x_both = jnp.concatenate([x_low, swap(x_low)], axis=0).astype(jnp.float32)
    dy_low = out_grad.reshape(ROWS, D)
    dy = dy_low.astype(jnp.float32)
    df = (branch_scale * jnp.concatenate([dy_low, swap(dy_low)], axis=0).astype(jnp.float32)).astype(low)

    which = lax.rem(shard // PARTS, 2)
    part = lax.rem(shard, PARTS)
    docs = jnp.where(which == 0, docs_mine, docs_other).astype(jnp.float32)
    counted = jnp.sum((docs[:, None, :] < docs[:, :, None]).astype(jnp.int32), axis=-1)
    q_start = lax.dynamic_slice_in_dim(counted.reshape(MB, SHARDS, SPAN), part * CHUNK, CHUNK, axis=2)
    q_start = q_start.reshape(MB, TILES, 1, TILE * CHUNK)
    first = (q_start[:, :, 0, 0] // BLOCK).reshape(-1)
    starts = jnp.broadcast_to(q_start, (MB, TILES, GROUP, TILE * CHUNK)).reshape(MB, TILES, TROWS, 1)
    starts = jnp.broadcast_to(starts, (MB, TILES, TROWS, 128))
    unit = jnp.stack([part, lax.rem(shard // (2 * PARTS), 2)]).astype(jnp.int32)

    places = (shard * SPAN + jnp.arange(SPAN, dtype=jnp.int32)).astype(jnp.float32)
    half_size = HD // 2
    inverse = jnp.exp(-jnp.arange(half_size, dtype=jnp.float32) * (math.log(10000.0) / half_size))
    angles = places[:, None] * inverse[None, :]
    cosine, sine = jnp.cos(angles), jnp.sin(angles)
    cosine = jnp.concatenate([cosine, cosine], axis=1)
    sine = jnp.concatenate([-sine, sine], axis=1)
    tables = jnp.stack(
        [
            jnp.concatenate([cosine, cosine], axis=1),
            jnp.concatenate([sine, sine], axis=1),
            jnp.concatenate([cosine, jnp.ones_like(cosine)], axis=1),
            jnp.concatenate([sine, jnp.zeros_like(sine)], axis=1),
        ]
    )

    r1_both = lax.rsqrt(jnp.mean(x_both * x_both, axis=-1, keepdims=True) + eps_norm)
    r1 = r1_both[:ROWS]
    n1 = (x_both * r1_both * gain_attn).astype(low)
    units = exchange(project(n1, w_first, tables))
    unit_o, lse = attend_fwd(unit, first, units, starts)
    attn, y1_mine, y1_other = out_project(exchange(unit_o), w_all)
    hmid = x + branch_scale * (y1_mine + swap(y1_other).astype(jnp.float32))

    r2 = lax.rsqrt(jnp.mean(hmid * hmid, axis=-1, keepdims=True) + eps_norm)
    z2 = hmid * r2
    n2_mine = (z2 * gain_ffn).astype(low)
    n2 = jnp.concatenate([n2_mine, swap(n2_mine)], axis=0)
    y2_mine, y2_other, dn2_mine, dn2_other, g_ffn = feed_forward(n2, df, w_all)
    result = hmid + branch_scale * (y2_mine + swap(y2_other).astype(jnp.float32))

    dn2 = dn2_mine + swap(dn2_other).astype(jnp.float32)
    e2 = dn2 * gain_ffn
    g_gain_ffn = jnp.sum(dn2 * z2, axis=0)
    dh = dy + r2 * (e2 - z2 * jnp.mean(e2 * z2, axis=-1, keepdims=True))

    da_mine = (branch_scale * dh).astype(low)
    da = jnp.concatenate([da_mine, swap(da_mine)], axis=0)
    unit_do, g_all = d_out_project(da, w_all, attn, g_ffn)
    s_all = lax.psum_scatter(g_all, ("z", "y"), scatter_dimension=0, tiled=True)
    unit_do = exchange(unit_do)
    unit_d = attend_bwd(unit, first, units, starts, unit_do, lse)
    d_qkv = collect(exchange(unit_d), tables)

    g_qkv = t_product(n1, d_qkv).astype(low)
    s_qkv = scatter_sum(g_qkv.reshape(SHARDS, 48, HQ + 2 * HK))
    dn1_both = product_t(d_qkv, w_qkv)
    dn1 = dn1_both[:ROWS] + swap(dn1_both[ROWS:].astype(low)).astype(jnp.float32)
    z1 = x * r1
    e1 = dn1 * gain_attn
    g_gain_attn = jnp.sum(dn1 * z1, axis=0)
    grad_in = (dh + r1 * (e1 - z1 * jnp.mean(e1 * z1, axis=-1, keepdims=True))).astype(low)

    gains = jnp.stack([g_gain_attn, g_gain_ffn])
    gains = gains + swap(gains)
    gains = total_axis(total_axis(total_axis(gains, "x"), "y"), "z")
    gains = lax.dynamic_slice_in_dim(gains, shard * 48, 48, axis=1)
    s_all = after(s_all, gains)
    rows = jnp.concatenate(
        [
            unfold(s_all[None, :, OUT_AT:], 2)[0],
            s_all[:, :D],
            unfold(s_all[None, :, REST_AT:GATE_AT], 3)[0][:24],
        ],
        axis=0,
    )
    rows = sum(return_rows(rows, a, b).astype(jnp.float32) for a in range(2) for b in range(2))
    s_gu = reduce_x(s_all[:, GATE_AT:OUT_AT])
    s_gu = jnp.concatenate([crop_units(s_gu[:, :PAD_FF]), crop_units(s_gu[:, PAD_FF:])], axis=1)
    other = swap(s_gu)
    lower = core == 0
    g_g, g_u = [
        jnp.concatenate([jnp.where(lower, m, t), jnp.where(lower, t, m)], axis=1).astype(jnp.float32)
        for m, t in ((s_gu[:, :HF], other[:, :HF]), (s_gu[:, HF:], other[:, HF:]))
    ]
    s_qkv = add_pair(s_qkv, "xl")
    other = swap(s_qkv)
    whole = [jnp.where(lower, s_qkv, other), jnp.where(lower, other, s_qkv)]

    def heads_of(offset):
        return jnp.concatenate(
            [w[:, HQ + 128 * j + offset : HQ + 128 * j + offset + HD] for w in whole for j in range(HALF_KV)], axis=1
        ).astype(jnp.float32)

    return (
        result.reshape(1, MB, SPAN, D).astype(low),
        grad_in.reshape(1, MB, SPAN, D),
        gains[0],
        jnp.concatenate([from_groups(w[:, :HQ]) for w in whole], axis=1).astype(jnp.float32),
        heads_of(0),
        heads_of(HD),
        rows[:48],
        gains[1],
        g_g,
        g_u,
        rows[48:],
    )


def solution(mesh):
    fine = Mesh(mesh.devices.reshape(2, 2, 4, 4, 2), ("xl", "c", "z", "y", "xh"))
    replica = ("xl", "c")
    tokens = P(replica, None, SHARD, None)
    matrix = P(SHARD, None)
    vector = P(SHARD)
    return jax.shard_map(
        on_device,
        mesh=fine,
        in_specs=(
            tokens,
            P(replica, None, SHARD),
            tokens,
            vector,
            matrix,
            matrix,
            matrix,
            matrix,
            vector,
            matrix,
            matrix,
            matrix,
        ),
        out_specs=(
            tokens,
            tokens,
            vector,
            matrix,
            matrix,
            matrix,
            matrix,
            vector,
            matrix,
            matrix,
            matrix,
        ),
        check_vma=False,
    )
```

```python
from functools import partial
import math

import jax
import jax.numpy as jnp
from jax import lax
from jax.experimental import pallas as pl
from jax.experimental.pallas import tpu as pltpu
from jax.sharding import Mesh
from jax.sharding import PartitionSpec as P

HEADS = 24
KVH = 8
HD = 64
D = 1536
FF = 3840
MB = 3
SPAN = 64
SHARDS = 32
SEQ = 2048
PARTS = 4
ROWS = MB * SPAN
BOTH = 2 * ROWS
GROUP = HEADS // KVH
HALF_KV = KVH // 2
HQ = HALF_KV * GROUP * HD
HK = HALF_KV * HD
HF = FF // 2
QKV = HQ + 2 * HK
UNIT_FF = 128
PAD_FF = 16 * UNIT_FF
REST_AT = D
GATE_AT = D + D // 3
UP_AT = GATE_AT + PAD_FF
OUT_AT = UP_AT + PAD_FF
FF_TILE = 256
FF_TILES = PAD_FF // FF_TILE
FF_ROWS = 96 * FF_TILE // UNIT_FF
CHUNK = SPAN // PARTS
TILE = 4
TILES = SHARDS // TILE
BLOCK = TILE * SPAN
TROWS = GROUP * TILE * CHUNK

SHARD = ("z", "y", "xh")
branch_scale = 1.4 / math.sqrt(52.0)
eps_norm = 1e-05
NEG = -1e30
VMEM_LIMIT = 48 * 1024 * 1024


def product(left, right):
    return jnp.dot(left, right, preferred_element_type=jnp.float32)


def product_t(left, right):
    return lax.dot_general(left, right, (((1,), (1,)), ((), ())), preferred_element_type=jnp.float32)


def t_product(left, right):
    return lax.dot_general(left, right, (((0,), (0,)), ((), ())), preferred_element_type=jnp.float32)


def swap(values):
    return lax.ppermute(values, "c", [(0, 1), (1, 0)])


def exchange(values):
    return lax.all_to_all(values, SHARD, 0, 0, tiled=True)


Q_ROWS = 2 * CHUNK
ALL_ROWS = SPAN + Q_ROWS


def to_groups(rows):
    parts = [rows[:, 192 * j : 192 * j + 128] for j in range(HALF_KV)]
    parts += [rows[:, 192 * j + 128 : 192 * j + 192] for j in range(HALF_KV)]
    return jnp.concatenate(parts, axis=1)


def from_groups(rows):
    parts = []
    for j in range(HALF_KV):
        parts += [rows[:, 128 * j : 128 * j + 128], rows[:, 512 + 64 * j : 576 + 64 * j]]
    return jnp.concatenate(parts, axis=1)


def interleave(keys, values):
    parts = []
    for j in range(HALF_KV):
        parts += [keys[:, HD * j : HD * j + HD], values[:, HD * j : HD * j + HD]]
    return jnp.concatenate(parts, axis=1)


def turn(values, cosine, sine):
    lane = lax.broadcasted_iota(jnp.int32, values.shape, values.ndim - 1)
    axis = values.ndim - 1
    other = jnp.where(lane % HD < HD // 2, pltpu.roll(values, 128 - HD // 2, axis), pltpu.roll(values, HD // 2, axis))
    return values * cosine + other * sine


def project_kernel(n_ref, w_ref, table_ref, out_ref):
    rows = n_ref[...]

    def group(g, table):
        wide = product(rows, w_ref[:, 128 * g : 128 * g + 128]).reshape(2 * MB, SPAN, 128)
        return turn(wide, table_ref[table][None], table_ref[table + 1][None]).astype(jnp.bfloat16)

    for j in range(HALF_KV):
        first, both = group(j, 0), group(6 + j, 2)
        if j % 2 == 0:
            third = group(4 + j // 2, 0)
        for o in range(2):
            for m in range(MB):
                for p in range(PARTS):
                    cut = slice(p * CHUNK, (p + 1) * CHUNK)
                    out_ref[j, o, p, m, 0:SPAN, :] = both[o * MB + m]
                    out_ref[j, o, p, m, SPAN : SPAN + CHUNK, :] = first[o * MB + m, cut]
                    out_ref[j, o, p, m, SPAN + CHUNK : ALL_ROWS, :] = third[o * MB + m, cut]


def third_head(pair_even, pair_odd):
    lane = lax.broadcasted_iota(jnp.int32, pair_even.shape, pair_even.ndim - 1)
    return jnp.where(lane < HD, pair_even, pair_odd)


def out_halves(ref):
    whole = ref[...].reshape(16, 2, 48, D // 2)
    return whole[:, 0].reshape(HQ, D // 2), whole[:, 1].reshape(HQ, D // 2)


def out_kernel(u_ref, w_ref, attn_ref, mine_ref, other_ref):
    for o in range(2):
        for m in range(MB):
            for p in range(PARTS):
                thirds = [
                    third_head(u_ref[2 * k, o, p, m, CHUNK:, :], u_ref[2 * k + 1, o, p, m, CHUNK:, :])
                    for k in range(2)
                ]
                parts = []
                for j in range(HALF_KV):
                    parts += [u_ref[j, o, p, m, :CHUNK, :], thirds[j // 2][:, HD * (j % 2) : HD * (j % 2) + HD]]
                at = (o * MB + m) * SPAN + p * CHUNK
                attn_ref[at : at + CHUNK, :] = jnp.concatenate(parts, axis=1)
    attn = attn_ref[...]
    for k, half in enumerate(out_halves(w_ref)):
        result = product(attn, half)
        cols = slice(k * (D // 2), (k + 1) * (D // 2))
        mine_ref[:, cols] = result[:ROWS]
        other_ref[:, cols] = result[ROWS:].astype(jnp.bfloat16)


def d_out_kernel(da_ref, w_ref, out_ref):
    left, right = out_halves(w_ref)
    rows = product_t(da_ref[:, : D // 2], left) + product_t(da_ref[:, D // 2 :], right)
    rows = rows.astype(jnp.bfloat16)
    for j in range(HALF_KV):
        first = rows[:, 192 * j : 192 * j + 128]
        if j % 2 == 0:
            third = jnp.concatenate([rows[:, 192 * j + 128 : 192 * j + 192], rows[:, 192 * j + 320 : 192 * j + 384]], axis=1)
        for o in range(2):
            for m in range(MB):
                for p in range(PARTS):
                    at = (o * MB + m) * SPAN + p * CHUNK
                    out_ref[j, o, p, m, :CHUNK, :] = first[at : at + CHUNK]
                    out_ref[j, o, p, m, CHUNK:, :] = third[at : at + CHUNK]


def collect_kernel(u_ref, table_ref, out_ref):
    def put(g, o, m, at, size, values, table, row):
        cosine = table_ref[table, row : row + size]
        sine = table_ref[table + 1, row : row + size]
        out_ref[at : at + size, 128 * g : 128 * g + 128] = turn(values, cosine, -sine).astype(jnp.bfloat16)

    wide = jnp.float32
    for o in range(2):
        for m in range(MB):
            base = (o * MB + m) * SPAN
            for j in range(HALF_KV):
                total = u_ref[j, o, 0, m, 0:SPAN, :].astype(wide)
                for p in range(1, PARTS):
                    total = total + u_ref[j, o, p, m, 0:SPAN, :].astype(wide)
                put(6 + j, o, m, base, SPAN, total, 2, 0)
            for p in range(PARTS):
                at = base + p * CHUNK
                for j in range(HALF_KV):
                    first = u_ref[j, o, p, m, SPAN : SPAN + CHUNK, :].astype(wide)
                    put(j, o, m, at, CHUNK, first, 0, p * CHUNK)
                for k in range(2):
                    third = third_head(
                        u_ref[2 * k, o, p, m, SPAN + CHUNK : ALL_ROWS, :].astype(wide),
                        u_ref[2 * k + 1, o, p, m, SPAN + CHUNK : ALL_ROWS, :].astype(wide),
                    )
                    put(4 + k, o, m, at, CHUNK, third, 0, p * CHUNK)


def stack_heads(first, third, odd):
    last = jnp.where(odd == 1, third[:, HD:], third[:, :HD])
    return jnp.concatenate([first[:, :HD], first[:, HD:], last], axis=0)


def lay_heads(rows):
    size = TILE * CHUNK
    parts = [rows[g * size : (g + 1) * size] for g in range(GROUP)]
    shape = (TILE, CHUNK, 128)
    return (
        jnp.concatenate(parts[:2], axis=1).astype(jnp.bfloat16).reshape(shape),
        jnp.concatenate([parts[2], parts[2]], axis=1).astype(jnp.bfloat16).reshape(shape),
    )


def tile_mask(part, start_rows, tile, blocks):
    wide = blocks * BLOCK
    row = lax.broadcasted_iota(jnp.int32, (TROWS, 1), 0)
    inside = lax.rem(row, TILE * CHUNK)
    q_pos = tile * BLOCK + (inside // CHUNK) * SPAN + part * CHUNK + lax.rem(inside, CHUNK)
    k_pos = (tile + 1 - blocks) * BLOCK + lax.broadcasted_iota(jnp.int32, (TROWS, wide), 1)
    return (k_pos >= start_rows) & (k_pos <= q_pos)


def tile_queries(ref, tile, begin, odd):
    where = pl.ds(tile * TILE, TILE)
    first = ref[where, 0, begin : begin + CHUNK, :].reshape(TILE * CHUNK, 128)
    third = ref[where, 0, begin + CHUNK : begin + 2 * CHUNK, :].reshape(TILE * CHUNK, 128)
    return stack_heads(first, third, odd)


def tile_keys(ref, begin, blocks):
    return ref[pl.ds(begin * TILE, blocks * TILE), 0, 0:SPAN, :].reshape(blocks * BLOCK, 128)


def each_tile(first_ref, work):
    micro = pl.program_id(0)

    def body(tile, carry):
        needed = tile + 1 - first_ref[micro * TILES + tile]
        for blocks in range(1, TILES + 1):
            pl.when(needed == blocks)(partial(work, tile, blocks))
        return carry

    lax.fori_loop(0, TILES, body, 0)


def fwd_kernel(unit_ref, first_ref, u_ref, start_ref, o_ref, lse_ref):
    part, odd = unit_ref[0], unit_ref[1]

    def work(tile, blocks):
        q_rows = tile_queries(u_ref, tile, SPAN, odd) * jnp.bfloat16(0.125)
        keys = tile_keys(u_ref, tile + 1 - blocks, blocks)
        scores = product_t(q_rows, keys[:, :HD])
        allowed = tile_mask(part, start_ref[0, tile][:, :1], tile, blocks)
        scores = jnp.where(allowed, scores, NEG)
        highest = jnp.max(scores, axis=-1, keepdims=True)
        expo = jnp.exp(scores - highest)
        total = jnp.sum(expo, axis=-1, keepdims=True)
        mixed = product(expo.astype(jnp.bfloat16), keys[:, HD:]) / total
        where = pl.ds(tile * TILE, TILE)
        o_ref[where, 0, :CHUNK, :], o_ref[where, 0, CHUNK:, :] = lay_heads(mixed)
        lse_ref[0, tile] = jnp.broadcast_to(highest + jnp.log(total), (TROWS, 128))

    each_tile(first_ref, work)


def bwd_kernel(unit_ref, first_ref, u_ref, start_ref, do_ref, lse_ref, d_ref, acc):
    part, odd = unit_ref[0], unit_ref[1]
    acc[...] = jnp.zeros_like(acc)

    def work(tile, blocks):
        begin = tile + 1 - blocks
        q_rows = tile_queries(u_ref, tile, SPAN, odd) * jnp.bfloat16(0.125)
        d_rows = tile_queries(do_ref, tile, 0, odd)
        keys = tile_keys(u_ref, begin, blocks)
        scores = product_t(q_rows, keys[:, :HD])
        allowed = tile_mask(part, start_ref[0, tile][:, :1], tile, blocks)
        probs = jnp.where(allowed, jnp.exp(scores - lse_ref[0, tile][:, :1]), 0.0)
        d_probs = product_t(d_rows, keys[:, HD:])
        offset = jnp.sum(d_probs * probs, axis=-1, keepdims=True)
        d_scores = (probs * (d_probs - offset)).astype(jnp.bfloat16)
        d_query = product(d_scores, keys[:, :HD]) * 0.125
        at = pl.ds(tile * TILE, TILE)
        d_ref[at, 0, SPAN : SPAN + CHUNK, :], d_ref[at, 0, SPAN + CHUNK : ALL_ROWS, :] = lay_heads(d_query)
        d_key = t_product(d_scores, q_rows)
        d_value = t_product(probs.astype(jnp.bfloat16), d_rows)
        where = pl.ds(begin * BLOCK, blocks * BLOCK)
        acc[where, :] += jnp.concatenate([d_key, d_value], axis=1)

    each_tile(first_ref, work)
    d_ref[:, 0, 0:SPAN, :] = acc[...].astype(jnp.bfloat16).reshape(SHARDS, SPAN, 128)


SMEM = pl.BlockSpec(memory_space=pltpu.SMEM)
UNIT_SPEC = pl.BlockSpec((SHARDS, 1, ALL_ROWS, 128), lambda m: (0, m, 0, 0))
QUERY_SPEC = pl.BlockSpec((SHARDS, 1, Q_ROWS, 128), lambda m: (0, m, 0, 0))
COL_SPEC = pl.BlockSpec((1, TILES, TROWS, 128), lambda m: (m, 0, 0, 0))
COL_SHAPE = jax.ShapeDtypeStruct((MB, TILES, TROWS, 128), jnp.float32)
PARAMS = pltpu.CompilerParams(vmem_limit_bytes=VMEM_LIMIT)


def split_units(values):
    return values.reshape((HALF_KV, 2, PARTS) + values.shape[1:])


def low_shape(*dims):
    return jax.ShapeDtypeStruct(dims, jnp.bfloat16)


def project(n1, w_qkv, tables):
    shape = low_shape(HALF_KV, 2, PARTS, MB, ALL_ROWS, 128)
    out = pl.pallas_call(project_kernel, out_shape=shape, compiler_params=PARAMS, cost_estimate=cost(6), name="project")(n1, w_qkv, tables)
    return out.reshape(SHARDS, MB, ALL_ROWS, 128)


def whole_spec(*dims):
    return pl.BlockSpec(dims, lambda i: (0,) * len(dims))


OUT_SPEC = pl.BlockSpec((D, D // 2), lambda i: (0, OUT_AT // (D // 2)))


def cost(micros):
    return pl.CostEstimate(flops=int(micros * 1e9), bytes_accessed=1 << 20, transcendentals=0)


def out_project(units, w_all):
    return pl.pallas_call(
        out_kernel,
        grid=(1,),
        in_specs=[whole_spec(HALF_KV, 2, PARTS, MB, Q_ROWS, 128), OUT_SPEC],
        out_specs=[whole_spec(BOTH, HQ), whole_spec(ROWS, D), whole_spec(ROWS, D)],
        out_shape=[low_shape(BOTH, HQ), jax.ShapeDtypeStruct((ROWS, D), jnp.float32), low_shape(ROWS, D)],
        compiler_params=PARAMS,
        cost_estimate=cost(3),
        name="out_project",
    )(split_units(units), w_all)


def d_out_project(da, w_all):
    dims = (HALF_KV, 2, PARTS, MB, Q_ROWS, 128)
    out = pl.pallas_call(
        d_out_kernel,
        grid=(1,),
        in_specs=[whole_spec(BOTH, D), OUT_SPEC],
        out_specs=whole_spec(*dims),
        out_shape=low_shape(*dims),
        compiler_params=PARAMS,
        cost_estimate=cost(3),
        name="d_out_project",
    )(da, w_all)
    return out.reshape(SHARDS, MB, Q_ROWS, 128)


def ffn_kernel(
    n_ref, df_ref, main_ref, rest_ref, gate_ref, up_ref,
    y_mine_ref, y_other_ref, dn_mine_ref, dn_other_ref, grad_ref,
    n_t, y_acc, dn_acc, g_gate, g_up, g_main, g_rest, sems,
):
    step = pl.program_id(0)
    slot = lax.rem(step, 2)

    def copies(at, slot):
        cols, rows = at * FF_TILE, at * FF_ROWS
        return [
            pltpu.make_async_copy(
                g_gate.at[slot], grad_ref.at[:, pl.ds(pl.multiple_of(GATE_AT + cols, FF_TILE), FF_TILE)], sems.at[slot, 0]
            ),
            pltpu.make_async_copy(
                g_up.at[slot], grad_ref.at[:, pl.ds(pl.multiple_of(UP_AT + cols, FF_TILE), FF_TILE)], sems.at[slot, 1]
            ),
            pltpu.make_async_copy(
                g_main.at[slot], grad_ref.at[pl.ds(pl.multiple_of(rows, 64), FF_ROWS), pl.ds(0, D)], sems.at[slot, 2]
            ),
            pltpu.make_async_copy(
                g_rest.at[slot],
                grad_ref.at[pl.ds(pl.multiple_of(rows, 64), FF_ROWS), pl.ds(REST_AT, D // 3)],
                sems.at[slot, 3],
            ),
        ]

    @pl.when(step == 0)
    def _():
        n_t[...] = n_ref[...].T
        y_acc[...] = jnp.zeros_like(y_acc)
        dn_acc[...] = jnp.zeros_like(dn_acc)

    @pl.when(step >= 2)
    def _():
        for copy in copies(step - 2, slot):
            copy.wait()

    low = jnp.bfloat16
    units = []
    for j in range(FF_TILE // UNIT_FF):
        rest = [rest_ref[j * 96 + q * 32 : j * 96 + q * 32 + 32, :] for q in range(3)]
        units += [main_ref[j * 96 : j * 96 + 96, :], jnp.concatenate(rest, axis=1)]
    w_down = jnp.concatenate(units, axis=0)
    rows, df = n_ref[...], df_ref[...]
    gate, up = product(rows, gate_ref[...]), product(rows, up_ref[...])
    sigma = jax.nn.sigmoid(gate)
    silu = gate * sigma
    act = (silu * up).astype(low)
    d_act = product_t(df, w_down)
    d_gate = (d_act * up * sigma * (1.0 + gate * (1.0 - sigma))).astype(low)
    d_up = (d_act * silu).astype(low)
    y_acc[...] += product(act, w_down)
    dn_acc[...] += product_t(d_gate, gate_ref[...]) + product_t(d_up, up_ref[...])
    g_gate[slot] = product(n_t[...], d_gate).astype(low)
    g_up[slot] = product(n_t[...], d_up).astype(low)
    g_down = product(act.T, df).astype(low)
    for j in range(FF_TILE // UNIT_FF):
        g_main[slot, j * 96 : j * 96 + 96, :] = g_down[j * UNIT_FF : j * UNIT_FF + 96]
        for q in range(3):
            g_rest[slot, j * 96 + q * 32 : j * 96 + q * 32 + 32, :] = g_down[
                j * UNIT_FF + 96 : (j + 1) * UNIT_FF, q * (D // 3) : (q + 1) * (D // 3)
            ]
    for copy in copies(step, slot):
        copy.start()

    @pl.when(step == FF_TILES - 1)
    def _():
        y_mine_ref[...] = y_acc[:ROWS]
        y_other_ref[...] = y_acc[ROWS:].astype(low)
        dn_mine_ref[...] = dn_acc[:ROWS]
        dn_other_ref[...] = dn_acc[ROWS:].astype(low)
        for back in (1, 0):
            for copy in copies(step - back, lax.rem(step - back, 2)):
                copy.wait()


def feed_forward(n2, df, w_all):
    wide = jax.ShapeDtypeStruct((ROWS, D), jnp.float32)
    return pl.pallas_call(
        ffn_kernel,
        grid=(FF_TILES,),
        in_specs=[
            whole_spec(BOTH, D),
            whole_spec(BOTH, D),
            pl.BlockSpec((FF_ROWS, D), lambda t: (t, 0)),
            pl.BlockSpec((FF_ROWS, D // 3), lambda t: (t, REST_AT // (D // 3))),
            pl.BlockSpec((D, FF_TILE), lambda t: (0, GATE_AT // FF_TILE + t)),
            pl.BlockSpec((D, FF_TILE), lambda t: (0, UP_AT // FF_TILE + t)),
        ],
        out_specs=[whole_spec(ROWS, D)] * 4 + [pl.BlockSpec(memory_space=pl.ANY)],
        out_shape=[wide, low_shape(ROWS, D), wide, low_shape(ROWS, D), low_shape(D, OUT_AT)],
        scratch_shapes=[
            pltpu.VMEM((D, BOTH), jnp.bfloat16),
            pltpu.VMEM((BOTH, D), jnp.float32),
            pltpu.VMEM((BOTH, D), jnp.float32),
            pltpu.VMEM((2, D, FF_TILE), jnp.bfloat16),
            pltpu.VMEM((2, D, FF_TILE), jnp.bfloat16),
            pltpu.VMEM((2, FF_ROWS, D), jnp.bfloat16),
            pltpu.VMEM((2, FF_ROWS, D // 3), jnp.bfloat16),
            pltpu.SemaphoreType.DMA((2, 4)),
        ],
        compiler_params=PARAMS,
        cost_estimate=cost(30),
        name="feed_forward",
    )(n2, df, w_all, w_all, w_all, w_all)


def collect(units, tables):
    shape = low_shape(BOTH, HQ + 2 * HK)
    return pl.pallas_call(collect_kernel, out_shape=shape, compiler_params=PARAMS, cost_estimate=cost(4), name="collect")(
        split_units(units), tables
    )


def attend_fwd(unit, first, units, starts):
    return pl.pallas_call(
        fwd_kernel,
        grid=(MB,),
        in_specs=[SMEM, SMEM, UNIT_SPEC, COL_SPEC],
        out_specs=[QUERY_SPEC, COL_SPEC],
        out_shape=[low_shape(SHARDS, MB, Q_ROWS, 128), COL_SHAPE],
        compiler_params=PARAMS,
        cost_estimate=cost(20),
        name="attend_forward",
    )(unit, first, units, starts)


def attend_bwd(unit, first, units, starts, d_mixed, lse):
    return pl.pallas_call(
        bwd_kernel,
        grid=(MB,),
        in_specs=[SMEM, SMEM, UNIT_SPEC, COL_SPEC, QUERY_SPEC, COL_SPEC],
        out_specs=UNIT_SPEC,
        out_shape=low_shape(SHARDS, MB, ALL_ROWS, 128),
        scratch_shapes=[pltpu.VMEM((SEQ, 128), jnp.float32)],
        compiler_params=PARAMS,
        cost_estimate=cost(40),
        name="attend_backward",
    )(unit, first, units, starts, d_mixed, lse)


def piece_perm():
    return [(k * SHARDS + s, (s // 16) * SHARDS + 2 * (s % 16) + k) for k in range(2) for s in range(SHARDS)]


def shift(values, axis, step):
    if axis == "x":
        line = lambda x: (x % 2) * 2 + x // 2
        return lax.ppermute(values, ("xl", "xh"), [(line(i), line((i + step) % 4)) for i in range(4)])
    return lax.ppermute(values, axis, [(i, (i + step) % 4) for i in range(4)])


def place(axis):
    if axis == "x":
        return lax.axis_index("xh") * 2 + lax.axis_index("xl")
    return lax.axis_index(axis)


def flip(values, axis):
    return lax.ppermute(values, axis, [(0, 1), (1, 0)])


def col_half(core, local):
    half = local.shape[1] // 2
    return lax.dynamic_slice_in_dim(local, core * half, half, axis=1)


def pad_units(local):
    return jnp.pad(local.reshape(-1, 16, 120), ((0, 0), (0, 0), (0, UNIT_FF - 120))).reshape(-1, PAD_FF)


def crop_units(local):
    return local.reshape(-1, 16, UNIT_FF)[:, :, :120].reshape(-1, HF)


def fold(rows, parts):
    n, r, w = rows.shape
    return rows.reshape(n, r, parts, w // parts).transpose(0, 2, 1, 3).reshape(n, parts * r, w // parts)


def unfold(rows, parts):
    n, r, w = rows.shape
    return rows.reshape(n, parts, r // parts, w).transpose(0, 2, 1, 3).reshape(n, r // parts, parts * w)


def wide_sum(*values):
    total = values[0].astype(jnp.float32)
    for value in values[1:]:
        total = total + value.astype(jnp.float32)
    return total.astype(jnp.bfloat16)


def after(values, event):
    return lax.optimization_barrier((values, event))[0]


def total_axis(values, axis):
    return values + shift(values, axis, 1) + shift(values, axis, 2) + shift(values, axis, 3)


def reduce_x(values, dim):
    size = values.shape[dim] // 2
    me = lax.axis_index("xh")
    keep = lax.dynamic_slice_in_dim(values, me * size, size, axis=dim)
    send = lax.dynamic_slice_in_dim(values, (1 - me) * size, size, axis=dim)
    cross = lax.ppermute(send, ("xl", "xh"), [(i, 3 - i) for i in range(4)])
    return wide_sum(keep, flip(keep, "xl"), flip(send, "xh"), cross)


def add_pair(values, axis):
    return wide_sum(values, flip(values, axis))


def join_pair(mine, axis, dim):
    other = flip(mine, axis)
    lower = lax.axis_index(axis) == 0
    return jnp.concatenate([jnp.where(lower, mine, other), jnp.where(lower, other, mine)], axis=dim)


def join_cores(mine):
    return join_pair(mine, "c", 1).astype(jnp.float32)


def scatter_sum(values):
    return jnp.sum(exchange(values).astype(jnp.float32), axis=0).astype(jnp.bfloat16)


def on_device(
    hidden_in,
    doc_ids,
    out_grad,
    norm_attn,
    w_query,
    w_key,
    w_value,
    w_out,
    norm_ffn,
    w_gate,
    w_up,
    w_down,
):
    core = lax.axis_index("c")
    shard = lax.axis_index(SHARD)
    low = jnp.bfloat16

    rows_in = lax.ppermute(jnp.concatenate([w_out, w_down], axis=0), ("c",) + SHARD, piece_perm())
    gu_piece = jnp.concatenate([pad_units(col_half(core, w_gate)), pad_units(col_half(core, w_up))], axis=1)
    w_all = lax.all_gather(
        jnp.concatenate(
            [
                rows_in[48:144],
                fold(jnp.pad(rows_in[144:], ((0, 8), (0, 0)))[None], 3)[0],
                join_pair(gu_piece, "xh", 0),
                fold(rows_in[:48][None], 2)[0],
            ],
            axis=1,
        ),
        ("z", "y"),
        axis=0,
        tiled=True,
    )
    small = jnp.concatenate(
        [norm_attn[:, None], norm_ffn[:, None], doc_ids.reshape(48, 4).astype(low), jnp.zeros((48, 122), low)], axis=1
    )
    piece = jnp.concatenate(
        [to_groups(col_half(core, w_query)), interleave(col_half(core, w_key), col_half(core, w_value)), small], axis=1
    )
    w_first = exchange(jnp.broadcast_to(piece[None], (SHARDS, 48, QKV + 128)))
    small = w_first[:, :, QKV : QKV + 6]
    w_first = w_first.reshape(D, QKV + 128)
    w_qkv = w_first[:, :QKV]
    gain_attn = small[:, :, 0].reshape(1, D).astype(jnp.float32)
    gain_ffn = small[:, :, 1].reshape(1, D).astype(jnp.float32)
    docs_mine = small[:, :, 2:].reshape(SHARDS, MB, SPAN).transpose(1, 0, 2).reshape(MB, SEQ)
    docs_other = swap(docs_mine)

    x_low = hidden_in.reshape(ROWS, D)
    x = x_low.astype(jnp.float32)
    x_both = jnp.concatenate([x_low, swap(x_low)], axis=0).astype(jnp.float32)
    dy_low = out_grad.reshape(ROWS, D)
    dy = dy_low.astype(jnp.float32)
    df = (branch_scale * jnp.concatenate([dy_low, swap(dy_low)], axis=0).astype(jnp.float32)).astype(low)

    which = lax.rem(shard // PARTS, 2)
    part = lax.rem(shard, PARTS)
    docs = jnp.where(which == 0, docs_mine, docs_other).astype(jnp.float32)
    counted = jnp.sum((docs[:, None, :] < docs[:, :, None]).astype(jnp.int32), axis=-1)
    q_start = lax.dynamic_slice_in_dim(counted.reshape(MB, SHARDS, SPAN), part * CHUNK, CHUNK, axis=2)
    q_start = q_start.reshape(MB, TILES, 1, TILE * CHUNK)
    first = (q_start[:, :, 0, 0] // BLOCK).reshape(-1)
    starts = jnp.broadcast_to(q_start, (MB, TILES, GROUP, TILE * CHUNK)).reshape(MB, TILES, TROWS, 1)
    starts = jnp.broadcast_to(starts, (MB, TILES, TROWS, 128))
    unit = jnp.stack([part, lax.rem(shard // (2 * PARTS), 2)]).astype(jnp.int32)

    places = (shard * SPAN + jnp.arange(SPAN, dtype=jnp.int32)).astype(jnp.float32)
    half_size = HD // 2
    inverse = jnp.exp(-jnp.arange(half_size, dtype=jnp.float32) * (math.log(10000.0) / half_size))
    angles = places[:, None] * inverse[None, :]
    cosine, sine = jnp.cos(angles), jnp.sin(angles)
    cosine = jnp.concatenate([cosine, cosine], axis=1)
    sine = jnp.concatenate([-sine, sine], axis=1)
    tables = jnp.stack(
        [
            jnp.concatenate([cosine, cosine], axis=1),
            jnp.concatenate([sine, sine], axis=1),
            jnp.concatenate([cosine, jnp.ones_like(cosine)], axis=1),
            jnp.concatenate([sine, jnp.zeros_like(sine)], axis=1),
        ]
    )

    r1_both = lax.rsqrt(jnp.mean(x_both * x_both, axis=-1, keepdims=True) + eps_norm)
    r1 = r1_both[:ROWS]
    n1 = (x_both * r1_both * gain_attn).astype(low)
    units = exchange(project(n1, w_first, tables))
    unit_o, lse = attend_fwd(unit, first, units, starts)
    attn, y1_mine, y1_other = out_project(exchange(unit_o), w_all)
    hmid = x + branch_scale * (y1_mine + swap(y1_other).astype(jnp.float32))

    r2 = lax.rsqrt(jnp.mean(hmid * hmid, axis=-1, keepdims=True) + eps_norm)
    z2 = hmid * r2
    n2_mine = (z2 * gain_ffn).astype(low)
    n2 = jnp.concatenate([n2_mine, swap(n2_mine)], axis=0)
    y2_mine, y2_other, dn2_mine, dn2_other, g_ffn = feed_forward(n2, df, w_all)
    result = hmid + branch_scale * (y2_mine + swap(y2_other).astype(jnp.float32))

    s_ffn = lax.psum_scatter(g_ffn, ("z", "y"), scatter_dimension=0, tiled=True)
    dn2 = dn2_mine + swap(dn2_other).astype(jnp.float32)
    e2 = dn2 * gain_ffn
    g_gain_ffn = jnp.sum(dn2 * z2, axis=0)
    dh = dy + r2 * (e2 - z2 * jnp.mean(e2 * z2, axis=-1, keepdims=True))

    da_mine = (branch_scale * dh).astype(low)
    da = jnp.concatenate([da_mine, swap(da_mine)], axis=0)
    unit_do = exchange(d_out_project(da, w_all))
    g_o = [t_product(attn, da[:, k * (D // 2) : (k + 1) * (D // 2)]).astype(low) for k in range(2)]
    g_o = jnp.stack([g.reshape(16, 48, D // 2) for g in g_o], axis=1).reshape(SHARDS, 48, D // 2)
    s_o = scatter_sum(after(g_o, unit_do))
    unit_d = attend_bwd(unit, first, units, starts, unit_do, lse)
    d_qkv = collect(exchange(after(unit_d, s_o)), tables)

    g_qkv = t_product(n1, d_qkv).astype(low)
    s_qkv = scatter_sum(g_qkv.reshape(SHARDS, 48, HQ + 2 * HK))
    dn1_both = product_t(d_qkv, w_qkv)
    dn1 = dn1_both[:ROWS] + swap(dn1_both[ROWS:].astype(low)).astype(jnp.float32)
    z1 = x * r1
    e1 = dn1 * gain_attn
    g_gain_attn = jnp.sum(dn1 * z1, axis=0)
    grad_in = (dh + r1 * (e1 - z1 * jnp.mean(e1 * z1, axis=-1, keepdims=True))).astype(low)

    gains = jnp.stack([g_gain_attn, g_gain_ffn])
    gains = gains + swap(gains)
    gains = total_axis(total_axis(total_axis(gains, "x"), "y"), "z")
    gains = lax.dynamic_slice_in_dim(gains, shard * 48, 48, axis=1)
    s_ffn, s_o = after((s_ffn, s_o), gains)
    s_d = jnp.concatenate([s_ffn[:, :D], unfold(s_ffn[None, :, REST_AT:GATE_AT], 3)[0][:24]], axis=0)
    rows = jnp.concatenate([add_pair(s_o, "xl"), reduce_x(s_d, 1)], axis=0)
    rows = join_cores(lax.ppermute(rows, ("c",) + SHARD, [(b, a) for a, b in piece_perm()]))
    s_gu = reduce_x(s_ffn[:, GATE_AT:], 0)
    s_gu = jnp.concatenate([crop_units(s_gu[:, :PAD_FF]), crop_units(s_gu[:, PAD_FF:])], axis=1)
    other = swap(s_gu)
    lower = core == 0
    g_g, g_u = [
        jnp.concatenate([jnp.where(lower, m, t), jnp.where(lower, t, m)], axis=1).astype(jnp.float32)
        for m, t in ((s_gu[:, :HF], other[:, :HF]), (s_gu[:, HF:], other[:, HF:]))
    ]
    s_qkv = add_pair(s_qkv, "xl")
    other = swap(s_qkv)
    whole = [jnp.where(lower, s_qkv, other), jnp.where(lower, other, s_qkv)]

    def heads_of(offset):
        return jnp.concatenate(
            [w[:, HQ + 128 * j + offset : HQ + 128 * j + offset + HD] for w in whole for j in range(HALF_KV)], axis=1
        ).astype(jnp.float32)

    return (
        result.reshape(1, MB, SPAN, D).astype(low),
        grad_in.reshape(1, MB, SPAN, D),
        gains[0],
        jnp.concatenate([from_groups(w[:, :HQ]) for w in whole], axis=1).astype(jnp.float32),
        heads_of(0),
        heads_of(HD),
        rows[:48],
        gains[1],
        g_g,
        g_u,
        rows[48:],
    )


def solution(mesh):
    fine = Mesh(mesh.devices.reshape(2, 2, 4, 4, 2), ("xl", "c", "z", "y", "xh"))
    replica = ("xl", "c")
    tokens = P(replica, None, SHARD, None)
    matrix = P(SHARD, None)
    vector = P(SHARD)
    return jax.shard_map(
        on_device,
        mesh=fine,
        in_specs=(
            tokens,
            P(replica, None, SHARD),
            tokens,
            vector,
            matrix,
            matrix,
            matrix,
            matrix,
            vector,
            matrix,
            matrix,
            matrix,
        ),
        out_specs=(
            tokens,
            tokens,
            vector,
            matrix,
            matrix,
            matrix,
            matrix,
            vector,
            matrix,
            matrix,
            matrix,
        ),
        check_vma=False,
    )
```

```python
from functools import partial
import math

import jax
import jax.numpy as jnp
from jax import lax
from jax.experimental import pallas as pl
from jax.experimental.pallas import tpu as pltpu
from jax.sharding import Mesh
from jax.sharding import PartitionSpec as P

HEADS = 24
KVH = 8
HD = 64
D = 1536
FF = 3840
MB = 3
SPAN = 64
SHARDS = 32
SEQ = 2048
PARTS = 4
ROWS = MB * SPAN
BOTH = 2 * ROWS
GROUP = HEADS // KVH
HALF_KV = KVH // 2
HQ = HALF_KV * GROUP * HD
HK = HALF_KV * HD
HF = FF // 2
QKV = HQ + 2 * HK
UNIT_FF = 128
PAD_FF = 16 * UNIT_FF
REST_AT = D
GATE_AT = D + D // 3
UP_AT = GATE_AT + PAD_FF
OUT_AT = UP_AT + PAD_FF
FF_TILE = 256
FF_TILES = PAD_FF // FF_TILE
FF_ROWS = 96 * FF_TILE // UNIT_FF
CHUNK = SPAN // PARTS
TILE = 4
TILES = SHARDS // TILE
BLOCK = TILE * SPAN
TROWS = GROUP * TILE * CHUNK

SHARD = ("z", "y", "xh")
branch_scale = 1.4 / math.sqrt(52.0)
eps_norm = 1e-05
NEG = -1e30
VMEM_LIMIT = 48 * 1024 * 1024


def product(left, right):
    return jnp.dot(left, right, preferred_element_type=jnp.float32)


def product_t(left, right):
    return lax.dot_general(left, right, (((1,), (1,)), ((), ())), preferred_element_type=jnp.float32)


def t_product(left, right):
    return lax.dot_general(left, right, (((0,), (0,)), ((), ())), preferred_element_type=jnp.float32)


def swap(values):
    return lax.ppermute(values, "c", [(0, 1), (1, 0)])


def exchange(values):
    return lax.all_to_all(values, SHARD, 0, 0, tiled=True)


Q_ROWS = 2 * CHUNK
ALL_ROWS = SPAN + Q_ROWS


def to_groups(rows):
    parts = [rows[:, 192 * j : 192 * j + 128] for j in range(HALF_KV)]
    parts += [rows[:, 192 * j + 128 : 192 * j + 192] for j in range(HALF_KV)]
    return jnp.concatenate(parts, axis=1)


def from_groups(rows):
    parts = []
    for j in range(HALF_KV):
        parts += [rows[:, 128 * j : 128 * j + 128], rows[:, 512 + 64 * j : 576 + 64 * j]]
    return jnp.concatenate(parts, axis=1)


def interleave(keys, values):
    parts = []
    for j in range(HALF_KV):
        parts += [keys[:, HD * j : HD * j + HD], values[:, HD * j : HD * j + HD]]
    return jnp.concatenate(parts, axis=1)


def turn(values, cosine, sine):
    lane = lax.broadcasted_iota(jnp.int32, values.shape, values.ndim - 1)
    axis = values.ndim - 1
    other = jnp.where(lane % HD < HD // 2, pltpu.roll(values, 128 - HD // 2, axis), pltpu.roll(values, HD // 2, axis))
    return values * cosine + other * sine


def project_kernel(n_ref, w_ref, table_ref, out_ref):
    rows = n_ref[...]

    def group(g, table):
        wide = product(rows, w_ref[:, 128 * g : 128 * g + 128]).reshape(2 * MB, SPAN, 128)
        return turn(wide, table_ref[table][None], table_ref[table + 1][None]).astype(jnp.bfloat16)

    for j in range(HALF_KV):
        first, both = group(j, 0), group(6 + j, 2)
        if j % 2 == 0:
            third = group(4 + j // 2, 0)
        for o in range(2):
            for m in range(MB):
                for p in range(PARTS):
                    cut = slice(p * CHUNK, (p + 1) * CHUNK)
                    out_ref[j, o, p, m, 0:SPAN, :] = both[o * MB + m]
                    out_ref[j, o, p, m, SPAN : SPAN + CHUNK, :] = first[o * MB + m, cut]
                    out_ref[j, o, p, m, SPAN + CHUNK : ALL_ROWS, :] = third[o * MB + m, cut]


def third_head(pair_even, pair_odd):
    lane = lax.broadcasted_iota(jnp.int32, pair_even.shape, pair_even.ndim - 1)
    return jnp.where(lane < HD, pair_even, pair_odd)


def out_halves(ref):
    whole = ref[...].reshape(16, 2, 48, D // 2)
    return whole[:, 0].reshape(HQ, D // 2), whole[:, 1].reshape(HQ, D // 2)


def out_kernel(u_ref, w_ref, attn_ref, mine_ref, other_ref):
    for o in range(2):
        for m in range(MB):
            for p in range(PARTS):
                thirds = [
                    third_head(u_ref[2 * k, o, p, m, CHUNK:, :], u_ref[2 * k + 1, o, p, m, CHUNK:, :])
                    for k in range(2)
                ]
                parts = []
                for j in range(HALF_KV):
                    parts += [u_ref[j, o, p, m, :CHUNK, :], thirds[j // 2][:, HD * (j % 2) : HD * (j % 2) + HD]]
                at = (o * MB + m) * SPAN + p * CHUNK
                attn_ref[at : at + CHUNK, :] = jnp.concatenate(parts, axis=1)
    attn = attn_ref[...]
    for k, half in enumerate(out_halves(w_ref)):
        result = product(attn, half)
        cols = slice(k * (D // 2), (k + 1) * (D // 2))
        mine_ref[:, cols] = result[:ROWS]
        other_ref[:, cols] = result[ROWS:].astype(jnp.bfloat16)


def d_out_kernel(da_ref, w_ref, attn_ref, held_ref, out_ref, grad_ref, g_out, sem):
    attn_t = attn_ref[...].T
    for k in range(2):
        half = product(attn_t, da_ref[:, k * (D // 2) : (k + 1) * (D // 2)]).astype(jnp.bfloat16)
        for j in range(16):
            g_out[j * 96 + k * 48 : j * 96 + k * 48 + 48, :] = half[j * 48 : j * 48 + 48]
    copy = pltpu.make_async_copy(g_out, grad_ref.at[:, pl.ds(OUT_AT, D // 2)], sem)
    copy.start()
    left, right = out_halves(w_ref)
    rows = product_t(da_ref[:, : D // 2], left) + product_t(da_ref[:, D // 2 :], right)
    rows = rows.astype(jnp.bfloat16)
    for j in range(HALF_KV):
        first = rows[:, 192 * j : 192 * j + 128]
        if j % 2 == 0:
            third = jnp.concatenate([rows[:, 192 * j + 128 : 192 * j + 192], rows[:, 192 * j + 320 : 192 * j + 384]], axis=1)
        for o in range(2):
            for m in range(MB):
                for p in range(PARTS):
                    at = (o * MB + m) * SPAN + p * CHUNK
                    out_ref[j, o, p, m, :CHUNK, :] = first[at : at + CHUNK]
                    out_ref[j, o, p, m, CHUNK:, :] = third[at : at + CHUNK]
    copy.wait()


def collect_kernel(u_ref, table_ref, out_ref):
    def put(g, o, m, at, size, values, table, row):
        cosine = table_ref[table, row : row + size]
        sine = table_ref[table + 1, row : row + size]
        out_ref[at : at + size, 128 * g : 128 * g + 128] = turn(values, cosine, -sine).astype(jnp.bfloat16)

    wide = jnp.float32
    for o in range(2):
        for m in range(MB):
            base = (o * MB + m) * SPAN
            for j in range(HALF_KV):
                total = u_ref[j, o, 0, m, 0:SPAN, :].astype(wide)
                for p in range(1, PARTS):
                    total = total + u_ref[j, o, p, m, 0:SPAN, :].astype(wide)
                put(6 + j, o, m, base, SPAN, total, 2, 0)
            for p in range(PARTS):
                at = base + p * CHUNK
                for j in range(HALF_KV):
                    first = u_ref[j, o, p, m, SPAN : SPAN + CHUNK, :].astype(wide)
                    put(j, o, m, at, CHUNK, first, 0, p * CHUNK)
                for k in range(2):
                    third = third_head(
                        u_ref[2 * k, o, p, m, SPAN + CHUNK : ALL_ROWS, :].astype(wide),
                        u_ref[2 * k + 1, o, p, m, SPAN + CHUNK : ALL_ROWS, :].astype(wide),
                    )
                    put(4 + k, o, m, at, CHUNK, third, 0, p * CHUNK)


def stack_heads(first, third, odd):
    last = jnp.where(odd == 1, third[:, HD:], third[:, :HD])
    return jnp.concatenate([first[:, :HD], first[:, HD:], last], axis=0)


def lay_heads(rows):
    size = TILE * CHUNK
    parts = [rows[g * size : (g + 1) * size] for g in range(GROUP)]
    shape = (TILE, CHUNK, 128)
    return (
        jnp.concatenate(parts[:2], axis=1).astype(jnp.bfloat16).reshape(shape),
        jnp.concatenate([parts[2], parts[2]], axis=1).astype(jnp.bfloat16).reshape(shape),
    )


def tile_mask(part, start_rows, tile, blocks):
    wide = blocks * BLOCK
    row = lax.broadcasted_iota(jnp.int32, (TROWS, 1), 0)
    inside = lax.rem(row, TILE * CHUNK)
    q_pos = tile * BLOCK + (inside // CHUNK) * SPAN + part * CHUNK + lax.rem(inside, CHUNK)
    k_pos = (tile + 1 - blocks) * BLOCK + lax.broadcasted_iota(jnp.int32, (TROWS, wide), 1)
    return (k_pos >= start_rows) & (k_pos <= q_pos)


def tile_queries(ref, tile, begin, odd):
    where = pl.ds(tile * TILE, TILE)
    first = ref[where, 0, begin : begin + CHUNK, :].reshape(TILE * CHUNK, 128)
    third = ref[where, 0, begin + CHUNK : begin + 2 * CHUNK, :].reshape(TILE * CHUNK, 128)
    return stack_heads(first, third, odd)


def tile_keys(ref, begin, blocks):
    return ref[pl.ds(begin * TILE, blocks * TILE), 0, 0:SPAN, :].reshape(blocks * BLOCK, 128)


def each_tile(first_ref, work):
    micro = pl.program_id(0)

    def body(tile, carry):
        needed = tile + 1 - first_ref[micro * TILES + tile]
        for blocks in range(1, TILES + 1):
            pl.when(needed == blocks)(partial(work, tile, blocks))
        return carry

    lax.fori_loop(0, TILES, body, 0)


def fwd_kernel(unit_ref, first_ref, u_ref, start_ref, o_ref, lse_ref):
    part, odd = unit_ref[0], unit_ref[1]

    def work(tile, blocks):
        q_rows = tile_queries(u_ref, tile, SPAN, odd) * jnp.bfloat16(0.125)
        keys = tile_keys(u_ref, tile + 1 - blocks, blocks)
        scores = product_t(q_rows, keys[:, :HD])
        allowed = tile_mask(part, start_ref[0, tile][:, :1], tile, blocks)
        scores = jnp.where(allowed, scores, NEG)
        highest = jnp.max(scores, axis=-1, keepdims=True)
        expo = jnp.exp(scores - highest)
        total = jnp.sum(expo, axis=-1, keepdims=True)
        mixed = product(expo.astype(jnp.bfloat16), keys[:, HD:]) / total
        where = pl.ds(tile * TILE, TILE)
        o_ref[where, 0, :CHUNK, :], o_ref[where, 0, CHUNK:, :] = lay_heads(mixed)
        lse_ref[0, tile] = jnp.broadcast_to(highest + jnp.log(total), (TROWS, 128))

    each_tile(first_ref, work)


def bwd_kernel(unit_ref, first_ref, u_ref, start_ref, do_ref, lse_ref, d_ref, acc):
    part, odd = unit_ref[0], unit_ref[1]
    acc[...] = jnp.zeros_like(acc)

    def work(tile, blocks):
        begin = tile + 1 - blocks
        q_rows = tile_queries(u_ref, tile, SPAN, odd) * jnp.bfloat16(0.125)
        d_rows = tile_queries(do_ref, tile, 0, odd)
        keys = tile_keys(u_ref, begin, blocks)
        scores = product_t(q_rows, keys[:, :HD])
        allowed = tile_mask(part, start_ref[0, tile][:, :1], tile, blocks)
        probs = jnp.where(allowed, jnp.exp(scores - lse_ref[0, tile][:, :1]), 0.0)
        d_probs = product_t(d_rows, keys[:, HD:])
        offset = jnp.sum(d_probs * probs, axis=-1, keepdims=True)
        d_scores = (probs * (d_probs - offset)).astype(jnp.bfloat16)
        d_query = product(d_scores, keys[:, :HD]) * 0.125
        at = pl.ds(tile * TILE, TILE)
        d_ref[at, 0, SPAN : SPAN + CHUNK, :], d_ref[at, 0, SPAN + CHUNK : ALL_ROWS, :] = lay_heads(d_query)
        d_key = t_product(d_scores, q_rows)
        d_value = t_product(probs.astype(jnp.bfloat16), d_rows)
        where = pl.ds(begin * BLOCK, blocks * BLOCK)
        acc[where, :] += jnp.concatenate([d_key, d_value], axis=1)

    each_tile(first_ref, work)
    d_ref[:, 0, 0:SPAN, :] = acc[...].astype(jnp.bfloat16).reshape(SHARDS, SPAN, 128)


SMEM = pl.BlockSpec(memory_space=pltpu.SMEM)
UNIT_SPEC = pl.BlockSpec((SHARDS, 1, ALL_ROWS, 128), lambda m: (0, m, 0, 0))
QUERY_SPEC = pl.BlockSpec((SHARDS, 1, Q_ROWS, 128), lambda m: (0, m, 0, 0))
COL_SPEC = pl.BlockSpec((1, TILES, TROWS, 128), lambda m: (m, 0, 0, 0))
COL_SHAPE = jax.ShapeDtypeStruct((MB, TILES, TROWS, 128), jnp.float32)
PARAMS = pltpu.CompilerParams(vmem_limit_bytes=VMEM_LIMIT)


def split_units(values):
    return values.reshape((HALF_KV, 2, PARTS) + values.shape[1:])


def low_shape(*dims):
    return jax.ShapeDtypeStruct(dims, jnp.bfloat16)


def project(n1, w_qkv, tables):
    shape = low_shape(HALF_KV, 2, PARTS, MB, ALL_ROWS, 128)
    out = pl.pallas_call(project_kernel, out_shape=shape, compiler_params=PARAMS, cost_estimate=cost(6), name="project")(n1, w_qkv, tables)
    return out.reshape(SHARDS, MB, ALL_ROWS, 128)


def whole_spec(*dims):
    return pl.BlockSpec(dims, lambda i: (0,) * len(dims))


OUT_SPEC = pl.BlockSpec((D, D // 2), lambda i: (0, OUT_AT // (D // 2)))


def cost(micros):
    return pl.CostEstimate(flops=int(micros * 1e9), bytes_accessed=1 << 20, transcendentals=0)


def out_project(units, w_all):
    return pl.pallas_call(
        out_kernel,
        grid=(1,),
        in_specs=[whole_spec(HALF_KV, 2, PARTS, MB, Q_ROWS, 128), OUT_SPEC],
        out_specs=[whole_spec(BOTH, HQ), whole_spec(ROWS, D), whole_spec(ROWS, D)],
        out_shape=[low_shape(BOTH, HQ), jax.ShapeDtypeStruct((ROWS, D), jnp.float32), low_shape(ROWS, D)],
        compiler_params=PARAMS,
        cost_estimate=cost(3),
        name="out_project",
    )(split_units(units), w_all)


def d_out_project(da, w_all, attn, g_ffn):
    dims = (HALF_KV, 2, PARTS, MB, Q_ROWS, 128)
    anywhere = pl.BlockSpec(memory_space=pl.ANY)
    out, grads = pl.pallas_call(
        d_out_kernel,
        grid=(1,),
        in_specs=[whole_spec(BOTH, D), OUT_SPEC, whole_spec(BOTH, HQ), anywhere],
        out_specs=[whole_spec(*dims), anywhere],
        out_shape=[low_shape(*dims), low_shape(*g_ffn.shape)],
        scratch_shapes=[pltpu.VMEM((D, D // 2), jnp.bfloat16), pltpu.SemaphoreType.DMA],
        input_output_aliases={3: 1},
        compiler_params=PARAMS,
        cost_estimate=cost(5),
        name="d_out_project",
    )(da, w_all, attn, g_ffn)
    return out.reshape(SHARDS, MB, Q_ROWS, 128), grads


def ffn_kernel(
    n_ref, df_ref, main_ref, rest_ref, gate_ref, up_ref,
    y_mine_ref, y_other_ref, dn_mine_ref, dn_other_ref, grad_ref,
    n_t, y_acc, dn_acc, g_gate, g_up, g_main, g_rest, sems,
):
    step = pl.program_id(0)
    slot = lax.rem(step, 2)

    def copies(at, slot):
        cols, rows = at * FF_TILE, at * FF_ROWS
        return [
            pltpu.make_async_copy(
                g_gate.at[slot], grad_ref.at[:, pl.ds(pl.multiple_of(GATE_AT + cols, FF_TILE), FF_TILE)], sems.at[slot, 0]
            ),
            pltpu.make_async_copy(
                g_up.at[slot], grad_ref.at[:, pl.ds(pl.multiple_of(UP_AT + cols, FF_TILE), FF_TILE)], sems.at[slot, 1]
            ),
            pltpu.make_async_copy(
                g_main.at[slot], grad_ref.at[pl.ds(pl.multiple_of(rows, 64), FF_ROWS), pl.ds(0, D)], sems.at[slot, 2]
            ),
            pltpu.make_async_copy(
                g_rest.at[slot],
                grad_ref.at[pl.ds(pl.multiple_of(rows, 64), FF_ROWS), pl.ds(REST_AT, D // 3)],
                sems.at[slot, 3],
            ),
        ]

    @pl.when(step == 0)
    def _():
        n_t[...] = n_ref[...].T
        y_acc[...] = jnp.zeros_like(y_acc)
        dn_acc[...] = jnp.zeros_like(dn_acc)

    @pl.when(step >= 2)
    def _():
        for copy in copies(step - 2, slot):
            copy.wait()

    low = jnp.bfloat16
    units = []
    for j in range(FF_TILE // UNIT_FF):
        rest = [rest_ref[j * 96 + q * 32 : j * 96 + q * 32 + 32, :] for q in range(3)]
        units += [main_ref[j * 96 : j * 96 + 96, :], jnp.concatenate(rest, axis=1)]
    w_down = jnp.concatenate(units, axis=0)
    rows, df = n_ref[...], df_ref[...]
    gate, up = product(rows, gate_ref[...]), product(rows, up_ref[...])
    sigma = jax.nn.sigmoid(gate)
    silu = gate * sigma
    act = (silu * up).astype(low)
    d_act = product_t(df, w_down)
    d_gate = (d_act * up * sigma * (1.0 + gate * (1.0 - sigma))).astype(low)
    d_up = (d_act * silu).astype(low)
    y_acc[...] += product(act, w_down)
    dn_acc[...] += product_t(d_gate, gate_ref[...]) + product_t(d_up, up_ref[...])
    g_gate[slot] = product(n_t[...], d_gate).astype(low)
    g_up[slot] = product(n_t[...], d_up).astype(low)
    g_down = product(act.T, df).astype(low)
    for j in range(FF_TILE // UNIT_FF):
        g_main[slot, j * 96 : j * 96 + 96, :] = g_down[j * UNIT_FF : j * UNIT_FF + 96]
        for q in range(3):
            g_rest[slot, j * 96 + q * 32 : j * 96 + q * 32 + 32, :] = g_down[
                j * UNIT_FF + 96 : (j + 1) * UNIT_FF, q * (D // 3) : (q + 1) * (D // 3)
            ]
    for copy in copies(step, slot):
        copy.start()

    @pl.when(step == FF_TILES - 1)
    def _():
        y_mine_ref[...] = y_acc[:ROWS]
        y_other_ref[...] = y_acc[ROWS:].astype(low)
        dn_mine_ref[...] = dn_acc[:ROWS]
        dn_other_ref[...] = dn_acc[ROWS:].astype(low)
        for back in (1, 0):
            for copy in copies(step - back, lax.rem(step - back, 2)):
                copy.wait()


def feed_forward(n2, df, w_all):
    wide = jax.ShapeDtypeStruct((ROWS, D), jnp.float32)
    return pl.pallas_call(
        ffn_kernel,
        grid=(FF_TILES,),
        in_specs=[
            whole_spec(BOTH, D),
            whole_spec(BOTH, D),
            pl.BlockSpec((FF_ROWS, D), lambda t: (t, 0)),
            pl.BlockSpec((FF_ROWS, D // 3), lambda t: (t, REST_AT // (D // 3))),
            pl.BlockSpec((D, FF_TILE), lambda t: (0, GATE_AT // FF_TILE + t)),
            pl.BlockSpec((D, FF_TILE), lambda t: (0, UP_AT // FF_TILE + t)),
        ],
        out_specs=[whole_spec(ROWS, D)] * 4 + [pl.BlockSpec(memory_space=pl.ANY)],
        out_shape=[wide, low_shape(ROWS, D), wide, low_shape(ROWS, D), low_shape(D, OUT_AT + D // 2)],
        scratch_shapes=[
            pltpu.VMEM((D, BOTH), jnp.bfloat16),
            pltpu.VMEM((BOTH, D), jnp.float32),
            pltpu.VMEM((BOTH, D), jnp.float32),
            pltpu.VMEM((2, D, FF_TILE), jnp.bfloat16),
            pltpu.VMEM((2, D, FF_TILE), jnp.bfloat16),
            pltpu.VMEM((2, FF_ROWS, D), jnp.bfloat16),
            pltpu.VMEM((2, FF_ROWS, D // 3), jnp.bfloat16),
            pltpu.SemaphoreType.DMA((2, 4)),
        ],
        compiler_params=PARAMS,
        cost_estimate=cost(30),
        name="feed_forward",
    )(n2, df, w_all, w_all, w_all, w_all)


def collect(units, tables):
    shape = low_shape(BOTH, HQ + 2 * HK)
    return pl.pallas_call(collect_kernel, out_shape=shape, compiler_params=PARAMS, cost_estimate=cost(4), name="collect")(
        split_units(units), tables
    )


def attend_fwd(unit, first, units, starts):
    return pl.pallas_call(
        fwd_kernel,
        grid=(MB,),
        in_specs=[SMEM, SMEM, UNIT_SPEC, COL_SPEC],
        out_specs=[QUERY_SPEC, COL_SPEC],
        out_shape=[low_shape(SHARDS, MB, Q_ROWS, 128), COL_SHAPE],
        compiler_params=PARAMS,
        cost_estimate=cost(20),
        name="attend_forward",
    )(unit, first, units, starts)


def attend_bwd(unit, first, units, starts, d_mixed, lse):
    return pl.pallas_call(
        bwd_kernel,
        grid=(MB,),
        in_specs=[SMEM, SMEM, UNIT_SPEC, COL_SPEC, QUERY_SPEC, COL_SPEC],
        out_specs=UNIT_SPEC,
        out_shape=low_shape(SHARDS, MB, ALL_ROWS, 128),
        scratch_shapes=[pltpu.VMEM((SEQ, 128), jnp.float32)],
        compiler_params=PARAMS,
        cost_estimate=cost(27),
        name="attend_backward",
    )(unit, first, units, starts, d_mixed, lse)


def piece_perm():
    return [(k * SHARDS + s, (s // 16) * SHARDS + 2 * (s % 16) + k) for k in range(2) for s in range(SHARDS)]


def shift(values, axis, step):
    if axis == "x":
        line = lambda x: (x % 2) * 2 + x // 2
        return lax.ppermute(values, ("xl", "xh"), [(line(i), line((i + step) % 4)) for i in range(4)])
    return lax.ppermute(values, axis, [(i, (i + step) % 4) for i in range(4)])


def place(axis):
    if axis == "x":
        return lax.axis_index("xh") * 2 + lax.axis_index("xl")
    return lax.axis_index(axis)


def flip(values, axis):
    return lax.ppermute(values, axis, [(0, 1), (1, 0)])


def col_half(core, local):
    half = local.shape[1] // 2
    return lax.dynamic_slice_in_dim(local, core * half, half, axis=1)


def pad_units(local):
    return jnp.pad(local.reshape(-1, 16, 120), ((0, 0), (0, 0), (0, UNIT_FF - 120))).reshape(-1, PAD_FF)


def crop_units(local):
    return local.reshape(-1, 16, UNIT_FF)[:, :, :120].reshape(-1, HF)


def fold(rows, parts):
    n, r, w = rows.shape
    return rows.reshape(n, r, parts, w // parts).transpose(0, 2, 1, 3).reshape(n, parts * r, w // parts)


def unfold(rows, parts):
    n, r, w = rows.shape
    return rows.reshape(n, parts, r // parts, w).transpose(0, 2, 1, 3).reshape(n, r // parts, parts * w)


def wide_sum(*values):
    total = values[0].astype(jnp.float32)
    for value in values[1:]:
        total = total + value.astype(jnp.float32)
    return total.astype(jnp.bfloat16)


def after(values, event):
    return lax.optimization_barrier((values, event))[0]


def total_axis(values, axis):
    return values + shift(values, axis, 1) + shift(values, axis, 2) + shift(values, axis, 3)


def reduce_x(values):
    size = values.shape[0] // 2
    me = lax.axis_index("xh")
    keep = lax.dynamic_slice_in_dim(values, me * size, size, axis=0)
    send = lax.dynamic_slice_in_dim(values, (1 - me) * size, size, axis=0)
    cross = lax.ppermute(send, ("xl", "xh"), [(i, 3 - i) for i in range(4)])
    return wide_sum(keep, flip(keep, "xl"), flip(send, "xh"), cross)


def to_owner(values, a):
    pairs = [
        ((c * 16 + j) * 2 + xh, (xh ^ a) * SHARDS + 16 * c + j) for c in range(2) for j in range(16) for xh in range(2)
    ]
    return lax.ppermute(values, ("c",) + SHARD, pairs)


def add_pair(values, axis):
    return wide_sum(values, flip(values, axis))


def join_pair(mine, axis, dim):
    other = flip(mine, axis)
    lower = lax.axis_index(axis) == 0
    return jnp.concatenate([jnp.where(lower, mine, other), jnp.where(lower, other, mine)], axis=dim)


def join_cores(mine):
    return join_pair(mine, "c", 1).astype(jnp.float32)


def scatter_sum(values):
    return jnp.sum(exchange(values).astype(jnp.float32), axis=0).astype(jnp.bfloat16)


def on_device(
    hidden_in,
    doc_ids,
    out_grad,
    norm_attn,
    w_query,
    w_key,
    w_value,
    w_out,
    norm_ffn,
    w_gate,
    w_up,
    w_down,
):
    core = lax.axis_index("c")
    shard = lax.axis_index(SHARD)
    low = jnp.bfloat16

    rows_in = lax.ppermute(jnp.concatenate([w_out, w_down], axis=0), ("c",) + SHARD, piece_perm())
    gu_piece = jnp.concatenate([pad_units(col_half(core, w_gate)), pad_units(col_half(core, w_up))], axis=1)
    w_all = lax.all_gather(
        jnp.concatenate(
            [
                rows_in[48:144],
                fold(jnp.pad(rows_in[144:], ((0, 8), (0, 0)))[None], 3)[0],
                join_pair(gu_piece, "xh", 0),
                fold(rows_in[:48][None], 2)[0],
            ],
            axis=1,
        ),
        ("z", "y"),
        axis=0,
        tiled=True,
    )
    small = jnp.concatenate(
        [norm_attn[:, None], norm_ffn[:, None], doc_ids.reshape(48, 4).astype(low), jnp.zeros((48, 122), low)], axis=1
    )
    piece = jnp.concatenate(
        [to_groups(col_half(core, w_query)), interleave(col_half(core, w_key), col_half(core, w_value)), small], axis=1
    )
    w_first = exchange(jnp.broadcast_to(piece[None], (SHARDS, 48, QKV + 128)))
    small = w_first[:, :, QKV : QKV + 6]
    w_first = w_first.reshape(D, QKV + 128)
    w_qkv = w_first[:, :QKV]
    gain_attn = small[:, :, 0].reshape(1, D).astype(jnp.float32)
    gain_ffn = small[:, :, 1].reshape(1, D).astype(jnp.float32)
    docs_mine = small[:, :, 2:].reshape(SHARDS, MB, SPAN).transpose(1, 0, 2).reshape(MB, SEQ)
    docs_other = swap(docs_mine)

    x_low = hidden_in.reshape(ROWS, D)
    x = x_low.astype(jnp.float32)
    x_both = jnp.concatenate([x_low, swap(x_low)], axis=0).astype(jnp.float32)
    dy_low = out_grad.reshape(ROWS, D)
    dy = dy_low.astype(jnp.float32)
    df = (branch_scale * jnp.concatenate([dy_low, swap(dy_low)], axis=0).astype(jnp.float32)).astype(low)

    which = lax.rem(shard // PARTS, 2)
    part = lax.rem(shard, PARTS)
    docs = jnp.where(which == 0, docs_mine, docs_other).astype(jnp.float32)
    counted = jnp.sum((docs[:, None, :] < docs[:, :, None]).astype(jnp.int32), axis=-1)
    q_start = lax.dynamic_slice_in_dim(counted.reshape(MB, SHARDS, SPAN), part * CHUNK, CHUNK, axis=2)
    q_start = q_start.reshape(MB, TILES, 1, TILE * CHUNK)
    first = (q_start[:, :, 0, 0] // BLOCK).reshape(-1)
    starts = jnp.broadcast_to(q_start, (MB, TILES, GROUP, TILE * CHUNK)).reshape(MB, TILES, TROWS, 1)
    starts = jnp.broadcast_to(starts, (MB, TILES, TROWS, 128))
    unit = jnp.stack([part, lax.rem(shard // (2 * PARTS), 2)]).astype(jnp.int32)

    places = (shard * SPAN + jnp.arange(SPAN, dtype=jnp.int32)).astype(jnp.float32)
    half_size = HD // 2
    inverse = jnp.exp(-jnp.arange(half_size, dtype=jnp.float32) * (math.log(10000.0) / half_size))
    angles = places[:, None] * inverse[None, :]
    cosine, sine = jnp.cos(angles), jnp.sin(angles)
    cosine = jnp.concatenate([cosine, cosine], axis=1)
    sine = jnp.concatenate([-sine, sine], axis=1)
    tables = jnp.stack(
        [
            jnp.concatenate([cosine, cosine], axis=1),
            jnp.concatenate([sine, sine], axis=1),
            jnp.concatenate([cosine, jnp.ones_like(cosine)], axis=1),
            jnp.concatenate([sine, jnp.zeros_like(sine)], axis=1),
        ]
    )

    r1_both = lax.rsqrt(jnp.mean(x_both * x_both, axis=-1, keepdims=True) + eps_norm)
    r1 = r1_both[:ROWS]
    n1 = (x_both * r1_both * gain_attn).astype(low)
    units = exchange(project(n1, w_first, tables))
    unit_o, lse = attend_fwd(unit, first, units, starts)
    attn, y1_mine, y1_other = out_project(exchange(unit_o), w_all)
    hmid = x + branch_scale * (y1_mine + swap(y1_other).astype(jnp.float32))

    r2 = lax.rsqrt(jnp.mean(hmid * hmid, axis=-1, keepdims=True) + eps_norm)
    z2 = hmid * r2
    n2_mine = (z2 * gain_ffn).astype(low)
    n2 = jnp.concatenate([n2_mine, swap(n2_mine)], axis=0)
    y2_mine, y2_other, dn2_mine, dn2_other, g_ffn = feed_forward(n2, df, w_all)
    result = hmid + branch_scale * (y2_mine + swap(y2_other).astype(jnp.float32))

    dn2 = dn2_mine + swap(dn2_other).astype(jnp.float32)
    e2 = dn2 * gain_ffn
    g_gain_ffn = jnp.sum(dn2 * z2, axis=0)
    dh = dy + r2 * (e2 - z2 * jnp.mean(e2 * z2, axis=-1, keepdims=True))

    da_mine = (branch_scale * dh).astype(low)
    da = jnp.concatenate([da_mine, swap(da_mine)], axis=0)
    unit_do, g_all = d_out_project(da, w_all, attn, g_ffn)
    s_all = lax.psum_scatter(g_all, ("z", "y"), scatter_dimension=0, tiled=True)
    unit_do = exchange(unit_do)
    unit_d = attend_bwd(unit, first, units, starts, unit_do, lse)
    d_qkv = collect(exchange(unit_d), tables)

    g_qkv = t_product(n1, d_qkv).astype(low)
    dn1_both = product_t(d_qkv, w_qkv)
    dn1 = dn1_both[:ROWS] + swap(dn1_both[ROWS:].astype(low)).astype(jnp.float32)
    z1 = x * r1
    e1 = dn1 * gain_attn
    g_gain_attn = jnp.sum(dn1 * z1, axis=0)
    grad_in = (dh + r1 * (e1 - z1 * jnp.mean(e1 * z1, axis=-1, keepdims=True))).astype(low)

    gains = jnp.concatenate(
        [g_gain_attn[:, None].astype(low), g_gain_ffn[:, None].astype(low), jnp.zeros((D, 126), low)], axis=1
    )
    g_qkv = jnp.concatenate([g_qkv, gains], axis=1)
    s_qkv = add_pair(scatter_sum(g_qkv.reshape(SHARDS, 48, QKV + 128)), "xl")
    s_all = reduce_x(after(s_all, d_qkv))
    rows = jnp.concatenate([s_all[:, :GATE_AT], s_all[:, OUT_AT:]], axis=1)
    here, there = to_owner(rows, 0), to_owner(rows, 1)
    rows = jnp.concatenate([jnp.where(core == 0, here, there), jnp.where(core == 0, there, here)], axis=0)
    g_o = unfold(rows[None, :, GATE_AT:], 2)[0].astype(jnp.float32)
    rest = unfold(rows[None, :, REST_AT:GATE_AT], 3)[0][:24]
    g_d = jnp.concatenate([rows[:, :D], rest], axis=0).astype(jnp.float32)
    s_gu = s_all[:, GATE_AT:OUT_AT]
    s_gu = jnp.concatenate([crop_units(s_gu[:, :PAD_FF]), crop_units(s_gu[:, PAD_FF:])], axis=1)
    other = swap(s_gu)
    lower = core == 0
    g_g, g_u = [
        jnp.concatenate([jnp.where(lower, m, t), jnp.where(lower, t, m)], axis=1).astype(jnp.float32)
        for m, t in ((s_gu[:, :HF], other[:, :HF]), (s_gu[:, HF:], other[:, HF:]))
    ]
    other = swap(s_qkv)
    whole = [jnp.where(lower, s_qkv, other), jnp.where(lower, other, s_qkv)]
    gains = s_qkv[:, QKV : QKV + 2].astype(jnp.float32) + other[:, QKV : QKV + 2].astype(jnp.float32)

    def heads_of(offset):
        return jnp.concatenate(
            [w[:, HQ + 128 * j + offset : HQ + 128 * j + offset + HD] for w in whole for j in range(HALF_KV)], axis=1
        ).astype(jnp.float32)

    return (
        result.reshape(1, MB, SPAN, D).astype(low),
        grad_in.reshape(1, MB, SPAN, D),
        gains[:, 0],
        jnp.concatenate([from_groups(w[:, :HQ]) for w in whole], axis=1).astype(jnp.float32),
        heads_of(0),
        heads_of(HD),
        g_o,
        gains[:, 1],
        g_g,
        g_u,
        g_d,
    )


def solution(mesh):
    fine = Mesh(mesh.devices.reshape(2, 2, 4, 4, 2), ("xl", "c", "z", "y", "xh"))
    replica = ("xl", "c")
    tokens = P(replica, None, SHARD, None)
    matrix = P(SHARD, None)
    vector = P(SHARD)
    return jax.shard_map(
        on_device,
        mesh=fine,
        in_specs=(
            tokens,
            P(replica, None, SHARD),
            tokens,
            vector,
            matrix,
            matrix,
            matrix,
            matrix,
            vector,
            matrix,
            matrix,
            matrix,
        ),
        out_specs=(
            tokens,
            tokens,
            vector,
            matrix,
            matrix,
            matrix,
            matrix,
            vector,
            matrix,
            matrix,
            matrix,
        ),
        check_vma=False,
    )
```

```python
from functools import partial
import math

import jax
import jax.numpy as jnp
from jax import lax
from jax.experimental import pallas as pl
from jax.experimental.pallas import tpu as pltpu
from jax.sharding import Mesh
from jax.sharding import PartitionSpec as P

HEADS = 24
KVH = 8
HD = 64
D = 1536
FF = 3840
MB = 3
SPAN = 64
SHARDS = 32
SEQ = 2048
PARTS = 4
ROWS = MB * SPAN
BOTH = 2 * ROWS
GROUP = HEADS // KVH
HALF_KV = KVH // 2
HQ = HALF_KV * GROUP * HD
HK = HALF_KV * HD
HF = FF // 2
QKV = HQ + 2 * HK
UNIT_FF = 128
PAD_FF = 16 * UNIT_FF
REST_AT = D
GATE_AT = D + D // 3
UP_AT = GATE_AT + PAD_FF
OUT_AT = UP_AT + PAD_FF
FF_TILE = 256
FF_TILES = PAD_FF // FF_TILE
FF_ROWS = 96 * FF_TILE // UNIT_FF
CHUNK = SPAN // PARTS
TILE = 4
TILES = SHARDS // TILE
BLOCK = TILE * SPAN
TROWS = GROUP * TILE * CHUNK

SHARD = ("z", "y", "xh")
branch_scale = 1.4 / math.sqrt(52.0)
eps_norm = 1e-05
NEG = -1e30
VMEM_LIMIT = 48 * 1024 * 1024


def product(left, right):
    return jnp.dot(left, right, preferred_element_type=jnp.float32)


def product_t(left, right):
    return lax.dot_general(left, right, (((1,), (1,)), ((), ())), preferred_element_type=jnp.float32)


def t_product(left, right):
    return lax.dot_general(left, right, (((0,), (0,)), ((), ())), preferred_element_type=jnp.float32)


def swap(values):
    return lax.ppermute(values, "c", [(0, 1), (1, 0)])


def exchange(values):
    return lax.all_to_all(values, SHARD, 0, 0, tiled=True)


Q_ROWS = 2 * CHUNK
ALL_ROWS = SPAN + Q_ROWS


def to_groups(rows):
    parts = [rows[:, 192 * j : 192 * j + 128] for j in range(HALF_KV)]
    parts += [rows[:, 192 * j + 128 : 192 * j + 192] for j in range(HALF_KV)]
    return jnp.concatenate(parts, axis=1)


def from_groups(rows):
    parts = []
    for j in range(HALF_KV):
        parts += [rows[:, 128 * j : 128 * j + 128], rows[:, 512 + 64 * j : 576 + 64 * j]]
    return jnp.concatenate(parts, axis=1)


def interleave(keys, values):
    parts = []
    for j in range(HALF_KV):
        parts += [keys[:, HD * j : HD * j + HD], values[:, HD * j : HD * j + HD]]
    return jnp.concatenate(parts, axis=1)


def turn(values, cosine, sine):
    lane = lax.broadcasted_iota(jnp.int32, values.shape, values.ndim - 1)
    axis = values.ndim - 1
    other = jnp.where(lane % HD < HD // 2, pltpu.roll(values, 128 - HD // 2, axis), pltpu.roll(values, HD // 2, axis))
    return values * cosine + other * sine


def project_kernel(n_ref, w_ref, table_ref, out_ref):
    rows = n_ref[...]

    def group(g, table):
        wide = product(rows, w_ref[:, 128 * g : 128 * g + 128]).reshape(2 * MB, SPAN, 128)
        return turn(wide, table_ref[table][None], table_ref[table + 1][None]).astype(jnp.bfloat16)

    for j in range(HALF_KV):
        first, both = group(j, 0), group(6 + j, 2)
        if j % 2 == 0:
            third = group(4 + j // 2, 0)
        for o in range(2):
            for m in range(MB):
                for p in range(PARTS):
                    cut = slice(p * CHUNK, (p + 1) * CHUNK)
                    out_ref[j, o, p, m, 0:SPAN, :] = both[o * MB + m]
                    out_ref[j, o, p, m, SPAN : SPAN + CHUNK, :] = first[o * MB + m, cut]
                    out_ref[j, o, p, m, SPAN + CHUNK : ALL_ROWS, :] = third[o * MB + m, cut]


def third_head(pair_even, pair_odd):
    lane = lax.broadcasted_iota(jnp.int32, pair_even.shape, pair_even.ndim - 1)
    return jnp.where(lane < HD, pair_even, pair_odd)


def out_halves(ref):
    whole = ref[...].reshape(16, 2, 48, D // 2)
    return whole[:, 0].reshape(HQ, D // 2), whole[:, 1].reshape(HQ, D // 2)


def out_kernel(u_ref, w_ref, attn_ref, mine_ref, other_ref):
    for o in range(2):
        for m in range(MB):
            for p in range(PARTS):
                thirds = [
                    third_head(u_ref[2 * k, o, p, m, CHUNK:, :], u_ref[2 * k + 1, o, p, m, CHUNK:, :])
                    for k in range(2)
                ]
                parts = []
                for j in range(HALF_KV):
                    parts += [u_ref[j, o, p, m, :CHUNK, :], thirds[j // 2][:, HD * (j % 2) : HD * (j % 2) + HD]]
                at = (o * MB + m) * SPAN + p * CHUNK
                attn_ref[at : at + CHUNK, :] = jnp.concatenate(parts, axis=1)
    attn = attn_ref[...]
    for k, half in enumerate(out_halves(w_ref)):
        result = product(attn, half)
        cols = slice(k * (D // 2), (k + 1) * (D // 2))
        mine_ref[:, cols] = result[:ROWS]
        other_ref[:, cols] = result[ROWS:].astype(jnp.bfloat16)


def d_out_kernel(da_ref, w_ref, out_ref):
    left, right = out_halves(w_ref)
    rows = product_t(da_ref[:, : D // 2], left) + product_t(da_ref[:, D // 2 :], right)
    rows = rows.astype(jnp.bfloat16)
    for j in range(HALF_KV):
        first = rows[:, 192 * j : 192 * j + 128]
        if j % 2 == 0:
            third = jnp.concatenate([rows[:, 192 * j + 128 : 192 * j + 192], rows[:, 192 * j + 320 : 192 * j + 384]], axis=1)
        for o in range(2):
            for m in range(MB):
                for p in range(PARTS):
                    at = (o * MB + m) * SPAN + p * CHUNK
                    out_ref[j, o, p, m, :CHUNK, :] = first[at : at + CHUNK]
                    out_ref[j, o, p, m, CHUNK:, :] = third[at : at + CHUNK]


def collect_kernel(u_ref, table_ref, out_ref):
    def put(g, o, m, at, size, values, table, row):
        cosine = table_ref[table, row : row + size]
        sine = table_ref[table + 1, row : row + size]
        out_ref[at : at + size, 128 * g : 128 * g + 128] = turn(values, cosine, -sine).astype(jnp.bfloat16)

    wide = jnp.float32
    for o in range(2):
        for m in range(MB):
            base = (o * MB + m) * SPAN
            for j in range(HALF_KV):
                total = u_ref[j, o, 0, m, 0:SPAN, :].astype(wide)
                for p in range(1, PARTS):
                    total = total + u_ref[j, o, p, m, 0:SPAN, :].astype(wide)
                put(6 + j, o, m, base, SPAN, total, 2, 0)
            for p in range(PARTS):
                at = base + p * CHUNK
                for j in range(HALF_KV):
                    first = u_ref[j, o, p, m, SPAN : SPAN + CHUNK, :].astype(wide)
                    put(j, o, m, at, CHUNK, first, 0, p * CHUNK)
                for k in range(2):
                    third = third_head(
                        u_ref[2 * k, o, p, m, SPAN + CHUNK : ALL_ROWS, :].astype(wide),
                        u_ref[2 * k + 1, o, p, m, SPAN + CHUNK : ALL_ROWS, :].astype(wide),
                    )
                    put(4 + k, o, m, at, CHUNK, third, 0, p * CHUNK)


def gradient_kernel(n_ref, d_ref, gains_ref, out_ref):
    out_ref[:, :QKV] = product(n_ref[...].T, d_ref[...]).astype(jnp.bfloat16)
    gains = jnp.concatenate([gains_ref[...], jnp.zeros((120, D), jnp.float32)], axis=0)
    out_ref[:, QKV:] = gains.T.astype(jnp.bfloat16)


def stack_heads(first, third, odd):
    last = jnp.where(odd == 1, third[:, HD:], third[:, :HD])
    return jnp.concatenate([first[:, :HD], first[:, HD:], last], axis=0)


def lay_heads(rows):
    size = TILE * CHUNK
    parts = [rows[g * size : (g + 1) * size] for g in range(GROUP)]
    shape = (TILE, CHUNK, 128)
    return (
        jnp.concatenate(parts[:2], axis=1).astype(jnp.bfloat16).reshape(shape),
        jnp.concatenate([parts[2], parts[2]], axis=1).astype(jnp.bfloat16).reshape(shape),
    )


def tile_mask(part, start_rows, tile, blocks):
    wide = blocks * BLOCK
    row = lax.broadcasted_iota(jnp.int32, (TROWS, 1), 0)
    inside = lax.rem(row, TILE * CHUNK)
    q_pos = tile * BLOCK + (inside // CHUNK) * SPAN + part * CHUNK + lax.rem(inside, CHUNK)
    k_pos = (tile + 1 - blocks) * BLOCK + lax.broadcasted_iota(jnp.int32, (TROWS, wide), 1)
    return (k_pos >= start_rows) & (k_pos <= q_pos)


def tile_queries(ref, tile, begin, odd):
    where = pl.ds(tile * TILE, TILE)
    first = ref[where, 0, begin : begin + CHUNK, :].reshape(TILE * CHUNK, 128)
    third = ref[where, 0, begin + CHUNK : begin + 2 * CHUNK, :].reshape(TILE * CHUNK, 128)
    return stack_heads(first, third, odd)


def tile_keys(ref, begin, blocks):
    return ref[pl.ds(begin * TILE, blocks * TILE), 0, 0:SPAN, :].reshape(blocks * BLOCK, 128)


def each_tile(first_ref, work):
    micro = pl.program_id(0)

    def body(tile, carry):
        needed = tile + 1 - first_ref[micro * TILES + tile]
        for blocks in range(1, TILES + 1):
            pl.when(needed == blocks)(partial(work, tile, blocks))
        return carry

    lax.fori_loop(0, TILES, body, 0)


def fwd_kernel(unit_ref, first_ref, u_ref, start_ref, o_ref, lse_ref):
    part, odd = unit_ref[0], unit_ref[1]

    def work(tile, blocks):
        q_rows = tile_queries(u_ref, tile, SPAN, odd) * jnp.bfloat16(0.125)
        keys = tile_keys(u_ref, tile + 1 - blocks, blocks)
        scores = product_t(q_rows, keys[:, :HD])
        allowed = tile_mask(part, start_ref[0, tile][:, :1], tile, blocks)
        scores = jnp.where(allowed, scores, NEG)
        highest = jnp.max(scores, axis=-1, keepdims=True)
        expo = jnp.exp(scores - highest)
        total = jnp.sum(expo, axis=-1, keepdims=True)
        mixed = product(expo.astype(jnp.bfloat16), keys[:, HD:]) / total
        where = pl.ds(tile * TILE, TILE)
        o_ref[where, 0, :CHUNK, :], o_ref[where, 0, CHUNK:, :] = lay_heads(mixed)
        lse_ref[0, tile] = jnp.broadcast_to(highest + jnp.log(total), (TROWS, 128))

    each_tile(first_ref, work)


def bwd_kernel(unit_ref, first_ref, u_ref, start_ref, do_ref, lse_ref, d_ref, acc):
    part, odd = unit_ref[0], unit_ref[1]
    acc[...] = jnp.zeros_like(acc)

    def work(tile, blocks):
        begin = tile + 1 - blocks
        q_rows = tile_queries(u_ref, tile, SPAN, odd) * jnp.bfloat16(0.125)
        d_rows = tile_queries(do_ref, tile, 0, odd)
        keys = tile_keys(u_ref, begin, blocks)
        scores = product_t(q_rows, keys[:, :HD])
        allowed = tile_mask(part, start_ref[0, tile][:, :1], tile, blocks)
        probs = jnp.where(allowed, jnp.exp(scores - lse_ref[0, tile][:, :1]), 0.0)
        d_probs = product_t(d_rows, keys[:, HD:])
        offset = jnp.sum(d_probs * probs, axis=-1, keepdims=True)
        d_scores = (probs * (d_probs - offset)).astype(jnp.bfloat16)
        d_query = product(d_scores, keys[:, :HD]) * 0.125
        at = pl.ds(tile * TILE, TILE)
        d_ref[at, 0, SPAN : SPAN + CHUNK, :], d_ref[at, 0, SPAN + CHUNK : ALL_ROWS, :] = lay_heads(d_query)
        d_key = t_product(d_scores, q_rows)
        d_value = t_product(probs.astype(jnp.bfloat16), d_rows)
        where = pl.ds(begin * BLOCK, blocks * BLOCK)
        acc[where, :] += jnp.concatenate([d_key, d_value], axis=1)

    each_tile(first_ref, work)
    d_ref[:, 0, 0:SPAN, :] = acc[...].astype(jnp.bfloat16).reshape(SHARDS, SPAN, 128)


SMEM = pl.BlockSpec(memory_space=pltpu.SMEM)
UNIT_SPEC = pl.BlockSpec((SHARDS, 1, ALL_ROWS, 128), lambda m: (0, m, 0, 0))
QUERY_SPEC = pl.BlockSpec((SHARDS, 1, Q_ROWS, 128), lambda m: (0, m, 0, 0))
COL_SPEC = pl.BlockSpec((1, TILES, TROWS, 128), lambda m: (m, 0, 0, 0))
COL_SHAPE = jax.ShapeDtypeStruct((MB, TILES, TROWS, 128), jnp.float32)
PARAMS = pltpu.CompilerParams(vmem_limit_bytes=VMEM_LIMIT)


def split_units(values):
    return values.reshape((HALF_KV, 2, PARTS) + values.shape[1:])


def low_shape(*dims):
    return jax.ShapeDtypeStruct(dims, jnp.bfloat16)


def project(n1, w_qkv, tables):
    shape = low_shape(HALF_KV, 2, PARTS, MB, ALL_ROWS, 128)
    out = pl.pallas_call(project_kernel, out_shape=shape, compiler_params=PARAMS, cost_estimate=cost(6), name="project")(n1, w_qkv, tables)
    return out.reshape(SHARDS, MB, ALL_ROWS, 128)


def whole_spec(*dims):
    return pl.BlockSpec(dims, lambda i: (0,) * len(dims))


OUT_SPEC = pl.BlockSpec((D, D // 2), lambda i: (0, OUT_AT // (D // 2)))


def cost(micros):
    return pl.CostEstimate(flops=int(micros * 1e9), bytes_accessed=1 << 20, transcendentals=0)


def out_project(units, w_all):
    return pl.pallas_call(
        out_kernel,
        grid=(1,),
        in_specs=[whole_spec(HALF_KV, 2, PARTS, MB, Q_ROWS, 128), OUT_SPEC],
        out_specs=[whole_spec(BOTH, HQ), whole_spec(ROWS, D), whole_spec(ROWS, D)],
        out_shape=[low_shape(BOTH, HQ), jax.ShapeDtypeStruct((ROWS, D), jnp.float32), low_shape(ROWS, D)],
        compiler_params=PARAMS,
        cost_estimate=cost(3),
        name="out_project",
    )(split_units(units), w_all)


def d_out_project(da, w_all):
    dims = (HALF_KV, 2, PARTS, MB, Q_ROWS, 128)
    out = pl.pallas_call(
        d_out_kernel,
        grid=(1,),
        in_specs=[whole_spec(BOTH, D), OUT_SPEC],
        out_specs=whole_spec(*dims),
        out_shape=low_shape(*dims),
        compiler_params=PARAMS,
        cost_estimate=cost(3),
        name="d_out_project",
    )(da, w_all)
    return out.reshape(SHARDS, MB, Q_ROWS, 128)


def ffn_kernel(
    n_ref, df_ref, main_ref, rest_ref, gate_ref, up_ref,
    y_mine_ref, y_other_ref, dn_mine_ref, dn_other_ref, grad_ref,
    n_t, y_acc, dn_acc, g_gate, g_up, g_main, g_rest, sems,
):
    step = pl.program_id(0)
    slot = lax.rem(step, 2)

    def copies(at, slot):
        cols, rows = at * FF_TILE, at * FF_ROWS
        return [
            pltpu.make_async_copy(
                g_gate.at[slot], grad_ref.at[:, pl.ds(pl.multiple_of(GATE_AT + cols, FF_TILE), FF_TILE)], sems.at[slot, 0]
            ),
            pltpu.make_async_copy(
                g_up.at[slot], grad_ref.at[:, pl.ds(pl.multiple_of(UP_AT + cols, FF_TILE), FF_TILE)], sems.at[slot, 1]
            ),
            pltpu.make_async_copy(
                g_main.at[slot], grad_ref.at[pl.ds(pl.multiple_of(rows, 64), FF_ROWS), pl.ds(0, D)], sems.at[slot, 2]
            ),
            pltpu.make_async_copy(
                g_rest.at[slot],
                grad_ref.at[pl.ds(pl.multiple_of(rows, 64), FF_ROWS), pl.ds(REST_AT, D // 3)],
                sems.at[slot, 3],
            ),
        ]

    @pl.when(step == 0)
    def _():
        n_t[...] = n_ref[...].T
        y_acc[...] = jnp.zeros_like(y_acc)
        dn_acc[...] = jnp.zeros_like(dn_acc)

    @pl.when(step >= 2)
    def _():
        for copy in copies(step - 2, slot):
            copy.wait()

    low = jnp.bfloat16
    units = []
    for j in range(FF_TILE // UNIT_FF):
        rest = [rest_ref[j * 96 + q * 32 : j * 96 + q * 32 + 32, :] for q in range(3)]
        units += [main_ref[j * 96 : j * 96 + 96, :], jnp.concatenate(rest, axis=1)]
    w_down = jnp.concatenate(units, axis=0)
    rows, df = n_ref[...], df_ref[...]
    gate, up = product(rows, gate_ref[...]), product(rows, up_ref[...])
    sigma = jax.nn.sigmoid(gate)
    silu = gate * sigma
    act = (silu * up).astype(low)
    d_act = product_t(df, w_down)
    d_gate = (d_act * up * sigma * (1.0 + gate * (1.0 - sigma))).astype(low)
    d_up = (d_act * silu).astype(low)
    y_acc[...] += product(act, w_down)
    dn_acc[...] += product_t(d_gate, gate_ref[...]) + product_t(d_up, up_ref[...])
    g_gate[slot] = product(n_t[...], d_gate).astype(low)
    g_up[slot] = product(n_t[...], d_up).astype(low)
    g_down = product(act.T, df).astype(low)
    for j in range(FF_TILE // UNIT_FF):
        g_main[slot, j * 96 : j * 96 + 96, :] = g_down[j * UNIT_FF : j * UNIT_FF + 96]
        for q in range(3):
            g_rest[slot, j * 96 + q * 32 : j * 96 + q * 32 + 32, :] = g_down[
                j * UNIT_FF + 96 : (j + 1) * UNIT_FF, q * (D // 3) : (q + 1) * (D // 3)
            ]
    for copy in copies(step, slot):
        copy.start()

    @pl.when(step == FF_TILES - 1)
    def _():
        y_mine_ref[...] = y_acc[:ROWS]
        y_other_ref[...] = y_acc[ROWS:].astype(low)
        dn_mine_ref[...] = dn_acc[:ROWS]
        dn_other_ref[...] = dn_acc[ROWS:].astype(low)
        for back in (1, 0):
            for copy in copies(step - back, lax.rem(step - back, 2)):
                copy.wait()


def feed_forward(n2, df, w_all):
    wide = jax.ShapeDtypeStruct((ROWS, D), jnp.float32)
    return pl.pallas_call(
        ffn_kernel,
        grid=(FF_TILES,),
        in_specs=[
            whole_spec(BOTH, D),
            whole_spec(BOTH, D),
            pl.BlockSpec((FF_ROWS, D), lambda t: (t, 0)),
            pl.BlockSpec((FF_ROWS, D // 3), lambda t: (t, REST_AT // (D // 3))),
            pl.BlockSpec((D, FF_TILE), lambda t: (0, GATE_AT // FF_TILE + t)),
            pl.BlockSpec((D, FF_TILE), lambda t: (0, UP_AT // FF_TILE + t)),
        ],
        out_specs=[whole_spec(ROWS, D)] * 4 + [pl.BlockSpec(memory_space=pl.ANY)],
        out_shape=[wide, low_shape(ROWS, D), wide, low_shape(ROWS, D), low_shape(D, OUT_AT)],
        scratch_shapes=[
            pltpu.VMEM((D, BOTH), jnp.bfloat16),
            pltpu.VMEM((BOTH, D), jnp.float32),
            pltpu.VMEM((BOTH, D), jnp.float32),
            pltpu.VMEM((2, D, FF_TILE), jnp.bfloat16),
            pltpu.VMEM((2, D, FF_TILE), jnp.bfloat16),
            pltpu.VMEM((2, FF_ROWS, D), jnp.bfloat16),
            pltpu.VMEM((2, FF_ROWS, D // 3), jnp.bfloat16),
            pltpu.SemaphoreType.DMA((2, 4)),
        ],
        compiler_params=PARAMS,
        cost_estimate=cost(30),
        name="feed_forward",
    )(n2, df, w_all, w_all, w_all, w_all)


def collect(units, tables):
    shape = low_shape(BOTH, HQ + 2 * HK)
    return pl.pallas_call(collect_kernel, out_shape=shape, compiler_params=PARAMS, cost_estimate=cost(4), name="collect")(
        split_units(units), tables
    )


def gradients(n1, d_qkv, gains):
    return pl.pallas_call(
        gradient_kernel,
        out_shape=low_shape(D, QKV + 128),
        compiler_params=PARAMS,
        cost_estimate=cost(5),
        name="gradients",
    )(n1, d_qkv, gains)


def attend_fwd(unit, first, units, starts):
    return pl.pallas_call(
        fwd_kernel,
        grid=(MB,),
        in_specs=[SMEM, SMEM, UNIT_SPEC, COL_SPEC],
        out_specs=[QUERY_SPEC, COL_SPEC],
        out_shape=[low_shape(SHARDS, MB, Q_ROWS, 128), COL_SHAPE],
        compiler_params=PARAMS,
        cost_estimate=cost(20),
        name="attend_forward",
    )(unit, first, units, starts)


def attend_bwd(unit, first, units, starts, d_mixed, lse):
    return pl.pallas_call(
        bwd_kernel,
        grid=(MB,),
        in_specs=[SMEM, SMEM, UNIT_SPEC, COL_SPEC, QUERY_SPEC, COL_SPEC],
        out_specs=UNIT_SPEC,
        out_shape=low_shape(SHARDS, MB, ALL_ROWS, 128),
        scratch_shapes=[pltpu.VMEM((SEQ, 128), jnp.float32)],
        compiler_params=PARAMS,
        cost_estimate=cost(40),
        name="attend_backward",
    )(unit, first, units, starts, d_mixed, lse)


def piece_perm():
    return [(k * SHARDS + s, (s // 16) * SHARDS + 2 * (s % 16) + k) for k in range(2) for s in range(SHARDS)]


def shift(values, axis, step):
    if axis == "x":
        line = lambda x: (x % 2) * 2 + x // 2
        return lax.ppermute(values, ("xl", "xh"), [(line(i), line((i + step) % 4)) for i in range(4)])
    return lax.ppermute(values, axis, [(i, (i + step) % 4) for i in range(4)])


def place(axis):
    if axis == "x":
        return lax.axis_index("xh") * 2 + lax.axis_index("xl")
    return lax.axis_index(axis)


def flip(values, axis):
    return lax.ppermute(values, axis, [(0, 1), (1, 0)])


def col_half(core, local):
    half = local.shape[1] // 2
    return lax.dynamic_slice_in_dim(local, core * half, half, axis=1)


def pad_units(local):
    return jnp.pad(local.reshape(-1, 16, 120), ((0, 0), (0, 0), (0, UNIT_FF - 120))).reshape(-1, PAD_FF)


def crop_units(local):
    return local.reshape(-1, 16, UNIT_FF)[:, :, :120].reshape(-1, HF)


def fold(rows, parts):
    n, r, w = rows.shape
    return rows.reshape(n, r, parts, w // parts).transpose(0, 2, 1, 3).reshape(n, parts * r, w // parts)


def unfold(rows, parts):
    n, r, w = rows.shape
    return rows.reshape(n, parts, r // parts, w).transpose(0, 2, 1, 3).reshape(n, r // parts, parts * w)


def wide_sum(*values):
    total = values[0].astype(jnp.float32)
    for value in values[1:]:
        total = total + value.astype(jnp.float32)
    return total.astype(jnp.bfloat16)


def after(values, event):
    return lax.optimization_barrier((values, event))[0]


def total_axis(values, axis):
    return values + shift(values, axis, 1) + shift(values, axis, 2) + shift(values, axis, 3)


def reduce_x(values, dim):
    size = values.shape[dim] // 2
    me = lax.axis_index("xh")
    keep = lax.dynamic_slice_in_dim(values, me * size, size, axis=dim)
    send = lax.dynamic_slice_in_dim(values, (1 - me) * size, size, axis=dim)
    cross = lax.ppermute(send, ("xl", "xh"), [(i, 3 - i) for i in range(4)])
    return wide_sum(keep, flip(keep, "xl"), flip(send, "xh"), cross)


def add_pair(values, axis):
    return wide_sum(values, flip(values, axis))


def join_pair(mine, axis, dim):
    other = flip(mine, axis)
    lower = lax.axis_index(axis) == 0
    return jnp.concatenate([jnp.where(lower, mine, other), jnp.where(lower, other, mine)], axis=dim)


def join_cores(mine):
    return join_pair(mine, "c", 1).astype(jnp.float32)


def scatter_sum(values):
    return jnp.sum(exchange(values).astype(jnp.float32), axis=0).astype(jnp.bfloat16)


def on_device(
    hidden_in,
    doc_ids,
    out_grad,
    norm_attn,
    w_query,
    w_key,
    w_value,
    w_out,
    norm_ffn,
    w_gate,
    w_up,
    w_down,
):
    core = lax.axis_index("c")
    shard = lax.axis_index(SHARD)
    low = jnp.bfloat16

    rows_in = lax.ppermute(jnp.concatenate([w_out, w_down], axis=0), ("c",) + SHARD, piece_perm())
    gu_piece = jnp.concatenate([pad_units(col_half(core, w_gate)), pad_units(col_half(core, w_up))], axis=1)
    w_all = lax.all_gather(
        jnp.concatenate(
            [
                rows_in[48:144],
                fold(jnp.pad(rows_in[144:], ((0, 8), (0, 0)))[None], 3)[0],
                join_pair(gu_piece, "xh", 0),
                fold(rows_in[:48][None], 2)[0],
            ],
            axis=1,
        ),
        ("z", "y"),
        axis=0,
        tiled=True,
    )
    small = jnp.concatenate(
        [norm_attn[:, None], norm_ffn[:, None], doc_ids.reshape(48, 4).astype(low), jnp.zeros((48, 122), low)], axis=1
    )
    piece = jnp.concatenate(
        [to_groups(col_half(core, w_query)), interleave(col_half(core, w_key), col_half(core, w_value)), small], axis=1
    )
    w_first = exchange(jnp.broadcast_to(piece[None], (SHARDS, 48, QKV + 128)))
    small = w_first[:, :, QKV : QKV + 6]
    w_first = w_first.reshape(D, QKV + 128)
    w_qkv = w_first[:, :QKV]
    gain_attn = small[:, :, 0].reshape(1, D).astype(jnp.float32)
    gain_ffn = small[:, :, 1].reshape(1, D).astype(jnp.float32)
    docs_mine = small[:, :, 2:].reshape(SHARDS, MB, SPAN).transpose(1, 0, 2).reshape(MB, SEQ)
    docs_other = swap(docs_mine)

    x_low = hidden_in.reshape(ROWS, D)
    x = x_low.astype(jnp.float32)
    x_both = jnp.concatenate([x_low, swap(x_low)], axis=0).astype(jnp.float32)
    dy_low = out_grad.reshape(ROWS, D)
    dy = dy_low.astype(jnp.float32)
    df = (branch_scale * jnp.concatenate([dy_low, swap(dy_low)], axis=0).astype(jnp.float32)).astype(low)

    which = lax.rem(shard // PARTS, 2)
    part = lax.rem(shard, PARTS)
    docs = jnp.where(which == 0, docs_mine, docs_other).astype(jnp.float32)
    counted = jnp.sum((docs[:, None, :] < docs[:, :, None]).astype(jnp.int32), axis=-1)
    q_start = lax.dynamic_slice_in_dim(counted.reshape(MB, SHARDS, SPAN), part * CHUNK, CHUNK, axis=2)
    q_start = q_start.reshape(MB, TILES, 1, TILE * CHUNK)
    first = (q_start[:, :, 0, 0] // BLOCK).reshape(-1)
    starts = jnp.broadcast_to(q_start, (MB, TILES, GROUP, TILE * CHUNK)).reshape(MB, TILES, TROWS, 1)
    starts = jnp.broadcast_to(starts, (MB, TILES, TROWS, 128))
    unit = jnp.stack([part, lax.rem(shard // (2 * PARTS), 2)]).astype(jnp.int32)

    places = (shard * SPAN + jnp.arange(SPAN, dtype=jnp.int32)).astype(jnp.float32)
    half_size = HD // 2
    inverse = jnp.exp(-jnp.arange(half_size, dtype=jnp.float32) * (math.log(10000.0) / half_size))
    angles = places[:, None] * inverse[None, :]
    cosine, sine = jnp.cos(angles), jnp.sin(angles)
    cosine = jnp.concatenate([cosine, cosine], axis=1)
    sine = jnp.concatenate([-sine, sine], axis=1)
    tables = jnp.stack(
        [
            jnp.concatenate([cosine, cosine], axis=1),
            jnp.concatenate([sine, sine], axis=1),
            jnp.concatenate([cosine, jnp.ones_like(cosine)], axis=1),
            jnp.concatenate([sine, jnp.zeros_like(sine)], axis=1),
        ]
    )

    r1_both = lax.rsqrt(jnp.mean(x_both * x_both, axis=-1, keepdims=True) + eps_norm)
    r1 = r1_both[:ROWS]
    n1 = (x_both * r1_both * gain_attn).astype(low)
    units = exchange(project(n1, w_first, tables))
    unit_o, lse = attend_fwd(unit, first, units, starts)
    attn, y1_mine, y1_other = out_project(exchange(unit_o), w_all)
    hmid = x + branch_scale * (y1_mine + swap(y1_other).astype(jnp.float32))

    r2 = lax.rsqrt(jnp.mean(hmid * hmid, axis=-1, keepdims=True) + eps_norm)
    z2 = hmid * r2
    n2_mine = (z2 * gain_ffn).astype(low)
    n2 = jnp.concatenate([n2_mine, swap(n2_mine)], axis=0)
    y2_mine, y2_other, dn2_mine, dn2_other, g_ffn = feed_forward(n2, df, w_all)
    result = hmid + branch_scale * (y2_mine + swap(y2_other).astype(jnp.float32))

    s_ffn = lax.psum_scatter(g_ffn, ("z", "y"), scatter_dimension=0, tiled=True)
    dn2 = dn2_mine + swap(dn2_other).astype(jnp.float32)
    e2 = dn2 * gain_ffn
    g_gain_ffn = jnp.sum(dn2 * z2, axis=0)
    dh = dy + r2 * (e2 - z2 * jnp.mean(e2 * z2, axis=-1, keepdims=True))

    da_mine = (branch_scale * dh).astype(low)
    da = jnp.concatenate([da_mine, swap(da_mine)], axis=0)
    unit_do = exchange(d_out_project(da, w_all))
    g_o = [t_product(attn, da[:, k * (D // 2) : (k + 1) * (D // 2)]).astype(low) for k in range(2)]
    g_o = jnp.stack([g.reshape(16, 48, D // 2) for g in g_o], axis=1).reshape(SHARDS, 48, D // 2)
    s_o = scatter_sum(after(g_o, unit_do))
    unit_d = attend_bwd(unit, first, units, starts, unit_do, lse)
    d_qkv = collect(exchange(after(unit_d, s_o)), tables)
    s_o = add_pair(s_o, "xl")

    dn1_both = product_t(d_qkv, w_qkv)
    dn1 = dn1_both[:ROWS] + swap(dn1_both[ROWS:].astype(low)).astype(jnp.float32)
    z1 = x * r1
    e1 = dn1 * gain_attn
    g_gain_attn = jnp.sum(dn1 * z1, axis=0)
    grad_in = (dh + r1 * (e1 - z1 * jnp.mean(e1 * z1, axis=-1, keepdims=True))).astype(low)

    gains = jnp.concatenate([g_gain_attn[None], g_gain_ffn[None], jnp.zeros((6, D), jnp.float32)], axis=0)
    g_qkv = gradients(n1, d_qkv, gains)
    received = exchange(g_qkv.reshape(SHARDS, 48, QKV + 128))
    s_ffn = after(s_ffn, d_qkv)
    s_d = jnp.concatenate([s_ffn[:, :D], unfold(s_ffn[None, :, REST_AT:GATE_AT], 3)[0][:24]], axis=0)
    rows_x = jnp.concatenate([s_o, reduce_x(s_d, 1)], axis=0)
    rows = join_cores(lax.ppermute(rows_x, ("c",) + SHARD, [(b, a) for a, b in piece_perm()]))
    s_gu = reduce_x(s_ffn[:, GATE_AT:], 0)
    received = after(received, (s_gu, rows_x))
    s_gu = jnp.concatenate([crop_units(s_gu[:, :PAD_FF]), crop_units(s_gu[:, PAD_FF:])], axis=1)
    other = swap(s_gu)
    lower = core == 0
    g_g, g_u = [
        jnp.concatenate([jnp.where(lower, m, t), jnp.where(lower, t, m)], axis=1).astype(jnp.float32)
        for m, t in ((s_gu[:, :HF], other[:, :HF]), (s_gu[:, HF:], other[:, HF:]))
    ]
    s_qkv = add_pair(jnp.sum(received.astype(jnp.float32), axis=0).astype(low), "xl")
    other = swap(s_qkv)
    whole = [jnp.where(lower, s_qkv, other), jnp.where(lower, other, s_qkv)]
    gains = s_qkv[:, QKV : QKV + 2].astype(jnp.float32) + other[:, QKV : QKV + 2].astype(jnp.float32)

    def heads_of(offset):
        return jnp.concatenate(
            [w[:, HQ + 128 * j + offset : HQ + 128 * j + offset + HD] for w in whole for j in range(HALF_KV)], axis=1
        ).astype(jnp.float32)

    return (
        result.reshape(1, MB, SPAN, D).astype(low),
        grad_in.reshape(1, MB, SPAN, D),
        gains[:, 0],
        jnp.concatenate([from_groups(w[:, :HQ]) for w in whole], axis=1).astype(jnp.float32),
        heads_of(0),
        heads_of(HD),
        rows[:48],
        gains[:, 1],
        g_g,
        g_u,
        rows[48:],
    )


def solution(mesh):
    fine = Mesh(mesh.devices.reshape(2, 2, 4, 4, 2), ("xl", "c", "z", "y", "xh"))
    replica = ("xl", "c")
    tokens = P(replica, None, SHARD, None)
    matrix = P(SHARD, None)
    vector = P(SHARD)
    return jax.shard_map(
        on_device,
        mesh=fine,
        in_specs=(
            tokens,
            P(replica, None, SHARD),
            tokens,
            vector,
            matrix,
            matrix,
            matrix,
            matrix,
            vector,
            matrix,
            matrix,
            matrix,
        ),
        out_specs=(
            tokens,
            tokens,
            vector,
            matrix,
            matrix,
            matrix,
            matrix,
            vector,
            matrix,
            matrix,
            matrix,
        ),
        check_vma=False,
    )
```

```python
from functools import partial
import math

import jax
import jax.numpy as jnp
from jax import lax
from jax.experimental import pallas as pl
from jax.experimental.pallas import tpu as pltpu
from jax.sharding import Mesh
from jax.sharding import PartitionSpec as P

HEADS = 24
KVH = 8
HD = 64
D = 1536
FF = 3840
MB = 3
SPAN = 64
SHARDS = 32
SEQ = 2048
PARTS = 4
ROWS = MB * SPAN
BOTH = 2 * ROWS
GROUP = HEADS // KVH
HALF_KV = KVH // 2
HQ = HALF_KV * GROUP * HD
HK = HALF_KV * HD
HF = FF // 2
QKV = HQ + 2 * HK
UNIT_FF = 128
PAD_FF = 16 * UNIT_FF
REST_AT = D
GATE_AT = D + D // 3
UP_AT = GATE_AT + PAD_FF
OUT_AT = UP_AT + PAD_FF
FF_TILE = 256
FF_TILES = PAD_FF // FF_TILE
FF_ROWS = 96 * FF_TILE // UNIT_FF
CHUNK = SPAN // PARTS
TILE = 4
TILES = SHARDS // TILE
BLOCK = TILE * SPAN
TROWS = GROUP * TILE * CHUNK

SHARD = ("z", "y", "xh")
branch_scale = 1.4 / math.sqrt(52.0)
eps_norm = 1e-05
NEG = -1e30
VMEM_LIMIT = 48 * 1024 * 1024


def product(left, right):
    return jnp.dot(left, right, preferred_element_type=jnp.float32)


def product_t(left, right):
    return lax.dot_general(left, right, (((1,), (1,)), ((), ())), preferred_element_type=jnp.float32)


def t_product(left, right):
    return lax.dot_general(left, right, (((0,), (0,)), ((), ())), preferred_element_type=jnp.float32)


def swap(values):
    return lax.ppermute(values, "c", [(0, 1), (1, 0)])


def exchange(values):
    return lax.all_to_all(values, SHARD, 0, 0, tiled=True)


Q_ROWS = 2 * CHUNK
ALL_ROWS = SPAN + Q_ROWS


def to_groups(rows):
    parts = [rows[:, 192 * j : 192 * j + 128] for j in range(HALF_KV)]
    parts += [rows[:, 192 * j + 128 : 192 * j + 192] for j in range(HALF_KV)]
    return jnp.concatenate(parts, axis=1)


def from_groups(rows):
    parts = []
    for j in range(HALF_KV):
        parts += [rows[:, 128 * j : 128 * j + 128], rows[:, 512 + 64 * j : 576 + 64 * j]]
    return jnp.concatenate(parts, axis=1)


def interleave(keys, values):
    parts = []
    for j in range(HALF_KV):
        parts += [keys[:, HD * j : HD * j + HD], values[:, HD * j : HD * j + HD]]
    return jnp.concatenate(parts, axis=1)


def turn(values, cosine, sine):
    lane = lax.broadcasted_iota(jnp.int32, values.shape, values.ndim - 1)
    axis = values.ndim - 1
    other = jnp.where(lane % HD < HD // 2, pltpu.roll(values, 128 - HD // 2, axis), pltpu.roll(values, HD // 2, axis))
    return values * cosine + other * sine


def project_kernel(n_ref, w_ref, table_ref, out_ref):
    rows = n_ref[...]

    def group(g, table):
        wide = product(rows, w_ref[:, 128 * g : 128 * g + 128]).reshape(2 * MB, SPAN, 128)
        return turn(wide, table_ref[table][None], table_ref[table + 1][None]).astype(jnp.bfloat16)

    for j in range(HALF_KV):
        first, both = group(j, 0), group(6 + j, 2)
        if j % 2 == 0:
            third = group(4 + j // 2, 0)
        for o in range(2):
            for m in range(MB):
                for p in range(PARTS):
                    cut = slice(p * CHUNK, (p + 1) * CHUNK)
                    out_ref[j, o, p, m, 0:SPAN, :] = both[o * MB + m]
                    out_ref[j, o, p, m, SPAN : SPAN + CHUNK, :] = first[o * MB + m, cut]
                    out_ref[j, o, p, m, SPAN + CHUNK : ALL_ROWS, :] = third[o * MB + m, cut]


def third_head(pair_even, pair_odd):
    lane = lax.broadcasted_iota(jnp.int32, pair_even.shape, pair_even.ndim - 1)
    return jnp.where(lane < HD, pair_even, pair_odd)


def out_halves(ref):
    whole = ref[...].reshape(16, 2, 48, D // 2)
    return whole[:, 0].reshape(HQ, D // 2), whole[:, 1].reshape(HQ, D // 2)


def out_kernel(u_ref, w_ref, attn_ref, mine_ref, other_ref):
    for o in range(2):
        for m in range(MB):
            for p in range(PARTS):
                thirds = [
                    third_head(u_ref[2 * k, o, p, m, CHUNK:, :], u_ref[2 * k + 1, o, p, m, CHUNK:, :])
                    for k in range(2)
                ]
                parts = []
                for j in range(HALF_KV):
                    parts += [u_ref[j, o, p, m, :CHUNK, :], thirds[j // 2][:, HD * (j % 2) : HD * (j % 2) + HD]]
                at = (o * MB + m) * SPAN + p * CHUNK
                attn_ref[at : at + CHUNK, :] = jnp.concatenate(parts, axis=1)
    attn = attn_ref[...]
    for k, half in enumerate(out_halves(w_ref)):
        result = product(attn, half)
        cols = slice(k * (D // 2), (k + 1) * (D // 2))
        mine_ref[:, cols] = result[:ROWS]
        other_ref[:, cols] = result[ROWS:].astype(jnp.bfloat16)


def d_out_kernel(da_ref, w_ref, attn_ref, held_ref, out_ref, grad_ref, g_out, sem):
    attn_t = attn_ref[...].T
    for k in range(2):
        half = product(attn_t, da_ref[:, k * (D // 2) : (k + 1) * (D // 2)]).astype(jnp.bfloat16)
        for j in range(16):
            g_out[j * 96 + k * 48 : j * 96 + k * 48 + 48, :] = half[j * 48 : j * 48 + 48]
    copy = pltpu.make_async_copy(g_out, grad_ref.at[:, pl.ds(OUT_AT, D // 2)], sem)
    copy.start()
    left, right = out_halves(w_ref)
    rows = product_t(da_ref[:, : D // 2], left) + product_t(da_ref[:, D // 2 :], right)
    rows = rows.astype(jnp.bfloat16)
    for j in range(HALF_KV):
        first = rows[:, 192 * j : 192 * j + 128]
        if j % 2 == 0:
            third = jnp.concatenate([rows[:, 192 * j + 128 : 192 * j + 192], rows[:, 192 * j + 320 : 192 * j + 384]], axis=1)
        for o in range(2):
            for m in range(MB):
                for p in range(PARTS):
                    at = (o * MB + m) * SPAN + p * CHUNK
                    out_ref[j, o, p, m, :CHUNK, :] = first[at : at + CHUNK]
                    out_ref[j, o, p, m, CHUNK:, :] = third[at : at + CHUNK]
    copy.wait()


def collect_kernel(u_ref, table_ref, out_ref):
    def put(g, o, m, at, size, values, table, row):
        cosine = table_ref[table, row : row + size]
        sine = table_ref[table + 1, row : row + size]
        out_ref[at : at + size, 128 * g : 128 * g + 128] = turn(values, cosine, -sine).astype(jnp.bfloat16)

    wide = jnp.float32
    for o in range(2):
        for m in range(MB):
            base = (o * MB + m) * SPAN
            for j in range(HALF_KV):
                total = u_ref[j, o, 0, m, 0:SPAN, :].astype(wide)
                for p in range(1, PARTS):
                    total = total + u_ref[j, o, p, m, 0:SPAN, :].astype(wide)
                put(6 + j, o, m, base, SPAN, total, 2, 0)
            for p in range(PARTS):
                at = base + p * CHUNK
                for j in range(HALF_KV):
                    first = u_ref[j, o, p, m, SPAN : SPAN + CHUNK, :].astype(wide)
                    put(j, o, m, at, CHUNK, first, 0, p * CHUNK)
                for k in range(2):
                    third = third_head(
                        u_ref[2 * k, o, p, m, SPAN + CHUNK : ALL_ROWS, :].astype(wide),
                        u_ref[2 * k + 1, o, p, m, SPAN + CHUNK : ALL_ROWS, :].astype(wide),
                    )
                    put(4 + k, o, m, at, CHUNK, third, 0, p * CHUNK)


def gradient_kernel(n_ref, d_ref, gains_ref, out_ref):
    out_ref[:, :QKV] = product(n_ref[...].T, d_ref[...]).astype(jnp.bfloat16)
    gains = jnp.concatenate([gains_ref[...], jnp.zeros((120, D), jnp.float32)], axis=0)
    out_ref[:, QKV:] = gains.T.astype(jnp.bfloat16)


def stack_heads(first, third, odd):
    last = jnp.where(odd == 1, third[:, HD:], third[:, :HD])
    return jnp.concatenate([first[:, :HD], first[:, HD:], last], axis=0)


def lay_heads(rows):
    size = TILE * CHUNK
    parts = [rows[g * size : (g + 1) * size] for g in range(GROUP)]
    shape = (TILE, CHUNK, 128)
    return (
        jnp.concatenate(parts[:2], axis=1).astype(jnp.bfloat16).reshape(shape),
        jnp.concatenate([parts[2], parts[2]], axis=1).astype(jnp.bfloat16).reshape(shape),
    )


def tile_mask(part, start_rows, tile, blocks):
    wide = blocks * BLOCK
    row = lax.broadcasted_iota(jnp.int32, (TROWS, 1), 0)
    inside = lax.rem(row, TILE * CHUNK)
    q_pos = tile * BLOCK + (inside // CHUNK) * SPAN + part * CHUNK + lax.rem(inside, CHUNK)
    k_pos = (tile + 1 - blocks) * BLOCK + lax.broadcasted_iota(jnp.int32, (TROWS, wide), 1)
    return (k_pos >= start_rows) & (k_pos <= q_pos)


def tile_queries(ref, tile, begin, odd):
    where = pl.ds(tile * TILE, TILE)
    first = ref[where, 0, begin : begin + CHUNK, :].reshape(TILE * CHUNK, 128)
    third = ref[where, 0, begin + CHUNK : begin + 2 * CHUNK, :].reshape(TILE * CHUNK, 128)
    return stack_heads(first, third, odd)


def tile_keys(ref, begin, blocks):
    return ref[pl.ds(begin * TILE, blocks * TILE), 0, 0:SPAN, :].reshape(blocks * BLOCK, 128)


def each_tile(first_ref, work):
    micro = pl.program_id(0)

    def body(tile, carry):
        needed = tile + 1 - first_ref[micro * TILES + tile]
        for blocks in range(1, TILES + 1):
            pl.when(needed == blocks)(partial(work, tile, blocks))
        return carry

    lax.fori_loop(0, TILES, body, 0)


def fwd_kernel(unit_ref, first_ref, u_ref, start_ref, o_ref, lse_ref):
    part, odd = unit_ref[0], unit_ref[1]

    def work(tile, blocks):
        q_rows = tile_queries(u_ref, tile, SPAN, odd) * jnp.bfloat16(0.125)
        keys = tile_keys(u_ref, tile + 1 - blocks, blocks)
        scores = product_t(q_rows, keys[:, :HD])
        allowed = tile_mask(part, start_ref[0, tile][:, :1], tile, blocks)
        scores = jnp.where(allowed, scores, NEG)
        highest = jnp.max(scores, axis=-1, keepdims=True)
        expo = jnp.exp(scores - highest)
        total = jnp.sum(expo, axis=-1, keepdims=True)
        mixed = product(expo.astype(jnp.bfloat16), keys[:, HD:]) / total
        where = pl.ds(tile * TILE, TILE)
        o_ref[where, 0, :CHUNK, :], o_ref[where, 0, CHUNK:, :] = lay_heads(mixed)
        lse_ref[0, tile] = jnp.broadcast_to(highest + jnp.log(total), (TROWS, 128))

    each_tile(first_ref, work)


def bwd_kernel(unit_ref, first_ref, u_ref, start_ref, do_ref, lse_ref, d_ref, acc):
    part, odd = unit_ref[0], unit_ref[1]
    acc[...] = jnp.zeros_like(acc)

    def work(tile, blocks):
        begin = tile + 1 - blocks
        q_rows = tile_queries(u_ref, tile, SPAN, odd) * jnp.bfloat16(0.125)
        d_rows = tile_queries(do_ref, tile, 0, odd)
        keys = tile_keys(u_ref, begin, blocks)
        scores = product_t(q_rows, keys[:, :HD])
        allowed = tile_mask(part, start_ref[0, tile][:, :1], tile, blocks)
        probs = jnp.where(allowed, jnp.exp(scores - lse_ref[0, tile][:, :1]), 0.0)
        d_probs = product_t(d_rows, keys[:, HD:])
        offset = jnp.sum(d_probs * probs, axis=-1, keepdims=True)
        d_scores = (probs * (d_probs - offset)).astype(jnp.bfloat16)
        d_query = product(d_scores, keys[:, :HD]) * 0.125
        at = pl.ds(tile * TILE, TILE)
        d_ref[at, 0, SPAN : SPAN + CHUNK, :], d_ref[at, 0, SPAN + CHUNK : ALL_ROWS, :] = lay_heads(d_query)
        d_key = t_product(d_scores, q_rows)
        d_value = t_product(probs.astype(jnp.bfloat16), d_rows)
        where = pl.ds(begin * BLOCK, blocks * BLOCK)
        acc[where, :] += jnp.concatenate([d_key, d_value], axis=1)

    each_tile(first_ref, work)
    d_ref[:, 0, 0:SPAN, :] = acc[...].astype(jnp.bfloat16).reshape(SHARDS, SPAN, 128)


SMEM = pl.BlockSpec(memory_space=pltpu.SMEM)
UNIT_SPEC = pl.BlockSpec((SHARDS, 1, ALL_ROWS, 128), lambda m: (0, m, 0, 0))
QUERY_SPEC = pl.BlockSpec((SHARDS, 1, Q_ROWS, 128), lambda m: (0, m, 0, 0))
COL_SPEC = pl.BlockSpec((1, TILES, TROWS, 128), lambda m: (m, 0, 0, 0))
COL_SHAPE = jax.ShapeDtypeStruct((MB, TILES, TROWS, 128), jnp.float32)
PARAMS = pltpu.CompilerParams(vmem_limit_bytes=VMEM_LIMIT)


def split_units(values):
    return values.reshape((HALF_KV, 2, PARTS) + values.shape[1:])


def low_shape(*dims):
    return jax.ShapeDtypeStruct(dims, jnp.bfloat16)


def project(n1, w_qkv, tables):
    shape = low_shape(HALF_KV, 2, PARTS, MB, ALL_ROWS, 128)
    out = pl.pallas_call(project_kernel, out_shape=shape, compiler_params=PARAMS, cost_estimate=cost(6), name="project")(n1, w_qkv, tables)
    return out.reshape(SHARDS, MB, ALL_ROWS, 128)


def whole_spec(*dims):
    return pl.BlockSpec(dims, lambda i: (0,) * len(dims))


OUT_SPEC = pl.BlockSpec((D, D // 2), lambda i: (0, OUT_AT // (D // 2)))


def cost(micros):
    return pl.CostEstimate(flops=int(micros * 1e9), bytes_accessed=1 << 20, transcendentals=0)


def out_project(units, w_all):
    return pl.pallas_call(
        out_kernel,
        grid=(1,),
        in_specs=[whole_spec(HALF_KV, 2, PARTS, MB, Q_ROWS, 128), OUT_SPEC],
        out_specs=[whole_spec(BOTH, HQ), whole_spec(ROWS, D), whole_spec(ROWS, D)],
        out_shape=[low_shape(BOTH, HQ), jax.ShapeDtypeStruct((ROWS, D), jnp.float32), low_shape(ROWS, D)],
        compiler_params=PARAMS,
        cost_estimate=cost(3),
        name="out_project",
    )(split_units(units), w_all)


def d_out_project(da, w_all, attn, g_ffn):
    dims = (HALF_KV, 2, PARTS, MB, Q_ROWS, 128)
    anywhere = pl.BlockSpec(memory_space=pl.ANY)
    out, grads = pl.pallas_call(
        d_out_kernel,
        grid=(1,),
        in_specs=[whole_spec(BOTH, D), OUT_SPEC, whole_spec(BOTH, HQ), anywhere],
        out_specs=[whole_spec(*dims), anywhere],
        out_shape=[low_shape(*dims), low_shape(*g_ffn.shape)],
        scratch_shapes=[pltpu.VMEM((D, D // 2), jnp.bfloat16), pltpu.SemaphoreType.DMA],
        input_output_aliases={3: 1},
        compiler_params=PARAMS,
        cost_estimate=cost(5),
        name="d_out_project",
    )(da, w_all, attn, g_ffn)
    return out.reshape(SHARDS, MB, Q_ROWS, 128), grads


def ffn_kernel(
    n_ref, df_ref, main_ref, rest_ref, gate_ref, up_ref,
    y_mine_ref, y_other_ref, dn_mine_ref, dn_other_ref, grad_ref,
    n_t, y_acc, dn_acc, g_gate, g_up, g_main, g_rest, sems,
):
    step = pl.program_id(0)
    slot = lax.rem(step, 2)

    def copies(at, slot):
        cols, rows = at * FF_TILE, at * FF_ROWS
        return [
            pltpu.make_async_copy(
                g_gate.at[slot], grad_ref.at[:, pl.ds(pl.multiple_of(GATE_AT + cols, FF_TILE), FF_TILE)], sems.at[slot, 0]
            ),
            pltpu.make_async_copy(
                g_up.at[slot], grad_ref.at[:, pl.ds(pl.multiple_of(UP_AT + cols, FF_TILE), FF_TILE)], sems.at[slot, 1]
            ),
            pltpu.make_async_copy(
                g_main.at[slot], grad_ref.at[pl.ds(pl.multiple_of(rows, 64), FF_ROWS), pl.ds(0, D)], sems.at[slot, 2]
            ),
            pltpu.make_async_copy(
                g_rest.at[slot],
                grad_ref.at[pl.ds(pl.multiple_of(rows, 64), FF_ROWS), pl.ds(REST_AT, D // 3)],
                sems.at[slot, 3],
            ),
        ]

    @pl.when(step == 0)
    def _():
        n_t[...] = n_ref[...].T
        y_acc[...] = jnp.zeros_like(y_acc)
        dn_acc[...] = jnp.zeros_like(dn_acc)

    @pl.when(step >= 2)
    def _():
        for copy in copies(step - 2, slot):
            copy.wait()

    low = jnp.bfloat16
    units = []
    for j in range(FF_TILE // UNIT_FF):
        rest = [rest_ref[j * 96 + q * 32 : j * 96 + q * 32 + 32, :] for q in range(3)]
        units += [main_ref[j * 96 : j * 96 + 96, :], jnp.concatenate(rest, axis=1)]
    w_down = jnp.concatenate(units, axis=0)
    rows, df = n_ref[...], df_ref[...]
    gate, up = product(rows, gate_ref[...]), product(rows, up_ref[...])
    sigma = jax.nn.sigmoid(gate)
    silu = gate * sigma
    act = (silu * up).astype(low)
    d_act = product_t(df, w_down)
    d_gate = (d_act * up * sigma * (1.0 + gate * (1.0 - sigma))).astype(low)
    d_up = (d_act * silu).astype(low)
    y_acc[...] += product(act, w_down)
    dn_acc[...] += product_t(d_gate, gate_ref[...]) + product_t(d_up, up_ref[...])
    g_gate[slot] = product(n_t[...], d_gate).astype(low)
    g_up[slot] = product(n_t[...], d_up).astype(low)
    g_down = product(act.T, df).astype(low)
    for j in range(FF_TILE // UNIT_FF):
        g_main[slot, j * 96 : j * 96 + 96, :] = g_down[j * UNIT_FF : j * UNIT_FF + 96]
        for q in range(3):
            g_rest[slot, j * 96 + q * 32 : j * 96 + q * 32 + 32, :] = g_down[
                j * UNIT_FF + 96 : (j + 1) * UNIT_FF, q * (D // 3) : (q + 1) * (D // 3)
            ]
    for copy in copies(step, slot):
        copy.start()

    @pl.when(step == FF_TILES - 1)
    def _():
        y_mine_ref[...] = y_acc[:ROWS]
        y_other_ref[...] = y_acc[ROWS:].astype(low)
        dn_mine_ref[...] = dn_acc[:ROWS]
        dn_other_ref[...] = dn_acc[ROWS:].astype(low)
        for back in (1, 0):
            for copy in copies(step - back, lax.rem(step - back, 2)):
                copy.wait()


def feed_forward(n2, df, w_all):
    wide = jax.ShapeDtypeStruct((ROWS, D), jnp.float32)
    return pl.pallas_call(
        ffn_kernel,
        grid=(FF_TILES,),
        in_specs=[
            whole_spec(BOTH, D),
            whole_spec(BOTH, D),
            pl.BlockSpec((FF_ROWS, D), lambda t: (t, 0)),
            pl.BlockSpec((FF_ROWS, D // 3), lambda t: (t, REST_AT // (D // 3))),
            pl.BlockSpec((D, FF_TILE), lambda t: (0, GATE_AT // FF_TILE + t)),
            pl.BlockSpec((D, FF_TILE), lambda t: (0, UP_AT // FF_TILE + t)),
        ],
        out_specs=[whole_spec(ROWS, D)] * 4 + [pl.BlockSpec(memory_space=pl.ANY)],
        out_shape=[wide, low_shape(ROWS, D), wide, low_shape(ROWS, D), low_shape(D, OUT_AT + D // 2)],
        scratch_shapes=[
            pltpu.VMEM((D, BOTH), jnp.bfloat16),
            pltpu.VMEM((BOTH, D), jnp.float32),
            pltpu.VMEM((BOTH, D), jnp.float32),
            pltpu.VMEM((2, D, FF_TILE), jnp.bfloat16),
            pltpu.VMEM((2, D, FF_TILE), jnp.bfloat16),
            pltpu.VMEM((2, FF_ROWS, D), jnp.bfloat16),
            pltpu.VMEM((2, FF_ROWS, D // 3), jnp.bfloat16),
            pltpu.SemaphoreType.DMA((2, 4)),
        ],
        compiler_params=PARAMS,
        cost_estimate=cost(30),
        name="feed_forward",
    )(n2, df, w_all, w_all, w_all, w_all)


def collect(units, tables):
    shape = low_shape(BOTH, HQ + 2 * HK)
    return pl.pallas_call(collect_kernel, out_shape=shape, compiler_params=PARAMS, cost_estimate=cost(4), name="collect")(
        split_units(units), tables
    )


def gradients(n1, d_qkv, gains):
    return pl.pallas_call(
        gradient_kernel,
        out_shape=low_shape(D, QKV + 128),
        compiler_params=PARAMS,
        cost_estimate=cost(5),
        name="gradients",
    )(n1, d_qkv, gains)


def attend_fwd(unit, first, units, starts):
    return pl.pallas_call(
        fwd_kernel,
        grid=(MB,),
        in_specs=[SMEM, SMEM, UNIT_SPEC, COL_SPEC],
        out_specs=[QUERY_SPEC, COL_SPEC],
        out_shape=[low_shape(SHARDS, MB, Q_ROWS, 128), COL_SHAPE],
        compiler_params=PARAMS,
        cost_estimate=cost(20),
        name="attend_forward",
    )(unit, first, units, starts)


def attend_bwd(unit, first, units, starts, d_mixed, lse):
    return pl.pallas_call(
        bwd_kernel,
        grid=(MB,),
        in_specs=[SMEM, SMEM, UNIT_SPEC, COL_SPEC, QUERY_SPEC, COL_SPEC],
        out_specs=UNIT_SPEC,
        out_shape=low_shape(SHARDS, MB, ALL_ROWS, 128),
        scratch_shapes=[pltpu.VMEM((SEQ, 128), jnp.float32)],
        compiler_params=PARAMS,
        cost_estimate=cost(27),
        name="attend_backward",
    )(unit, first, units, starts, d_mixed, lse)


def piece_perm():
    return [(k * SHARDS + s, (s // 16) * SHARDS + 2 * (s % 16) + k) for k in range(2) for s in range(SHARDS)]


def shift(values, axis, step):
    if axis == "x":
        line = lambda x: (x % 2) * 2 + x // 2
        return lax.ppermute(values, ("xl", "xh"), [(line(i), line((i + step) % 4)) for i in range(4)])
    return lax.ppermute(values, axis, [(i, (i + step) % 4) for i in range(4)])


def place(axis):
    if axis == "x":
        return lax.axis_index("xh") * 2 + lax.axis_index("xl")
    return lax.axis_index(axis)


def flip(values, axis):
    return lax.ppermute(values, axis, [(0, 1), (1, 0)])


def col_half(core, local):
    half = local.shape[1] // 2
    return lax.dynamic_slice_in_dim(local, core * half, half, axis=1)


def pad_units(local):
    return jnp.pad(local.reshape(-1, 16, 120), ((0, 0), (0, 0), (0, UNIT_FF - 120))).reshape(-1, PAD_FF)


def crop_units(local):
    return local.reshape(-1, 16, UNIT_FF)[:, :, :120].reshape(-1, HF)


def fold(rows, parts):
    n, r, w = rows.shape
    return rows.reshape(n, r, parts, w // parts).transpose(0, 2, 1, 3).reshape(n, parts * r, w // parts)


def unfold(rows, parts):
    n, r, w = rows.shape
    return rows.reshape(n, parts, r // parts, w).transpose(0, 2, 1, 3).reshape(n, r // parts, parts * w)


def wide_sum(*values):
    total = values[0].astype(jnp.float32)
    for value in values[1:]:
        total = total + value.astype(jnp.float32)
    return total.astype(jnp.bfloat16)


def after(values, event):
    return lax.optimization_barrier((values, event))[0]


def total_axis(values, axis):
    return values + shift(values, axis, 1) + shift(values, axis, 2) + shift(values, axis, 3)


def reduce_x(values, dim):
    size = values.shape[dim] // 2
    me = lax.axis_index("xh")
    keep = lax.dynamic_slice_in_dim(values, me * size, size, axis=dim)
    send = lax.dynamic_slice_in_dim(values, (1 - me) * size, size, axis=dim)
    cross = lax.ppermute(send, ("xl", "xh"), [(i, 3 - i) for i in range(4)])
    return wide_sum(keep, flip(keep, "xl"), flip(send, "xh"), cross)


def add_pair(values, axis):
    return wide_sum(values, flip(values, axis))


def join_pair(mine, axis, dim):
    other = flip(mine, axis)
    lower = lax.axis_index(axis) == 0
    return jnp.concatenate([jnp.where(lower, mine, other), jnp.where(lower, other, mine)], axis=dim)


def join_cores(mine):
    return join_pair(mine, "c", 1).astype(jnp.float32)


def scatter_sum(values):
    return jnp.sum(exchange(values).astype(jnp.float32), axis=0).astype(jnp.bfloat16)


def on_device(
    hidden_in,
    doc_ids,
    out_grad,
    norm_attn,
    w_query,
    w_key,
    w_value,
    w_out,
    norm_ffn,
    w_gate,
    w_up,
    w_down,
):
    core = lax.axis_index("c")
    shard = lax.axis_index(SHARD)
    low = jnp.bfloat16

    rows_in = lax.ppermute(jnp.concatenate([w_out, w_down], axis=0), ("c",) + SHARD, piece_perm())
    gu_piece = jnp.concatenate([pad_units(col_half(core, w_gate)), pad_units(col_half(core, w_up))], axis=1)
    w_all = lax.all_gather(
        jnp.concatenate(
            [
                rows_in[48:144],
                fold(jnp.pad(rows_in[144:], ((0, 8), (0, 0)))[None], 3)[0],
                join_pair(gu_piece, "xh", 0),
                fold(rows_in[:48][None], 2)[0],
            ],
            axis=1,
        ),
        ("z", "y"),
        axis=0,
        tiled=True,
    )
    small = jnp.concatenate(
        [norm_attn[:, None], norm_ffn[:, None], doc_ids.reshape(48, 4).astype(low), jnp.zeros((48, 122), low)], axis=1
    )
    piece = jnp.concatenate(
        [to_groups(col_half(core, w_query)), interleave(col_half(core, w_key), col_half(core, w_value)), small], axis=1
    )
    w_first = exchange(jnp.broadcast_to(piece[None], (SHARDS, 48, QKV + 128)))
    small = w_first[:, :, QKV : QKV + 6]
    w_first = w_first.reshape(D, QKV + 128)
    w_qkv = w_first[:, :QKV]
    gain_attn = small[:, :, 0].reshape(1, D).astype(jnp.float32)
    gain_ffn = small[:, :, 1].reshape(1, D).astype(jnp.float32)
    docs_mine = small[:, :, 2:].reshape(SHARDS, MB, SPAN).transpose(1, 0, 2).reshape(MB, SEQ)
    docs_other = swap(docs_mine)

    x_low = hidden_in.reshape(ROWS, D)
    x = x_low.astype(jnp.float32)
    x_both = jnp.concatenate([x_low, swap(x_low)], axis=0).astype(jnp.float32)
    dy_low = out_grad.reshape(ROWS, D)
    dy = dy_low.astype(jnp.float32)
    df = (branch_scale * jnp.concatenate([dy_low, swap(dy_low)], axis=0).astype(jnp.float32)).astype(low)

    which = lax.rem(shard // PARTS, 2)
    part = lax.rem(shard, PARTS)
    docs = jnp.where(which == 0, docs_mine, docs_other).astype(jnp.float32)
    counted = jnp.sum((docs[:, None, :] < docs[:, :, None]).astype(jnp.int32), axis=-1)
    q_start = lax.dynamic_slice_in_dim(counted.reshape(MB, SHARDS, SPAN), part * CHUNK, CHUNK, axis=2)
    q_start = q_start.reshape(MB, TILES, 1, TILE * CHUNK)
    first = (q_start[:, :, 0, 0] // BLOCK).reshape(-1)
    starts = jnp.broadcast_to(q_start, (MB, TILES, GROUP, TILE * CHUNK)).reshape(MB, TILES, TROWS, 1)
    starts = jnp.broadcast_to(starts, (MB, TILES, TROWS, 128))
    unit = jnp.stack([part, lax.rem(shard // (2 * PARTS), 2)]).astype(jnp.int32)

    places = (shard * SPAN + jnp.arange(SPAN, dtype=jnp.int32)).astype(jnp.float32)
    half_size = HD // 2
    inverse = jnp.exp(-jnp.arange(half_size, dtype=jnp.float32) * (math.log(10000.0) / half_size))
    angles = places[:, None] * inverse[None, :]
    cosine, sine = jnp.cos(angles), jnp.sin(angles)
    cosine = jnp.concatenate([cosine, cosine], axis=1)
    sine = jnp.concatenate([-sine, sine], axis=1)
    tables = jnp.stack(
        [
            jnp.concatenate([cosine, cosine], axis=1),
            jnp.concatenate([sine, sine], axis=1),
            jnp.concatenate([cosine, jnp.ones_like(cosine)], axis=1),
            jnp.concatenate([sine, jnp.zeros_like(sine)], axis=1),
        ]
    )

    r1_both = lax.rsqrt(jnp.mean(x_both * x_both, axis=-1, keepdims=True) + eps_norm)
    r1 = r1_both[:ROWS]
    n1 = (x_both * r1_both * gain_attn).astype(low)
    units = exchange(project(n1, w_first, tables))
    unit_o, lse = attend_fwd(unit, first, units, starts)
    attn, y1_mine, y1_other = out_project(exchange(unit_o), w_all)
    hmid = x + branch_scale * (y1_mine + swap(y1_other).astype(jnp.float32))

    r2 = lax.rsqrt(jnp.mean(hmid * hmid, axis=-1, keepdims=True) + eps_norm)
    z2 = hmid * r2
    n2_mine = (z2 * gain_ffn).astype(low)
    n2 = jnp.concatenate([n2_mine, swap(n2_mine)], axis=0)
    y2_mine, y2_other, dn2_mine, dn2_other, g_ffn = feed_forward(n2, df, w_all)
    result = hmid + branch_scale * (y2_mine + swap(y2_other).astype(jnp.float32))

    dn2 = dn2_mine + swap(dn2_other).astype(jnp.float32)
    e2 = dn2 * gain_ffn
    g_gain_ffn = jnp.sum(dn2 * z2, axis=0)
    dh = dy + r2 * (e2 - z2 * jnp.mean(e2 * z2, axis=-1, keepdims=True))

    da_mine = (branch_scale * dh).astype(low)
    da = jnp.concatenate([da_mine, swap(da_mine)], axis=0)
    unit_do, g_all = d_out_project(da, w_all, attn, g_ffn)
    s_all = lax.psum_scatter(g_all, ("z", "y"), scatter_dimension=0, tiled=True)
    unit_do = exchange(unit_do)
    unit_d = attend_bwd(unit, first, units, starts, unit_do, lse)
    d_qkv = collect(exchange(unit_d), tables)

    dn1_both = product_t(d_qkv, w_qkv)
    dn1 = dn1_both[:ROWS] + swap(dn1_both[ROWS:].astype(low)).astype(jnp.float32)
    z1 = x * r1
    e1 = dn1 * gain_attn
    g_gain_attn = jnp.sum(dn1 * z1, axis=0)
    grad_in = (dh + r1 * (e1 - z1 * jnp.mean(e1 * z1, axis=-1, keepdims=True))).astype(low)

    gains = jnp.concatenate([g_gain_attn[None], g_gain_ffn[None], jnp.zeros((6, D), jnp.float32)], axis=0)
    received = exchange(gradients(n1, d_qkv, gains).reshape(SHARDS, 48, QKV + 128))
    s_all = after(s_all, d_qkv)
    rows = jnp.concatenate(
        [
            unfold(s_all[None, :, OUT_AT:], 2)[0],
            s_all[:, :D],
            unfold(s_all[None, :, REST_AT:GATE_AT], 3)[0][:24],
        ],
        axis=0,
    )
    rows_x = reduce_x(rows, 1)
    rows = join_cores(lax.ppermute(rows_x, ("c",) + SHARD, [(b, a) for a, b in piece_perm()]))
    s_gu = reduce_x(s_all[:, GATE_AT:OUT_AT], 0)
    received = after(received, (s_gu, rows_x))
    s_qkv = add_pair(jnp.sum(received.astype(jnp.float32), axis=0).astype(low), "xl")
    s_gu = jnp.concatenate([crop_units(s_gu[:, :PAD_FF]), crop_units(s_gu[:, PAD_FF:])], axis=1)
    other = swap(s_gu)
    lower = core == 0
    g_g, g_u = [
        jnp.concatenate([jnp.where(lower, m, t), jnp.where(lower, t, m)], axis=1).astype(jnp.float32)
        for m, t in ((s_gu[:, :HF], other[:, :HF]), (s_gu[:, HF:], other[:, HF:]))
    ]
    other = swap(s_qkv)
    whole = [jnp.where(lower, s_qkv, other), jnp.where(lower, other, s_qkv)]
    gains = s_qkv[:, QKV : QKV + 2].astype(jnp.float32) + other[:, QKV : QKV + 2].astype(jnp.float32)

    def heads_of(offset):
        return jnp.concatenate(
            [w[:, HQ + 128 * j + offset : HQ + 128 * j + offset + HD] for w in whole for j in range(HALF_KV)], axis=1
        ).astype(jnp.float32)

    return (
        result.reshape(1, MB, SPAN, D).astype(low),
        grad_in.reshape(1, MB, SPAN, D),
        gains[:, 0],
        jnp.concatenate([from_groups(w[:, :HQ]) for w in whole], axis=1).astype(jnp.float32),
        heads_of(0),
        heads_of(HD),
        rows[:48],
        gains[:, 1],
        g_g,
        g_u,
        rows[48:],
    )


def solution(mesh):
    fine = Mesh(mesh.devices.reshape(2, 2, 4, 4, 2), ("xl", "c", "z", "y", "xh"))
    replica = ("xl", "c")
    tokens = P(replica, None, SHARD, None)
    matrix = P(SHARD, None)
    vector = P(SHARD)
    return jax.shard_map(
        on_device,
        mesh=fine,
        in_specs=(
            tokens,
            P(replica, None, SHARD),
            tokens,
            vector,
            matrix,
            matrix,
            matrix,
            matrix,
            vector,
            matrix,
            matrix,
            matrix,
        ),
        out_specs=(
            tokens,
            tokens,
            vector,
            matrix,
            matrix,
            matrix,
            matrix,
            vector,
            matrix,
            matrix,
            matrix,
        ),
        check_vma=False,
    )
```

```python
from functools import partial
import math

import jax
import jax.numpy as jnp
from jax import lax
from jax.experimental import pallas as pl
from jax.experimental.pallas import tpu as pltpu
from jax.sharding import Mesh
from jax.sharding import PartitionSpec as P

HEADS = 24
KVH = 8
HD = 64
D = 1536
FF = 3840
MB = 3
SPAN = 64
SHARDS = 32
SEQ = 2048
PARTS = 4
ROWS = MB * SPAN
BOTH = 2 * ROWS
GROUP = HEADS // KVH
HALF_KV = KVH // 2
HQ = HALF_KV * GROUP * HD
HK = HALF_KV * HD
HF = FF // 2
QKV = HQ + 2 * HK
UNIT_FF = 128
PAD_FF = 16 * UNIT_FF
REST_AT = D
GATE_AT = D + D // 3
UP_AT = GATE_AT + PAD_FF
OUT_AT = UP_AT + PAD_FF
FF_TILE = 256
FF_TILES = PAD_FF // FF_TILE
FF_ROWS = 96 * FF_TILE // UNIT_FF
CHUNK = SPAN // PARTS
TILE = 4
TILES = SHARDS // TILE
BLOCK = TILE * SPAN
TROWS = GROUP * TILE * CHUNK

SHARD = ("z", "y", "xh")
branch_scale = 1.4 / math.sqrt(52.0)
eps_norm = 1e-05
NEG = -1e30
VMEM_LIMIT = 48 * 1024 * 1024


def product(left, right):
    return jnp.dot(left, right, preferred_element_type=jnp.float32)


def product_t(left, right):
    return lax.dot_general(left, right, (((1,), (1,)), ((), ())), preferred_element_type=jnp.float32)


def t_product(left, right):
    return lax.dot_general(left, right, (((0,), (0,)), ((), ())), preferred_element_type=jnp.float32)


def swap(values):
    return lax.ppermute(values, "c", [(0, 1), (1, 0)])


def exchange(values):
    return lax.all_to_all(values, SHARD, 0, 0, tiled=True)


Q_ROWS = 2 * CHUNK
ALL_ROWS = SPAN + Q_ROWS


def to_groups(rows):
    parts = [rows[:, 192 * j : 192 * j + 128] for j in range(HALF_KV)]
    parts += [rows[:, 192 * j + 128 : 192 * j + 192] for j in range(HALF_KV)]
    return jnp.concatenate(parts, axis=1)


def from_groups(rows):
    parts = []
    for j in range(HALF_KV):
        parts += [rows[:, 128 * j : 128 * j + 128], rows[:, 512 + 64 * j : 576 + 64 * j]]
    return jnp.concatenate(parts, axis=1)


def interleave(keys, values):
    parts = []
    for j in range(HALF_KV):
        parts += [keys[:, HD * j : HD * j + HD], values[:, HD * j : HD * j + HD]]
    return jnp.concatenate(parts, axis=1)


def turn(values, cosine, sine):
    lane = lax.broadcasted_iota(jnp.int32, values.shape, values.ndim - 1)
    axis = values.ndim - 1
    other = jnp.where(lane % HD < HD // 2, pltpu.roll(values, 128 - HD // 2, axis), pltpu.roll(values, HD // 2, axis))
    return values * cosine + other * sine


def project_kernel(n_ref, w_ref, table_ref, out_ref):
    rows = n_ref[...]

    def group(g, table):
        wide = product(rows, w_ref[:, 128 * g : 128 * g + 128]).reshape(2 * MB, SPAN, 128)
        return turn(wide, table_ref[table][None], table_ref[table + 1][None]).astype(jnp.bfloat16)

    for j in range(HALF_KV):
        first, both = group(j, 0), group(6 + j, 2)
        if j % 2 == 0:
            third = group(4 + j // 2, 0)
        for o in range(2):
            for m in range(MB):
                for p in range(PARTS):
                    cut = slice(p * CHUNK, (p + 1) * CHUNK)
                    out_ref[j, o, p, m, 0:SPAN, :] = both[o * MB + m]
                    out_ref[j, o, p, m, SPAN : SPAN + CHUNK, :] = first[o * MB + m, cut]
                    out_ref[j, o, p, m, SPAN + CHUNK : ALL_ROWS, :] = third[o * MB + m, cut]


def third_head(pair_even, pair_odd):
    lane = lax.broadcasted_iota(jnp.int32, pair_even.shape, pair_even.ndim - 1)
    return jnp.where(lane < HD, pair_even, pair_odd)


def out_halves(ref):
    whole = ref[...].reshape(16, 2, 48, D // 2)
    return whole[:, 0].reshape(HQ, D // 2), whole[:, 1].reshape(HQ, D // 2)


def out_kernel(u_ref, w_ref, attn_ref, mine_ref, other_ref):
    for o in range(2):
        for m in range(MB):
            for p in range(PARTS):
                thirds = [
                    third_head(u_ref[2 * k, o, p, m, CHUNK:, :], u_ref[2 * k + 1, o, p, m, CHUNK:, :])
                    for k in range(2)
                ]
                parts = []
                for j in range(HALF_KV):
                    parts += [u_ref[j, o, p, m, :CHUNK, :], thirds[j // 2][:, HD * (j % 2) : HD * (j % 2) + HD]]
                at = (o * MB + m) * SPAN + p * CHUNK
                attn_ref[at : at + CHUNK, :] = jnp.concatenate(parts, axis=1)
    attn = attn_ref[...]
    for k, half in enumerate(out_halves(w_ref)):
        result = product(attn, half)
        cols = slice(k * (D // 2), (k + 1) * (D // 2))
        mine_ref[:, cols] = result[:ROWS]
        other_ref[:, cols] = result[ROWS:].astype(jnp.bfloat16)


def d_out_kernel(da_ref, w_ref, attn_ref, held_ref, out_ref, grad_ref, g_out, sem):
    attn_t = attn_ref[...].T
    for k in range(2):
        half = product(attn_t, da_ref[:, k * (D // 2) : (k + 1) * (D // 2)]).astype(jnp.bfloat16)
        for j in range(16):
            g_out[j * 96 + k * 48 : j * 96 + k * 48 + 48, :] = half[j * 48 : j * 48 + 48]
    copy = pltpu.make_async_copy(g_out, grad_ref.at[:, pl.ds(OUT_AT, D // 2)], sem)
    copy.start()
    left, right = out_halves(w_ref)
    rows = product_t(da_ref[:, : D // 2], left) + product_t(da_ref[:, D // 2 :], right)
    rows = rows.astype(jnp.bfloat16)
    for j in range(HALF_KV):
        first = rows[:, 192 * j : 192 * j + 128]
        if j % 2 == 0:
            third = jnp.concatenate([rows[:, 192 * j + 128 : 192 * j + 192], rows[:, 192 * j + 320 : 192 * j + 384]], axis=1)
        for o in range(2):
            for m in range(MB):
                for p in range(PARTS):
                    at = (o * MB + m) * SPAN + p * CHUNK
                    out_ref[j, o, p, m, :CHUNK, :] = first[at : at + CHUNK]
                    out_ref[j, o, p, m, CHUNK:, :] = third[at : at + CHUNK]
    copy.wait()


def collect_kernel(u_ref, table_ref, out_ref):
    def put(g, o, m, at, size, values, table, row):
        cosine = table_ref[table, row : row + size]
        sine = table_ref[table + 1, row : row + size]
        out_ref[at : at + size, 128 * g : 128 * g + 128] = turn(values, cosine, -sine).astype(jnp.bfloat16)

    wide = jnp.float32
    for o in range(2):
        for m in range(MB):
            base = (o * MB + m) * SPAN
            for j in range(HALF_KV):
                total = u_ref[j, o, 0, m, 0:SPAN, :].astype(wide)
                for p in range(1, PARTS):
                    total = total + u_ref[j, o, p, m, 0:SPAN, :].astype(wide)
                put(6 + j, o, m, base, SPAN, total, 2, 0)
            for p in range(PARTS):
                at = base + p * CHUNK
                for j in range(HALF_KV):
                    first = u_ref[j, o, p, m, SPAN : SPAN + CHUNK, :].astype(wide)
                    put(j, o, m, at, CHUNK, first, 0, p * CHUNK)
                for k in range(2):
                    third = third_head(
                        u_ref[2 * k, o, p, m, SPAN + CHUNK : ALL_ROWS, :].astype(wide),
                        u_ref[2 * k + 1, o, p, m, SPAN + CHUNK : ALL_ROWS, :].astype(wide),
                    )
                    put(4 + k, o, m, at, CHUNK, third, 0, p * CHUNK)


def gradient_kernel(n_ref, d_ref, gains_ref, out_ref):
    out_ref[:, :QKV] = product(n_ref[...].T, d_ref[...]).astype(jnp.bfloat16)
    gains = jnp.concatenate([gains_ref[...], jnp.zeros((120, D), jnp.float32)], axis=0)
    out_ref[:, QKV:] = gains.T.astype(jnp.bfloat16)


def stack_heads(first, third, odd):
    last = jnp.where(odd == 1, third[:, HD:], third[:, :HD])
    return jnp.concatenate([first[:, :HD], first[:, HD:], last], axis=0)


def lay_heads(rows):
    size = TILE * CHUNK
    parts = [rows[g * size : (g + 1) * size] for g in range(GROUP)]
    shape = (TILE, CHUNK, 128)
    return (
        jnp.concatenate(parts[:2], axis=1).astype(jnp.bfloat16).reshape(shape),
        jnp.concatenate([parts[2], parts[2]], axis=1).astype(jnp.bfloat16).reshape(shape),
    )


def tile_mask(part, start_rows, tile, blocks):
    wide = blocks * BLOCK
    row = lax.broadcasted_iota(jnp.int32, (TROWS, 1), 0)
    inside = lax.rem(row, TILE * CHUNK)
    q_pos = tile * BLOCK + (inside // CHUNK) * SPAN + part * CHUNK + lax.rem(inside, CHUNK)
    k_pos = (tile + 1 - blocks) * BLOCK + lax.broadcasted_iota(jnp.int32, (TROWS, wide), 1)
    return (k_pos >= start_rows) & (k_pos <= q_pos)


def tile_queries(ref, tile, begin, odd):
    where = pl.ds(tile * TILE, TILE)
    first = ref[where, 0, begin : begin + CHUNK, :].reshape(TILE * CHUNK, 128)
    third = ref[where, 0, begin + CHUNK : begin + 2 * CHUNK, :].reshape(TILE * CHUNK, 128)
    return stack_heads(first, third, odd)


def tile_keys(ref, begin, blocks):
    return ref[pl.ds(begin * TILE, blocks * TILE), 0, 0:SPAN, :].reshape(blocks * BLOCK, 128)


def each_tile(first_ref, work):
    micro = pl.program_id(0)

    def body(tile, carry):
        needed = tile + 1 - first_ref[micro * TILES + tile]
        for blocks in range(1, TILES + 1):
            pl.when(needed == blocks)(partial(work, tile, blocks))
        return carry

    lax.fori_loop(0, TILES, body, 0)


def fwd_kernel(unit_ref, first_ref, u_ref, start_ref, o_ref, lse_ref):
    part, odd = unit_ref[0], unit_ref[1]

    def work(tile, blocks):
        q_rows = tile_queries(u_ref, tile, SPAN, odd) * jnp.bfloat16(0.125)
        keys = tile_keys(u_ref, tile + 1 - blocks, blocks)
        scores = product_t(q_rows, keys[:, :HD])
        allowed = tile_mask(part, start_ref[0, tile][:, :1], tile, blocks)
        scores = jnp.where(allowed, scores, NEG)
        highest = jnp.max(scores, axis=-1, keepdims=True)
        expo = jnp.exp(scores - highest)
        total = jnp.sum(expo, axis=-1, keepdims=True)
        mixed = product(expo.astype(jnp.bfloat16), keys[:, HD:]) / total
        where = pl.ds(tile * TILE, TILE)
        o_ref[where, 0, :CHUNK, :], o_ref[where, 0, CHUNK:, :] = lay_heads(mixed)
        lse_ref[0, tile] = jnp.broadcast_to(highest + jnp.log(total), (TROWS, 128))

    each_tile(first_ref, work)


def bwd_kernel(unit_ref, first_ref, u_ref, start_ref, do_ref, lse_ref, d_ref, acc):
    part, odd = unit_ref[0], unit_ref[1]
    acc[...] = jnp.zeros_like(acc)

    def work(tile, blocks):
        begin = tile + 1 - blocks
        q_rows = tile_queries(u_ref, tile, SPAN, odd) * jnp.bfloat16(0.125)
        d_rows = tile_queries(do_ref, tile, 0, odd)
        keys = tile_keys(u_ref, begin, blocks)
        scores = product_t(q_rows, keys[:, :HD])
        allowed = tile_mask(part, start_ref[0, tile][:, :1], tile, blocks)
        probs = jnp.where(allowed, jnp.exp(scores - lse_ref[0, tile][:, :1]), 0.0)
        d_probs = product_t(d_rows, keys[:, HD:])
        offset = jnp.sum(d_probs * probs, axis=-1, keepdims=True)
        d_scores = (probs * (d_probs - offset)).astype(jnp.bfloat16)
        d_query = product(d_scores, keys[:, :HD]) * 0.125
        at = pl.ds(tile * TILE, TILE)
        d_ref[at, 0, SPAN : SPAN + CHUNK, :], d_ref[at, 0, SPAN + CHUNK : ALL_ROWS, :] = lay_heads(d_query)
        d_key = t_product(d_scores, q_rows)
        d_value = t_product(probs.astype(jnp.bfloat16), d_rows)
        where = pl.ds(begin * BLOCK, blocks * BLOCK)
        acc[where, :] += jnp.concatenate([d_key, d_value], axis=1)

    each_tile(first_ref, work)
    d_ref[:, 0, 0:SPAN, :] = acc[...].astype(jnp.bfloat16).reshape(SHARDS, SPAN, 128)


SMEM = pl.BlockSpec(memory_space=pltpu.SMEM)
UNIT_SPEC = pl.BlockSpec((SHARDS, 1, ALL_ROWS, 128), lambda m: (0, m, 0, 0))
QUERY_SPEC = pl.BlockSpec((SHARDS, 1, Q_ROWS, 128), lambda m: (0, m, 0, 0))
COL_SPEC = pl.BlockSpec((1, TILES, TROWS, 128), lambda m: (m, 0, 0, 0))
COL_SHAPE = jax.ShapeDtypeStruct((MB, TILES, TROWS, 128), jnp.float32)
PARAMS = pltpu.CompilerParams(vmem_limit_bytes=VMEM_LIMIT)


def split_units(values):
    return values.reshape((HALF_KV, 2, PARTS) + values.shape[1:])


def low_shape(*dims):
    return jax.ShapeDtypeStruct(dims, jnp.bfloat16)


def project(n1, w_qkv, tables):
    shape = low_shape(HALF_KV, 2, PARTS, MB, ALL_ROWS, 128)
    out = pl.pallas_call(project_kernel, out_shape=shape, compiler_params=PARAMS, cost_estimate=cost(6), name="project")(n1, w_qkv, tables)
    return out.reshape(SHARDS, MB, ALL_ROWS, 128)


def whole_spec(*dims):
    return pl.BlockSpec(dims, lambda i: (0,) * len(dims))


OUT_SPEC = pl.BlockSpec((D, D // 2), lambda i: (0, OUT_AT // (D // 2)))


def cost(micros):
    return pl.CostEstimate(flops=int(micros * 1e9), bytes_accessed=1 << 20, transcendentals=0)


def out_project(units, w_all):
    return pl.pallas_call(
        out_kernel,
        grid=(1,),
        in_specs=[whole_spec(HALF_KV, 2, PARTS, MB, Q_ROWS, 128), OUT_SPEC],
        out_specs=[whole_spec(BOTH, HQ), whole_spec(ROWS, D), whole_spec(ROWS, D)],
        out_shape=[low_shape(BOTH, HQ), jax.ShapeDtypeStruct((ROWS, D), jnp.float32), low_shape(ROWS, D)],
        compiler_params=PARAMS,
        cost_estimate=cost(3),
        name="out_project",
    )(split_units(units), w_all)


def d_out_project(da, w_all, attn, g_ffn):
    dims = (HALF_KV, 2, PARTS, MB, Q_ROWS, 128)
    anywhere = pl.BlockSpec(memory_space=pl.ANY)
    out, grads = pl.pallas_call(
        d_out_kernel,
        grid=(1,),
        in_specs=[whole_spec(BOTH, D), OUT_SPEC, whole_spec(BOTH, HQ), anywhere],
        out_specs=[whole_spec(*dims), anywhere],
        out_shape=[low_shape(*dims), low_shape(*g_ffn.shape)],
        scratch_shapes=[pltpu.VMEM((D, D // 2), jnp.bfloat16), pltpu.SemaphoreType.DMA],
        input_output_aliases={3: 1},
        compiler_params=PARAMS,
        cost_estimate=cost(5),
        name="d_out_project",
    )(da, w_all, attn, g_ffn)
    return out.reshape(SHARDS, MB, Q_ROWS, 128), grads


def ffn_kernel(
    n_ref, df_ref, main_ref, rest_ref, gate_ref, up_ref,
    y_mine_ref, y_other_ref, dn_mine_ref, dn_other_ref, grad_ref,
    n_t, y_acc, dn_acc, g_gate, g_up, g_main, g_rest, sems,
):
    step = pl.program_id(0)
    slot = lax.rem(step, 2)

    def copies(at, slot):
        cols, rows = at * FF_TILE, at * FF_ROWS
        return [
            pltpu.make_async_copy(
                g_gate.at[slot], grad_ref.at[:, pl.ds(pl.multiple_of(GATE_AT + cols, FF_TILE), FF_TILE)], sems.at[slot, 0]
            ),
            pltpu.make_async_copy(
                g_up.at[slot], grad_ref.at[:, pl.ds(pl.multiple_of(UP_AT + cols, FF_TILE), FF_TILE)], sems.at[slot, 1]
            ),
            pltpu.make_async_copy(
                g_main.at[slot], grad_ref.at[pl.ds(pl.multiple_of(rows, 64), FF_ROWS), pl.ds(0, D)], sems.at[slot, 2]
            ),
            pltpu.make_async_copy(
                g_rest.at[slot],
                grad_ref.at[pl.ds(pl.multiple_of(rows, 64), FF_ROWS), pl.ds(REST_AT, D // 3)],
                sems.at[slot, 3],
            ),
        ]

    @pl.when(step == 0)
    def _():
        n_t[...] = n_ref[...].T
        y_acc[...] = jnp.zeros_like(y_acc)
        dn_acc[...] = jnp.zeros_like(dn_acc)

    @pl.when(step >= 2)
    def _():
        for copy in copies(step - 2, slot):
            copy.wait()

    low = jnp.bfloat16
    units = []
    for j in range(FF_TILE // UNIT_FF):
        rest = [rest_ref[j * 96 + q * 32 : j * 96 + q * 32 + 32, :] for q in range(3)]
        units += [main_ref[j * 96 : j * 96 + 96, :], jnp.concatenate(rest, axis=1)]
    w_down = jnp.concatenate(units, axis=0)
    rows, df = n_ref[...], df_ref[...]
    gate, up = product(rows, gate_ref[...]), product(rows, up_ref[...])
    sigma = jax.nn.sigmoid(gate)
    silu = gate * sigma
    act = (silu * up).astype(low)
    d_act = product_t(df, w_down)
    d_gate = (d_act * up * sigma * (1.0 + gate * (1.0 - sigma))).astype(low)
    d_up = (d_act * silu).astype(low)
    y_acc[...] += product(act, w_down)
    dn_acc[...] += product_t(d_gate, gate_ref[...]) + product_t(d_up, up_ref[...])
    g_gate[slot] = product(n_t[...], d_gate).astype(low)
    g_up[slot] = product(n_t[...], d_up).astype(low)
    g_down = product(act.T, df).astype(low)
    for j in range(FF_TILE // UNIT_FF):
        g_main[slot, j * 96 : j * 96 + 96, :] = g_down[j * UNIT_FF : j * UNIT_FF + 96]
        for q in range(3):
            g_rest[slot, j * 96 + q * 32 : j * 96 + q * 32 + 32, :] = g_down[
                j * UNIT_FF + 96 : (j + 1) * UNIT_FF, q * (D // 3) : (q + 1) * (D // 3)
            ]
    for copy in copies(step, slot):
        copy.start()

    @pl.when(step == FF_TILES - 1)
    def _():
        y_mine_ref[...] = y_acc[:ROWS]
        y_other_ref[...] = y_acc[ROWS:].astype(low)
        dn_mine_ref[...] = dn_acc[:ROWS]
        dn_other_ref[...] = dn_acc[ROWS:].astype(low)
        for back in (1, 0):
            for copy in copies(step - back, lax.rem(step - back, 2)):
                copy.wait()


def feed_forward(n2, df, w_all):
    wide = jax.ShapeDtypeStruct((ROWS, D), jnp.float32)
    return pl.pallas_call(
        ffn_kernel,
        grid=(FF_TILES,),
        in_specs=[
            whole_spec(BOTH, D),
            whole_spec(BOTH, D),
            pl.BlockSpec((FF_ROWS, D), lambda t: (t, 0)),
            pl.BlockSpec((FF_ROWS, D // 3), lambda t: (t, REST_AT // (D // 3))),
            pl.BlockSpec((D, FF_TILE), lambda t: (0, GATE_AT // FF_TILE + t)),
            pl.BlockSpec((D, FF_TILE), lambda t: (0, UP_AT // FF_TILE + t)),
        ],
        out_specs=[whole_spec(ROWS, D)] * 4 + [pl.BlockSpec(memory_space=pl.ANY)],
        out_shape=[wide, low_shape(ROWS, D), wide, low_shape(ROWS, D), low_shape(D, OUT_AT + D // 2)],
        scratch_shapes=[
            pltpu.VMEM((D, BOTH), jnp.bfloat16),
            pltpu.VMEM((BOTH, D), jnp.float32),
            pltpu.VMEM((BOTH, D), jnp.float32),
            pltpu.VMEM((2, D, FF_TILE), jnp.bfloat16),
            pltpu.VMEM((2, D, FF_TILE), jnp.bfloat16),
            pltpu.VMEM((2, FF_ROWS, D), jnp.bfloat16),
            pltpu.VMEM((2, FF_ROWS, D // 3), jnp.bfloat16),
            pltpu.SemaphoreType.DMA((2, 4)),
        ],
        compiler_params=PARAMS,
        cost_estimate=cost(30),
        name="feed_forward",
    )(n2, df, w_all, w_all, w_all, w_all)


def collect(units, tables):
    shape = low_shape(BOTH, HQ + 2 * HK)
    return pl.pallas_call(collect_kernel, out_shape=shape, compiler_params=PARAMS, cost_estimate=cost(4), name="collect")(
        split_units(units), tables
    )


def gradients(n1, d_qkv, gains):
    return pl.pallas_call(
        gradient_kernel,
        out_shape=low_shape(D, QKV + 128),
        compiler_params=PARAMS,
        cost_estimate=cost(5),
        name="gradients",
    )(n1, d_qkv, gains)


def attend_fwd(unit, first, units, starts):
    return pl.pallas_call(
        fwd_kernel,
        grid=(MB,),
        in_specs=[SMEM, SMEM, UNIT_SPEC, COL_SPEC],
        out_specs=[QUERY_SPEC, COL_SPEC],
        out_shape=[low_shape(SHARDS, MB, Q_ROWS, 128), COL_SHAPE],
        compiler_params=PARAMS,
        cost_estimate=cost(20),
        name="attend_forward",
    )(unit, first, units, starts)


def attend_bwd(unit, first, units, starts, d_mixed, lse):
    return pl.pallas_call(
        bwd_kernel,
        grid=(MB,),
        in_specs=[SMEM, SMEM, UNIT_SPEC, COL_SPEC, QUERY_SPEC, COL_SPEC],
        out_specs=UNIT_SPEC,
        out_shape=low_shape(SHARDS, MB, ALL_ROWS, 128),
        scratch_shapes=[pltpu.VMEM((SEQ, 128), jnp.float32)],
        compiler_params=PARAMS,
        cost_estimate=cost(27),
        name="attend_backward",
    )(unit, first, units, starts, d_mixed, lse)


def piece_perm():
    return [(k * SHARDS + s, (s // 16) * SHARDS + 2 * (s % 16) + k) for k in range(2) for s in range(SHARDS)]


def shift(values, axis, step):
    if axis == "x":
        line = lambda x: (x % 2) * 2 + x // 2
        return lax.ppermute(values, ("xl", "xh"), [(line(i), line((i + step) % 4)) for i in range(4)])
    return lax.ppermute(values, axis, [(i, (i + step) % 4) for i in range(4)])


def place(axis):
    if axis == "x":
        return lax.axis_index("xh") * 2 + lax.axis_index("xl")
    return lax.axis_index(axis)


def flip(values, axis):
    return lax.ppermute(values, axis, [(0, 1), (1, 0)])


def col_half(core, local):
    half = local.shape[1] // 2
    return lax.dynamic_slice_in_dim(local, core * half, half, axis=1)


def pad_units(local):
    return jnp.pad(local.reshape(-1, 16, 120), ((0, 0), (0, 0), (0, UNIT_FF - 120))).reshape(-1, PAD_FF)


def crop_units(local):
    return local.reshape(-1, 16, UNIT_FF)[:, :, :120].reshape(-1, HF)


def fold(rows, parts):
    n, r, w = rows.shape
    return rows.reshape(n, r, parts, w // parts).transpose(0, 2, 1, 3).reshape(n, parts * r, w // parts)


def unfold(rows, parts):
    n, r, w = rows.shape
    return rows.reshape(n, parts, r // parts, w).transpose(0, 2, 1, 3).reshape(n, r // parts, parts * w)


def wide_sum(*values):
    total = values[0].astype(jnp.float32)
    for value in values[1:]:
        total = total + value.astype(jnp.float32)
    return total.astype(jnp.bfloat16)


def after(values, event):
    return lax.optimization_barrier((values, event))[0]


def total_axis(values, axis):
    return values + shift(values, axis, 1) + shift(values, axis, 2) + shift(values, axis, 3)


def reduce_x(values, dim):
    size = values.shape[dim] // 2
    me = lax.axis_index("xh")
    keep = lax.dynamic_slice_in_dim(values, me * size, size, axis=dim)
    send = lax.dynamic_slice_in_dim(values, (1 - me) * size, size, axis=dim)
    cross = lax.ppermute(send, ("xl", "xh"), [(i, 3 - i) for i in range(4)])
    return wide_sum(keep, flip(keep, "xl"), flip(send, "xh"), cross)


def add_pair(values, axis):
    return wide_sum(values, flip(values, axis))


def join_pair(mine, axis, dim):
    other = flip(mine, axis)
    lower = lax.axis_index(axis) == 0
    return jnp.concatenate([jnp.where(lower, mine, other), jnp.where(lower, other, mine)], axis=dim)


def join_cores(mine):
    return join_pair(mine, "c", 1).astype(jnp.float32)


def scatter_sum(values):
    return jnp.sum(exchange(values).astype(jnp.float32), axis=0).astype(jnp.bfloat16)


def on_device(
    hidden_in,
    doc_ids,
    out_grad,
    norm_attn,
    w_query,
    w_key,
    w_value,
    w_out,
    norm_ffn,
    w_gate,
    w_up,
    w_down,
):
    core = lax.axis_index("c")
    shard = lax.axis_index(SHARD)
    low = jnp.bfloat16

    rows_in = lax.ppermute(jnp.concatenate([w_out, w_down], axis=0), ("c",) + SHARD, piece_perm())
    gu_piece = jnp.concatenate([pad_units(col_half(core, w_gate)), pad_units(col_half(core, w_up))], axis=1)
    w_all = lax.all_gather(
        jnp.concatenate(
            [
                rows_in[48:144],
                fold(jnp.pad(rows_in[144:], ((0, 8), (0, 0)))[None], 3)[0],
                join_pair(gu_piece, "xh", 0),
                fold(rows_in[:48][None], 2)[0],
            ],
            axis=1,
        ),
        ("z", "y"),
        axis=0,
        tiled=True,
    )
    small = jnp.concatenate(
        [norm_attn[:, None], norm_ffn[:, None], doc_ids.reshape(48, 4).astype(low), jnp.zeros((48, 122), low)], axis=1
    )
    piece = jnp.concatenate(
        [to_groups(col_half(core, w_query)), interleave(col_half(core, w_key), col_half(core, w_value)), small], axis=1
    )
    w_first = exchange(jnp.broadcast_to(piece[None], (SHARDS, 48, QKV + 128)))
    small = w_first[:, :, QKV : QKV + 6]
    w_first = w_first.reshape(D, QKV + 128)
    w_qkv = w_first[:, :QKV]
    gain_attn = small[:, :, 0].reshape(1, D).astype(jnp.float32)
    gain_ffn = small[:, :, 1].reshape(1, D).astype(jnp.float32)
    docs_mine = small[:, :, 2:].reshape(SHARDS, MB, SPAN).transpose(1, 0, 2).reshape(MB, SEQ)
    docs_other = swap(docs_mine)

    x_low = hidden_in.reshape(ROWS, D)
    x = x_low.astype(jnp.float32)
    x_both = jnp.concatenate([x_low, swap(x_low)], axis=0).astype(jnp.float32)
    dy_low = out_grad.reshape(ROWS, D)
    dy = dy_low.astype(jnp.float32)
    df = (branch_scale * jnp.concatenate([dy_low, swap(dy_low)], axis=0).astype(jnp.float32)).astype(low)

    which = lax.rem(shard // PARTS, 2)
    part = lax.rem(shard, PARTS)
    docs = jnp.where(which == 0, docs_mine, docs_other).astype(jnp.float32)
    counted = jnp.sum((docs[:, None, :] < docs[:, :, None]).astype(jnp.int32), axis=-1)
    q_start = lax.dynamic_slice_in_dim(counted.reshape(MB, SHARDS, SPAN), part * CHUNK, CHUNK, axis=2)
    q_start = q_start.reshape(MB, TILES, 1, TILE * CHUNK)
    first = (q_start[:, :, 0, 0] // BLOCK).reshape(-1)
    starts = jnp.broadcast_to(q_start, (MB, TILES, GROUP, TILE * CHUNK)).reshape(MB, TILES, TROWS, 1)
    starts = jnp.broadcast_to(starts, (MB, TILES, TROWS, 128))
    unit = jnp.stack([part, lax.rem(shard // (2 * PARTS), 2)]).astype(jnp.int32)

    places = (shard * SPAN + jnp.arange(SPAN, dtype=jnp.int32)).astype(jnp.float32)
    half_size = HD // 2
    inverse = jnp.exp(-jnp.arange(half_size, dtype=jnp.float32) * (math.log(10000.0) / half_size))
    angles = places[:, None] * inverse[None, :]
    cosine, sine = jnp.cos(angles), jnp.sin(angles)
    cosine = jnp.concatenate([cosine, cosine], axis=1)
    sine = jnp.concatenate([-sine, sine], axis=1)
    tables = jnp.stack(
        [
            jnp.concatenate([cosine, cosine], axis=1),
            jnp.concatenate([sine, sine], axis=1),
            jnp.concatenate([cosine, jnp.ones_like(cosine)], axis=1),
            jnp.concatenate([sine, jnp.zeros_like(sine)], axis=1),
        ]
    )

    r1_both = lax.rsqrt(jnp.mean(x_both * x_both, axis=-1, keepdims=True) + eps_norm)
    r1 = r1_both[:ROWS]
    n1 = (x_both * r1_both * gain_attn).astype(low)
    units = exchange(project(n1, w_first, tables))
    unit_o, lse = attend_fwd(unit, first, units, starts)
    attn, y1_mine, y1_other = out_project(exchange(unit_o), w_all)
    hmid = x + branch_scale * (y1_mine + swap(y1_other).astype(jnp.float32))

    r2 = lax.rsqrt(jnp.mean(hmid * hmid, axis=-1, keepdims=True) + eps_norm)
    z2 = hmid * r2
    n2_mine = (z2 * gain_ffn).astype(low)
    n2 = jnp.concatenate([n2_mine, swap(n2_mine)], axis=0)
    y2_mine, y2_other, dn2_mine, dn2_other, g_ffn = feed_forward(n2, df, w_all)
    result = hmid + branch_scale * (y2_mine + swap(y2_other).astype(jnp.float32))

    dn2 = dn2_mine + swap(dn2_other).astype(jnp.float32)
    e2 = dn2 * gain_ffn
    g_gain_ffn = jnp.sum(dn2 * z2, axis=0)
    dh = dy + r2 * (e2 - z2 * jnp.mean(e2 * z2, axis=-1, keepdims=True))

    da_mine = (branch_scale * dh).astype(low)
    da = jnp.concatenate([da_mine, swap(da_mine)], axis=0)
    unit_do, g_all = d_out_project(da, w_all, attn, g_ffn)
    s_all = lax.psum_scatter(g_all, ("z", "y"), scatter_dimension=0, tiled=True)
    unit_do = exchange(unit_do)
    unit_d = attend_bwd(unit, first, units, starts, unit_do, lse)
    d_qkv = collect(exchange(unit_d), tables)

    dn1_both = product_t(d_qkv, w_qkv)
    dn1 = dn1_both[:ROWS] + swap(dn1_both[ROWS:].astype(low)).astype(jnp.float32)
    z1 = x * r1
    e1 = dn1 * gain_attn
    g_gain_attn = jnp.sum(dn1 * z1, axis=0)
    grad_in = (dh + r1 * (e1 - z1 * jnp.mean(e1 * z1, axis=-1, keepdims=True))).astype(low)

    gains = jnp.concatenate([g_gain_attn[None], g_gain_ffn[None], jnp.zeros((6, D), jnp.float32)], axis=0)
    s_qkv = add_pair(scatter_sum(gradients(n1, d_qkv, gains).reshape(SHARDS, 48, QKV + 128)), "xl")
    other_qkv = swap(s_qkv)
    s_all = after(s_all, other_qkv)
    rows = jnp.concatenate(
        [
            unfold(s_all[None, :, OUT_AT:], 2)[0],
            s_all[:, :D],
            unfold(s_all[None, :, REST_AT:GATE_AT], 3)[0][:24],
        ],
        axis=0,
    )
    rows_x = reduce_x(rows, 1)
    rows = join_cores(lax.ppermute(rows_x, ("c",) + SHARD, [(b, a) for a, b in piece_perm()]))
    s_gu = reduce_x(s_all[:, GATE_AT:OUT_AT], 0)
    other = swap(s_gu)
    lower = core == 0
    s_gu, other = [
        [crop_units(v[:, :PAD_FF]), crop_units(v[:, PAD_FF:])] for v in (s_gu.astype(jnp.float32), other.astype(jnp.float32))
    ]
    g_g, g_u = [
        jnp.concatenate([jnp.where(lower, m, t), jnp.where(lower, t, m)], axis=1) for m, t in zip(s_gu, other)
    ]
    whole = [jnp.where(lower, s_qkv, other_qkv), jnp.where(lower, other_qkv, s_qkv)]
    gains = s_qkv[:, QKV : QKV + 2].astype(jnp.float32) + other_qkv[:, QKV : QKV + 2].astype(jnp.float32)

    def heads_of(offset):
        return jnp.concatenate(
            [w[:, HQ + 128 * j + offset : HQ + 128 * j + offset + HD] for w in whole for j in range(HALF_KV)], axis=1
        ).astype(jnp.float32)

    return (
        result.reshape(1, MB, SPAN, D).astype(low),
        grad_in.reshape(1, MB, SPAN, D),
        gains[:, 0],
        jnp.concatenate([from_groups(w[:, :HQ]) for w in whole], axis=1).astype(jnp.float32),
        heads_of(0),
        heads_of(HD),
        rows[:48],
        gains[:, 1],
        g_g,
        g_u,
        rows[48:],
    )


def solution(mesh):
    fine = Mesh(mesh.devices.reshape(2, 2, 4, 4, 2), ("xl", "c", "z", "y", "xh"))
    replica = ("xl", "c")
    tokens = P(replica, None, SHARD, None)
    matrix = P(SHARD, None)
    vector = P(SHARD)
    return jax.shard_map(
        on_device,
        mesh=fine,
        in_specs=(
            tokens,
            P(replica, None, SHARD),
            tokens,
            vector,
            matrix,
            matrix,
            matrix,
            matrix,
            vector,
            matrix,
            matrix,
            matrix,
        ),
        out_specs=(
            tokens,
            tokens,
            vector,
            matrix,
            matrix,
            matrix,
            matrix,
            vector,
            matrix,
            matrix,
            matrix,
        ),
        check_vma=False,
    )
```

```python
from functools import partial
import math

import jax
import jax.numpy as jnp
from jax import lax
from jax.experimental import pallas as pl
from jax.experimental.pallas import tpu as pltpu
from jax.sharding import Mesh
from jax.sharding import PartitionSpec as P

HEADS = 24
KVH = 8
HD = 64
D = 1536
FF = 3840
MB = 3
SPAN = 64
SHARDS = 32
SEQ = 2048
PARTS = 4
ROWS = MB * SPAN
BOTH = 2 * ROWS
GROUP = HEADS // KVH
HALF_KV = KVH // 2
HQ = HALF_KV * GROUP * HD
HK = HALF_KV * HD
HF = FF // 2
QKV = HQ + 2 * HK
UNIT_FF = 128
PAD_FF = 16 * UNIT_FF
REST_AT = D
GATE_AT = D + D // 3
UP_AT = GATE_AT + PAD_FF
OUT_AT = UP_AT + PAD_FF
FF_TILE = 512
FF_TILES = PAD_FF // FF_TILE
FF_ROWS = 96 * FF_TILE // UNIT_FF
CHUNK = SPAN // PARTS
TILE = 4
TILES = SHARDS // TILE
BLOCK = TILE * SPAN
TROWS = GROUP * TILE * CHUNK

SHARD = ("z", "y", "xh")
branch_scale = 1.4 / math.sqrt(52.0)
eps_norm = 1e-05
NEG = -1e30
VMEM_LIMIT = 48 * 1024 * 1024


def product(left, right):
    return jnp.dot(left, right, preferred_element_type=jnp.float32)


def product_t(left, right):
    return lax.dot_general(left, right, (((1,), (1,)), ((), ())), preferred_element_type=jnp.float32)


def t_product(left, right):
    return lax.dot_general(left, right, (((0,), (0,)), ((), ())), preferred_element_type=jnp.float32)


def swap(values):
    return lax.ppermute(values, "c", [(0, 1), (1, 0)])


def exchange(values):
    return lax.all_to_all(values, SHARD, 0, 0, tiled=True)


Q_ROWS = 2 * CHUNK
ALL_ROWS = SPAN + Q_ROWS


def to_groups(rows):
    parts = [rows[:, 192 * j : 192 * j + 128] for j in range(HALF_KV)]
    parts += [rows[:, 192 * j + 128 : 192 * j + 192] for j in range(HALF_KV)]
    return jnp.concatenate(parts, axis=1)


def from_groups(rows):
    parts = []
    for j in range(HALF_KV):
        parts += [rows[:, 128 * j : 128 * j + 128], rows[:, 512 + 64 * j : 576 + 64 * j]]
    return jnp.concatenate(parts, axis=1)


def interleave(keys, values):
    parts = []
    for j in range(HALF_KV):
        parts += [keys[:, HD * j : HD * j + HD], values[:, HD * j : HD * j + HD]]
    return jnp.concatenate(parts, axis=1)


def turn(values, cosine, sine):
    lane = lax.broadcasted_iota(jnp.int32, values.shape, values.ndim - 1)
    axis = values.ndim - 1
    other = jnp.where(lane % HD < HD // 2, pltpu.roll(values, 128 - HD // 2, axis), pltpu.roll(values, HD // 2, axis))
    return values * cosine + other * sine


def project_kernel(n_ref, w_ref, table_ref, out_ref):
    rows = n_ref[...]

    def group(g, table):
        wide = product(rows, w_ref[:, 128 * g : 128 * g + 128]).reshape(2 * MB, SPAN, 128)
        return turn(wide, table_ref[table][None], table_ref[table + 1][None]).astype(jnp.bfloat16)

    for j in range(HALF_KV):
        first, both = group(j, 0), group(6 + j, 2)
        if j % 2 == 0:
            third = group(4 + j // 2, 0)
        for o in range(2):
            for m in range(MB):
                for p in range(PARTS):
                    cut = slice(p * CHUNK, (p + 1) * CHUNK)
                    out_ref[j, o, p, m, 0:SPAN, :] = both[o * MB + m]
                    out_ref[j, o, p, m, SPAN : SPAN + CHUNK, :] = first[o * MB + m, cut]
                    out_ref[j, o, p, m, SPAN + CHUNK : ALL_ROWS, :] = third[o * MB + m, cut]


def third_head(pair_even, pair_odd):
    lane = lax.broadcasted_iota(jnp.int32, pair_even.shape, pair_even.ndim - 1)
    return jnp.where(lane < HD, pair_even, pair_odd)


def out_halves(ref):
    whole = ref[...].reshape(16, 2, 48, D // 2)
    return whole[:, 0].reshape(HQ, D // 2), whole[:, 1].reshape(HQ, D // 2)


def out_kernel(u_ref, w_ref, attn_ref, mine_ref, other_ref):
    for o in range(2):
        for m in range(MB):
            for p in range(PARTS):
                thirds = [
                    third_head(u_ref[2 * k, o, p, m, CHUNK:, :], u_ref[2 * k + 1, o, p, m, CHUNK:, :])
                    for k in range(2)
                ]
                parts = []
                for j in range(HALF_KV):
                    parts += [u_ref[j, o, p, m, :CHUNK, :], thirds[j // 2][:, HD * (j % 2) : HD * (j % 2) + HD]]
                at = (o * MB + m) * SPAN + p * CHUNK
                attn_ref[at : at + CHUNK, :] = jnp.concatenate(parts, axis=1)
    attn = attn_ref[...]
    for k, half in enumerate(out_halves(w_ref)):
        result = product(attn, half)
        cols = slice(k * (D // 2), (k + 1) * (D // 2))
        mine_ref[:, cols] = result[:ROWS]
        other_ref[:, cols] = result[ROWS:].astype(jnp.bfloat16)


def d_out_kernel(da_ref, w_ref, attn_ref, held_ref, out_ref, grad_ref, g_out, sem):
    attn_t = attn_ref[...].T
    for k in range(2):
        half = product(attn_t, da_ref[:, k * (D // 2) : (k + 1) * (D // 2)]).astype(jnp.bfloat16)
        for j in range(16):
            g_out[j * 96 + k * 48 : j * 96 + k * 48 + 48, :] = half[j * 48 : j * 48 + 48]
    copy = pltpu.make_async_copy(g_out, grad_ref.at[:, pl.ds(OUT_AT, D // 2)], sem)
    copy.start()
    left, right = out_halves(w_ref)
    rows = product_t(da_ref[:, : D // 2], left) + product_t(da_ref[:, D // 2 :], right)
    rows = rows.astype(jnp.bfloat16)
    for j in range(HALF_KV):
        first = rows[:, 192 * j : 192 * j + 128]
        if j % 2 == 0:
            third = jnp.concatenate([rows[:, 192 * j + 128 : 192 * j + 192], rows[:, 192 * j + 320 : 192 * j + 384]], axis=1)
        for o in range(2):
            for m in range(MB):
                for p in range(PARTS):
                    at = (o * MB + m) * SPAN + p * CHUNK
                    out_ref[j, o, p, m, :CHUNK, :] = first[at : at + CHUNK]
                    out_ref[j, o, p, m, CHUNK:, :] = third[at : at + CHUNK]
    copy.wait()


def collect_kernel(u_ref, table_ref, out_ref):
    def put(g, o, m, at, size, values, table, row):
        cosine = table_ref[table, row : row + size]
        sine = table_ref[table + 1, row : row + size]
        out_ref[at : at + size, 128 * g : 128 * g + 128] = turn(values, cosine, -sine).astype(jnp.bfloat16)

    wide = jnp.float32
    for o in range(2):
        for m in range(MB):
            base = (o * MB + m) * SPAN
            for j in range(HALF_KV):
                total = u_ref[j, o, 0, m, 0:SPAN, :].astype(wide)
                for p in range(1, PARTS):
                    total = total + u_ref[j, o, p, m, 0:SPAN, :].astype(wide)
                put(6 + j, o, m, base, SPAN, total, 2, 0)
            for p in range(PARTS):
                at = base + p * CHUNK
                for j in range(HALF_KV):
                    first = u_ref[j, o, p, m, SPAN : SPAN + CHUNK, :].astype(wide)
                    put(j, o, m, at, CHUNK, first, 0, p * CHUNK)
                for k in range(2):
                    third = third_head(
                        u_ref[2 * k, o, p, m, SPAN + CHUNK : ALL_ROWS, :].astype(wide),
                        u_ref[2 * k + 1, o, p, m, SPAN + CHUNK : ALL_ROWS, :].astype(wide),
                    )
                    put(4 + k, o, m, at, CHUNK, third, 0, p * CHUNK)


def gradient_kernel(n_ref, d_ref, gains_ref, out_ref):
    out_ref[:, :QKV] = product(n_ref[...].T, d_ref[...]).astype(jnp.bfloat16)
    gains = jnp.concatenate([gains_ref[...], jnp.zeros((120, D), jnp.float32)], axis=0)
    out_ref[:, QKV:] = gains.T.astype(jnp.bfloat16)


def stack_heads(first, third, odd):
    last = jnp.where(odd == 1, third[:, HD:], third[:, :HD])
    return jnp.concatenate([first[:, :HD], first[:, HD:], last], axis=0)


def lay_heads(rows):
    size = TILE * CHUNK
    parts = [rows[g * size : (g + 1) * size] for g in range(GROUP)]
    shape = (TILE, CHUNK, 128)
    return (
        jnp.concatenate(parts[:2], axis=1).astype(jnp.bfloat16).reshape(shape),
        jnp.concatenate([parts[2], parts[2]], axis=1).astype(jnp.bfloat16).reshape(shape),
    )


def tile_mask(part, start_rows, tile, blocks):
    wide = blocks * BLOCK
    row = lax.broadcasted_iota(jnp.int32, (TROWS, 1), 0)
    inside = lax.rem(row, TILE * CHUNK)
    q_pos = tile * BLOCK + (inside // CHUNK) * SPAN + part * CHUNK + lax.rem(inside, CHUNK)
    k_pos = (tile + 1 - blocks) * BLOCK + lax.broadcasted_iota(jnp.int32, (TROWS, wide), 1)
    return (k_pos >= start_rows) & (k_pos <= q_pos)


def tile_queries(ref, tile, begin, odd):
    where = pl.ds(tile * TILE, TILE)
    first = ref[where, 0, begin : begin + CHUNK, :].reshape(TILE * CHUNK, 128)
    third = ref[where, 0, begin + CHUNK : begin + 2 * CHUNK, :].reshape(TILE * CHUNK, 128)
    return stack_heads(first, third, odd)


def tile_keys(ref, begin, blocks):
    return ref[pl.ds(begin * TILE, blocks * TILE), 0, 0:SPAN, :].reshape(blocks * BLOCK, 128)


def each_tile(first_ref, work):
    micro = pl.program_id(0)

    def body(tile, carry):
        needed = tile + 1 - first_ref[micro * TILES + tile]
        for blocks in range(1, TILES + 1):
            pl.when(needed == blocks)(partial(work, tile, blocks))
        return carry

    lax.fori_loop(0, TILES, body, 0)


def fwd_kernel(unit_ref, first_ref, u_ref, start_ref, o_ref, lse_ref):
    part, odd = unit_ref[0], unit_ref[1]

    def work(tile, blocks):
        q_rows = tile_queries(u_ref, tile, SPAN, odd) * jnp.bfloat16(0.125)
        keys = tile_keys(u_ref, tile + 1 - blocks, blocks)
        scores = product_t(q_rows, keys[:, :HD])
        allowed = tile_mask(part, start_ref[0, tile][:, :1], tile, blocks)
        scores = jnp.where(allowed, scores, NEG)
        highest = jnp.max(scores, axis=-1, keepdims=True)
        expo = jnp.exp(scores - highest)
        total = jnp.sum(expo, axis=-1, keepdims=True)
        mixed = product(expo.astype(jnp.bfloat16), keys[:, HD:]) / total
        where = pl.ds(tile * TILE, TILE)
        o_ref[where, 0, :CHUNK, :], o_ref[where, 0, CHUNK:, :] = lay_heads(mixed)
        lse_ref[0, tile] = jnp.broadcast_to(highest + jnp.log(total), (TROWS, 128))

    each_tile(first_ref, work)


def bwd_kernel(unit_ref, first_ref, u_ref, start_ref, do_ref, lse_ref, d_ref, acc):
    part, odd = unit_ref[0], unit_ref[1]
    acc[...] = jnp.zeros_like(acc)

    def work(tile, blocks):
        begin = tile + 1 - blocks
        q_rows = tile_queries(u_ref, tile, SPAN, odd) * jnp.bfloat16(0.125)
        d_rows = tile_queries(do_ref, tile, 0, odd)
        keys = tile_keys(u_ref, begin, blocks)
        scores = product_t(q_rows, keys[:, :HD])
        allowed = tile_mask(part, start_ref[0, tile][:, :1], tile, blocks)
        probs = jnp.where(allowed, jnp.exp(scores - lse_ref[0, tile][:, :1]), 0.0)
        d_probs = product_t(d_rows, keys[:, HD:])
        offset = jnp.sum(d_probs * probs, axis=-1, keepdims=True)
        d_scores = (probs * (d_probs - offset)).astype(jnp.bfloat16)
        d_query = product(d_scores, keys[:, :HD]) * 0.125
        at = pl.ds(tile * TILE, TILE)
        d_ref[at, 0, SPAN : SPAN + CHUNK, :], d_ref[at, 0, SPAN + CHUNK : ALL_ROWS, :] = lay_heads(d_query)
        d_key = t_product(d_scores, q_rows)
        d_value = t_product(probs.astype(jnp.bfloat16), d_rows)
        where = pl.ds(begin * BLOCK, blocks * BLOCK)
        acc[where, :] += jnp.concatenate([d_key, d_value], axis=1)

    each_tile(first_ref, work)
    d_ref[:, 0, 0:SPAN, :] = acc[...].astype(jnp.bfloat16).reshape(SHARDS, SPAN, 128)


SMEM = pl.BlockSpec(memory_space=pltpu.SMEM)
UNIT_SPEC = pl.BlockSpec((SHARDS, 1, ALL_ROWS, 128), lambda m: (0, m, 0, 0))
QUERY_SPEC = pl.BlockSpec((SHARDS, 1, Q_ROWS, 128), lambda m: (0, m, 0, 0))
COL_SPEC = pl.BlockSpec((1, TILES, TROWS, 128), lambda m: (m, 0, 0, 0))
COL_SHAPE = jax.ShapeDtypeStruct((MB, TILES, TROWS, 128), jnp.float32)
PARAMS = pltpu.CompilerParams(vmem_limit_bytes=VMEM_LIMIT)


def split_units(values):
    return values.reshape((HALF_KV, 2, PARTS) + values.shape[1:])


def low_shape(*dims):
    return jax.ShapeDtypeStruct(dims, jnp.bfloat16)


def project(n1, w_qkv, tables):
    shape = low_shape(HALF_KV, 2, PARTS, MB, ALL_ROWS, 128)
    out = pl.pallas_call(project_kernel, out_shape=shape, compiler_params=PARAMS, cost_estimate=cost(6), name="project")(n1, w_qkv, tables)
    return out.reshape(SHARDS, MB, ALL_ROWS, 128)


def whole_spec(*dims):
    return pl.BlockSpec(dims, lambda i: (0,) * len(dims))


OUT_SPEC = pl.BlockSpec((D, D // 2), lambda i: (0, OUT_AT // (D // 2)))


def cost(micros):
    return pl.CostEstimate(flops=int(micros * 1e9), bytes_accessed=1 << 20, transcendentals=0)


def out_project(units, w_all):
    return pl.pallas_call(
        out_kernel,
        grid=(1,),
        in_specs=[whole_spec(HALF_KV, 2, PARTS, MB, Q_ROWS, 128), OUT_SPEC],
        out_specs=[whole_spec(BOTH, HQ), whole_spec(ROWS, D), whole_spec(ROWS, D)],
        out_shape=[low_shape(BOTH, HQ), jax.ShapeDtypeStruct((ROWS, D), jnp.float32), low_shape(ROWS, D)],
        compiler_params=PARAMS,
        cost_estimate=cost(3),
        name="out_project",
    )(split_units(units), w_all)


def d_out_project(da, w_all, attn, g_ffn):
    dims = (HALF_KV, 2, PARTS, MB, Q_ROWS, 128)
    anywhere = pl.BlockSpec(memory_space=pl.ANY)
    out, grads = pl.pallas_call(
        d_out_kernel,
        grid=(1,),
        in_specs=[whole_spec(BOTH, D), OUT_SPEC, whole_spec(BOTH, HQ), anywhere],
        out_specs=[whole_spec(*dims), anywhere],
        out_shape=[low_shape(*dims), low_shape(*g_ffn.shape)],
        scratch_shapes=[pltpu.VMEM((D, D // 2), jnp.bfloat16), pltpu.SemaphoreType.DMA],
        input_output_aliases={3: 1},
        compiler_params=PARAMS,
        cost_estimate=cost(5),
        name="d_out_project",
    )(da, w_all, attn, g_ffn)
    return out.reshape(SHARDS, MB, Q_ROWS, 128), grads


def ffn_kernel(
    n_ref, df_ref, main_ref, rest_ref, gate_ref, up_ref,
    y_mine_ref, y_other_ref, dn_mine_ref, dn_other_ref, grad_ref,
    n_t, y_acc, dn_acc, g_gate, g_up, g_main, g_rest, sems,
):
    step = pl.program_id(0)
    slot = lax.rem(step, 2)

    def copies(at, slot):
        cols, rows = at * FF_TILE, at * FF_ROWS
        return [
            pltpu.make_async_copy(
                g_gate.at[slot], grad_ref.at[:, pl.ds(pl.multiple_of(GATE_AT + cols, FF_TILE), FF_TILE)], sems.at[slot, 0]
            ),
            pltpu.make_async_copy(
                g_up.at[slot], grad_ref.at[:, pl.ds(pl.multiple_of(UP_AT + cols, FF_TILE), FF_TILE)], sems.at[slot, 1]
            ),
            pltpu.make_async_copy(
                g_main.at[slot], grad_ref.at[pl.ds(pl.multiple_of(rows, 64), FF_ROWS), pl.ds(0, D)], sems.at[slot, 2]
            ),
            pltpu.make_async_copy(
                g_rest.at[slot],
                grad_ref.at[pl.ds(pl.multiple_of(rows, 64), FF_ROWS), pl.ds(REST_AT, D // 3)],
                sems.at[slot, 3],
            ),
        ]

    @pl.when(step == 0)
    def _():
        n_t[...] = n_ref[...].T
        y_acc[...] = jnp.zeros_like(y_acc)
        dn_acc[...] = jnp.zeros_like(dn_acc)

    @pl.when(step >= 2)
    def _():
        for copy in copies(step - 2, slot):
            copy.wait()

    low = jnp.bfloat16
    units = []
    for j in range(FF_TILE // UNIT_FF):
        rest = [rest_ref[j * 96 + q * 32 : j * 96 + q * 32 + 32, :] for q in range(3)]
        units += [main_ref[j * 96 : j * 96 + 96, :], jnp.concatenate(rest, axis=1)]
    w_down = jnp.concatenate(units, axis=0)
    rows, df = n_ref[...], df_ref[...]
    gate, up = product(rows, gate_ref[...]), product(rows, up_ref[...])
    sigma = jax.nn.sigmoid(gate)
    silu = gate * sigma
    act = (silu * up).astype(low)
    d_act = product_t(df, w_down)
    d_gate = (d_act * up * sigma * (1.0 + gate * (1.0 - sigma))).astype(low)
    d_up = (d_act * silu).astype(low)
    y_acc[...] += product(act, w_down)
    dn_acc[...] += product_t(d_gate, gate_ref[...]) + product_t(d_up, up_ref[...])
    g_gate[slot] = product(n_t[...], d_gate).astype(low)
    g_up[slot] = product(n_t[...], d_up).astype(low)
    g_down = product(act.T, df).astype(low)
    for j in range(FF_TILE // UNIT_FF):
        g_main[slot, j * 96 : j * 96 + 96, :] = g_down[j * UNIT_FF : j * UNIT_FF + 96]
        for q in range(3):
            g_rest[slot, j * 96 + q * 32 : j * 96 + q * 32 + 32, :] = g_down[
                j * UNIT_FF + 96 : (j + 1) * UNIT_FF, q * (D // 3) : (q + 1) * (D // 3)
            ]
    for copy in copies(step, slot):
        copy.start()

    @pl.when(step == FF_TILES - 1)
    def _():
        y_mine_ref[...] = y_acc[:ROWS]
        y_other_ref[...] = y_acc[ROWS:].astype(low)
        dn_mine_ref[...] = dn_acc[:ROWS]
        dn_other_ref[...] = dn_acc[ROWS:].astype(low)
        for back in (1, 0):
            for copy in copies(step - back, lax.rem(step - back, 2)):
                copy.wait()


def feed_forward(n2, df, w_all):
    wide = jax.ShapeDtypeStruct((ROWS, D), jnp.float32)
    return pl.pallas_call(
        ffn_kernel,
        grid=(FF_TILES,),
        in_specs=[
            whole_spec(BOTH, D),
            whole_spec(BOTH, D),
            pl.BlockSpec((FF_ROWS, D), lambda t: (t, 0)),
            pl.BlockSpec((FF_ROWS, D // 3), lambda t: (t, REST_AT // (D // 3))),
            pl.BlockSpec((D, FF_TILE), lambda t: (0, GATE_AT // FF_TILE + t)),
            pl.BlockSpec((D, FF_TILE), lambda t: (0, UP_AT // FF_TILE + t)),
        ],
        out_specs=[whole_spec(ROWS, D)] * 4 + [pl.BlockSpec(memory_space=pl.ANY)],
        out_shape=[wide, low_shape(ROWS, D), wide, low_shape(ROWS, D), low_shape(D, OUT_AT + D // 2)],
        scratch_shapes=[
            pltpu.VMEM((D, BOTH), jnp.bfloat16),
            pltpu.VMEM((BOTH, D), jnp.float32),
            pltpu.VMEM((BOTH, D), jnp.float32),
            pltpu.VMEM((2, D, FF_TILE), jnp.bfloat16),
            pltpu.VMEM((2, D, FF_TILE), jnp.bfloat16),
            pltpu.VMEM((2, FF_ROWS, D), jnp.bfloat16),
            pltpu.VMEM((2, FF_ROWS, D // 3), jnp.bfloat16),
            pltpu.SemaphoreType.DMA((2, 4)),
        ],
        compiler_params=PARAMS,
        cost_estimate=cost(30),
        name="feed_forward",
    )(n2, df, w_all, w_all, w_all, w_all)


def collect(units, tables):
    shape = low_shape(BOTH, HQ + 2 * HK)
    return pl.pallas_call(collect_kernel, out_shape=shape, compiler_params=PARAMS, cost_estimate=cost(4), name="collect")(
        split_units(units), tables
    )


def gradients(n1, d_qkv, gains):
    return pl.pallas_call(
        gradient_kernel,
        out_shape=low_shape(D, QKV + 128),
        compiler_params=PARAMS,
        cost_estimate=cost(5),
        name="gradients",
    )(n1, d_qkv, gains)


def attend_fwd(unit, first, units, starts):
    return pl.pallas_call(
        fwd_kernel,
        grid=(MB,),
        in_specs=[SMEM, SMEM, UNIT_SPEC, COL_SPEC],
        out_specs=[QUERY_SPEC, COL_SPEC],
        out_shape=[low_shape(SHARDS, MB, Q_ROWS, 128), COL_SHAPE],
        compiler_params=PARAMS,
        cost_estimate=cost(20),
        name="attend_forward",
    )(unit, first, units, starts)


def attend_bwd(unit, first, units, starts, d_mixed, lse):
    return pl.pallas_call(
        bwd_kernel,
        grid=(MB,),
        in_specs=[SMEM, SMEM, UNIT_SPEC, COL_SPEC, QUERY_SPEC, COL_SPEC],
        out_specs=UNIT_SPEC,
        out_shape=low_shape(SHARDS, MB, ALL_ROWS, 128),
        scratch_shapes=[pltpu.VMEM((SEQ, 128), jnp.float32)],
        compiler_params=PARAMS,
        cost_estimate=cost(27),
        name="attend_backward",
    )(unit, first, units, starts, d_mixed, lse)


def piece_perm():
    return [(k * SHARDS + s, (s // 16) * SHARDS + 2 * (s % 16) + k) for k in range(2) for s in range(SHARDS)]


def shift(values, axis, step):
    if axis == "x":
        line = lambda x: (x % 2) * 2 + x // 2
        return lax.ppermute(values, ("xl", "xh"), [(line(i), line((i + step) % 4)) for i in range(4)])
    return lax.ppermute(values, axis, [(i, (i + step) % 4) for i in range(4)])


def place(axis):
    if axis == "x":
        return lax.axis_index("xh") * 2 + lax.axis_index("xl")
    return lax.axis_index(axis)


def flip(values, axis):
    return lax.ppermute(values, axis, [(0, 1), (1, 0)])


def col_half(core, local):
    half = local.shape[1] // 2
    return lax.dynamic_slice_in_dim(local, core * half, half, axis=1)


def pad_units(local):
    return jnp.pad(local.reshape(-1, 16, 120), ((0, 0), (0, 0), (0, UNIT_FF - 120))).reshape(-1, PAD_FF)


def crop_units(local):
    return local.reshape(-1, 16, UNIT_FF)[:, :, :120].reshape(-1, HF)


def fold(rows, parts):
    n, r, w = rows.shape
    return rows.reshape(n, r, parts, w // parts).transpose(0, 2, 1, 3).reshape(n, parts * r, w // parts)


def unfold(rows, parts):
    n, r, w = rows.shape
    return rows.reshape(n, parts, r // parts, w).transpose(0, 2, 1, 3).reshape(n, r // parts, parts * w)


def wide_sum(*values):
    total = values[0].astype(jnp.float32)
    for value in values[1:]:
        total = total + value.astype(jnp.float32)
    return total.astype(jnp.bfloat16)


def after(values, event):
    return lax.optimization_barrier((values, event))[0]


def total_axis(values, axis):
    return values + shift(values, axis, 1) + shift(values, axis, 2) + shift(values, axis, 3)


def reduce_x(values, dim):
    size = values.shape[dim] // 2
    me = lax.axis_index("xh")
    keep = lax.dynamic_slice_in_dim(values, me * size, size, axis=dim)
    send = lax.dynamic_slice_in_dim(values, (1 - me) * size, size, axis=dim)
    cross = lax.ppermute(send, ("xl", "xh"), [(i, 3 - i) for i in range(4)])
    return wide_sum(keep, flip(keep, "xl"), flip(send, "xh"), cross)


def add_pair(values, axis):
    return wide_sum(values, flip(values, axis))


def join_pair(mine, axis, dim):
    other = flip(mine, axis)
    lower = lax.axis_index(axis) == 0
    return jnp.concatenate([jnp.where(lower, mine, other), jnp.where(lower, other, mine)], axis=dim)


def join_cores(mine):
    return join_pair(mine, "c", 1).astype(jnp.float32)


def scatter_sum(values):
    return jnp.sum(exchange(values).astype(jnp.float32), axis=0).astype(jnp.bfloat16)


def on_device(
    hidden_in,
    doc_ids,
    out_grad,
    norm_attn,
    w_query,
    w_key,
    w_value,
    w_out,
    norm_ffn,
    w_gate,
    w_up,
    w_down,
):
    core = lax.axis_index("c")
    shard = lax.axis_index(SHARD)
    low = jnp.bfloat16

    rows_in = lax.ppermute(jnp.concatenate([w_out, w_down], axis=0), ("c",) + SHARD, piece_perm())
    gu_piece = jnp.concatenate([pad_units(col_half(core, w_gate)), pad_units(col_half(core, w_up))], axis=1)
    w_all = lax.all_gather(
        jnp.concatenate(
            [
                rows_in[48:144],
                fold(jnp.pad(rows_in[144:], ((0, 8), (0, 0)))[None], 3)[0],
                join_pair(gu_piece, "xh", 0),
                fold(rows_in[:48][None], 2)[0],
            ],
            axis=1,
        ),
        ("z", "y"),
        axis=0,
        tiled=True,
    )
    small = jnp.concatenate(
        [norm_attn[:, None], norm_ffn[:, None], doc_ids.reshape(48, 4).astype(low), jnp.zeros((48, 122), low)], axis=1
    )
    piece = jnp.concatenate(
        [to_groups(col_half(core, w_query)), interleave(col_half(core, w_key), col_half(core, w_value)), small], axis=1
    )
    w_first = exchange(jnp.broadcast_to(piece[None], (SHARDS, 48, QKV + 128)))
    small = w_first[:, :, QKV : QKV + 6]
    w_first = w_first.reshape(D, QKV + 128)
    w_qkv = w_first[:, :QKV]
    gain_attn = small[:, :, 0].reshape(1, D).astype(jnp.float32)
    gain_ffn = small[:, :, 1].reshape(1, D).astype(jnp.float32)
    docs_mine = small[:, :, 2:].reshape(SHARDS, MB, SPAN).transpose(1, 0, 2).reshape(MB, SEQ)
    docs_other = swap(docs_mine)

    x_low = hidden_in.reshape(ROWS, D)
    x = x_low.astype(jnp.float32)
    x_both = jnp.concatenate([x_low, swap(x_low)], axis=0).astype(jnp.float32)
    dy_low = out_grad.reshape(ROWS, D)
    dy = dy_low.astype(jnp.float32)
    df = (branch_scale * jnp.concatenate([dy_low, swap(dy_low)], axis=0).astype(jnp.float32)).astype(low)

    which = lax.rem(shard // PARTS, 2)
    part = lax.rem(shard, PARTS)
    docs = jnp.where(which == 0, docs_mine, docs_other).astype(jnp.float32)
    counted = jnp.sum((docs[:, None, :] < docs[:, :, None]).astype(jnp.int32), axis=-1)
    q_start = lax.dynamic_slice_in_dim(counted.reshape(MB, SHARDS, SPAN), part * CHUNK, CHUNK, axis=2)
    q_start = q_start.reshape(MB, TILES, 1, TILE * CHUNK)
    first = (q_start[:, :, 0, 0] // BLOCK).reshape(-1)
    starts = jnp.broadcast_to(q_start, (MB, TILES, GROUP, TILE * CHUNK)).reshape(MB, TILES, TROWS, 1)
    starts = jnp.broadcast_to(starts, (MB, TILES, TROWS, 128))
    unit = jnp.stack([part, lax.rem(shard // (2 * PARTS), 2)]).astype(jnp.int32)

    places = (shard * SPAN + jnp.arange(SPAN, dtype=jnp.int32)).astype(jnp.float32)
    half_size = HD // 2
    inverse = jnp.exp(-jnp.arange(half_size, dtype=jnp.float32) * (math.log(10000.0) / half_size))
    angles = places[:, None] * inverse[None, :]
    cosine, sine = jnp.cos(angles), jnp.sin(angles)
    cosine = jnp.concatenate([cosine, cosine], axis=1)
    sine = jnp.concatenate([-sine, sine], axis=1)
    tables = jnp.stack(
        [
            jnp.concatenate([cosine, cosine], axis=1),
            jnp.concatenate([sine, sine], axis=1),
            jnp.concatenate([cosine, jnp.ones_like(cosine)], axis=1),
            jnp.concatenate([sine, jnp.zeros_like(sine)], axis=1),
        ]
    )

    r1_both = lax.rsqrt(jnp.mean(x_both * x_both, axis=-1, keepdims=True) + eps_norm)
    r1 = r1_both[:ROWS]
    n1 = (x_both * r1_both * gain_attn).astype(low)
    units = exchange(project(n1, w_first, tables))
    unit_o, lse = attend_fwd(unit, first, units, starts)
    attn, y1_mine, y1_other = out_project(exchange(unit_o), w_all)
    hmid = x + branch_scale * (y1_mine + swap(y1_other).astype(jnp.float32))

    r2 = lax.rsqrt(jnp.mean(hmid * hmid, axis=-1, keepdims=True) + eps_norm)
    z2 = hmid * r2
    n2_mine = (z2 * gain_ffn).astype(low)
    n2 = jnp.concatenate([n2_mine, swap(n2_mine)], axis=0)
    y2_mine, y2_other, dn2_mine, dn2_other, g_ffn = feed_forward(n2, df, w_all)
    result = hmid + branch_scale * (y2_mine + swap(y2_other).astype(jnp.float32))

    dn2 = dn2_mine + swap(dn2_other).astype(jnp.float32)
    e2 = dn2 * gain_ffn
    g_gain_ffn = jnp.sum(dn2 * z2, axis=0)
    dh = dy + r2 * (e2 - z2 * jnp.mean(e2 * z2, axis=-1, keepdims=True))

    da_mine = (branch_scale * dh).astype(low)
    da = jnp.concatenate([da_mine, swap(da_mine)], axis=0)
    unit_do, g_all = d_out_project(da, w_all, attn, g_ffn)
    s_all = lax.psum_scatter(g_all, ("z", "y"), scatter_dimension=0, tiled=True)
    unit_do = exchange(unit_do)
    unit_d = attend_bwd(unit, first, units, starts, unit_do, lse)
    d_qkv = collect(exchange(unit_d), tables)

    dn1_both = product_t(d_qkv, w_qkv)
    dn1 = dn1_both[:ROWS] + swap(dn1_both[ROWS:].astype(low)).astype(jnp.float32)
    z1 = x * r1
    e1 = dn1 * gain_attn
    g_gain_attn = jnp.sum(dn1 * z1, axis=0)
    grad_in = (dh + r1 * (e1 - z1 * jnp.mean(e1 * z1, axis=-1, keepdims=True))).astype(low)

    gains = jnp.concatenate([g_gain_attn[None], g_gain_ffn[None], jnp.zeros((6, D), jnp.float32)], axis=0)
    s_qkv = add_pair(scatter_sum(gradients(n1, d_qkv, gains).reshape(SHARDS, 48, QKV + 128)), "xl")
    other_qkv = swap(s_qkv)
    s_all = after(s_all, other_qkv)
    rows = jnp.concatenate(
        [
            unfold(s_all[None, :, OUT_AT:], 2)[0],
            s_all[:, :D],
            unfold(s_all[None, :, REST_AT:GATE_AT], 3)[0][:24],
        ],
        axis=0,
    )
    rows_x = reduce_x(rows, 1)
    rows = join_cores(lax.ppermute(rows_x, ("c",) + SHARD, [(b, a) for a, b in piece_perm()]))
    s_gu = reduce_x(s_all[:, GATE_AT:OUT_AT], 0)
    other = swap(s_gu)
    lower = core == 0
    s_gu, other = [
        [crop_units(v[:, :PAD_FF]), crop_units(v[:, PAD_FF:])] for v in (s_gu.astype(jnp.float32), other.astype(jnp.float32))
    ]
    g_g, g_u = [
        jnp.concatenate([jnp.where(lower, m, t), jnp.where(lower, t, m)], axis=1) for m, t in zip(s_gu, other)
    ]
    whole = [jnp.where(lower, s_qkv, other_qkv), jnp.where(lower, other_qkv, s_qkv)]
    gains = s_qkv[:, QKV : QKV + 2].astype(jnp.float32) + other_qkv[:, QKV : QKV + 2].astype(jnp.float32)

    def heads_of(offset):
        return jnp.concatenate(
            [w[:, HQ + 128 * j + offset : HQ + 128 * j + offset + HD] for w in whole for j in range(HALF_KV)], axis=1
        ).astype(jnp.float32)

    return (
        result.reshape(1, MB, SPAN, D).astype(low),
        grad_in.reshape(1, MB, SPAN, D),
        gains[:, 0],
        jnp.concatenate([from_groups(w[:, :HQ]) for w in whole], axis=1).astype(jnp.float32),
        heads_of(0),
        heads_of(HD),
        rows[:48],
        gains[:, 1],
        g_g,
        g_u,
        rows[48:],
    )


def solution(mesh):
    fine = Mesh(mesh.devices.reshape(2, 2, 4, 4, 2), ("xl", "c", "z", "y", "xh"))
    replica = ("xl", "c")
    tokens = P(replica, None, SHARD, None)
    matrix = P(SHARD, None)
    vector = P(SHARD)
    return jax.shard_map(
        on_device,
        mesh=fine,
        in_specs=(
            tokens,
            P(replica, None, SHARD),
            tokens,
            vector,
            matrix,
            matrix,
            matrix,
            matrix,
            vector,
            matrix,
            matrix,
            matrix,
        ),
        out_specs=(
            tokens,
            tokens,
            vector,
            matrix,
            matrix,
            matrix,
            matrix,
            vector,
            matrix,
            matrix,
            matrix,
        ),
        check_vma=False,
    )
```
